32 devices in a mesh: sample: 4 (over y, core), turb: 8 (over z, x).
Axes of the slice: x: 2, y: 2, z: 4, core: 2. Of those that a mesh axis runs over, the one named last changes fastest.
Arguments:
- inflow: bfloat16 [32, 1024, 512], P('sample', 'turb'), may hold values from -6 to 6
- cotangent: bfloat16 [32, 1024, 512], P('sample', 'turb'), may hold values from -6 to 6
- norm_gain: float32 [512], replicated, may hold values from 0.25 to 1.75
- query_weight: bfloat16 [512, 512], replicated, may hold values from -2 to 2, as said below
- key_weight: bfloat16 [512, 512], replicated, may hold values from -2 to 2, as said below
- value_weight: bfloat16 [512, 512], replicated, may hold values from -0.25 to 0.25
- out_weight: bfloat16 [512, 512], replicated, may hold values from -0.25 to 0.25
- adjacency: int32 [8, 8, 3], replicated, may hold values from -1 to 7, as said below
- sectors: int32 [32], P('sample'), may hold values from 0 to 7, as said below
Outputs:
- layer_output: bfloat16 [32, 1024, 512], P('sample', 'turb')
- grad_inflow: bfloat16 [32, 1024, 512], P('sample', 'turb')
- grad_query_weight: float32 [512, 512], replicated
- grad_key_weight: float32 [512, 512], replicated
- grad_value_weight: float32 [512, 512], replicated
- grad_out_weight: float32 [512, 512], replicated
- grad_norm_gain: float32 [512], replicated
The draws below stay inside these ranges and needn't reach their ends.
Inputs may be any that keep to these rules, and one draw needn't show every extreme that they name: `adjacency`: row [s, b] lists distinct blocks other than b, the used entries first and -1 after them. For every block and every group of 8 consecutive samples, another block is listed upstream of it for at most 4 of the group's samples, and some pair of blocks reaches 4. `sectors`: every group of 8 consecutive samples holds each sector exactly 1 times. `query_weight`: A projection of rows of 512 features. `key_weight`: A projection of rows of 512 features.
All inputs are finite; a program needn't handle non-finite values.
Results may differ from the reference program's by a relative error of at most 0.004.
The reference program's roundings to bfloat16 on the way count: a program that leaves them out, or rounds other values in their place, can miss the bound.
Values may be sent and summed in bfloat16 or wider, within the bound.
No kernel may reach another device: no remote copies, remote signals or barrier semaphores. Data moves between devices by JAX's collectives and lax.ppermute only.
A program may use at most 192 MiB of HBM per device.

```python
import math
import jax
import jax.numpy as jnp
from jax import lax

D = 512
HEADS = 8
BLOCK = 128
UPSTREAM = 3
SECTORS = 8
SAMP_DEV = 8
SAMPLES = 32
BLOCKS = 8
TURBINES = 1024


def draw_adjacency(key, part):
    base = jax.random.fold_in(key, 101)
    order_key, count_key, pick_key = jax.random.split(base, 3)
    others = BLOCKS - 1
    orders = jax.vmap(lambda single: jax.random.permutation(single, others))(jax.random.split(order_key, BLOCKS))
    block_ids = jnp.arange(BLOCKS, dtype=jnp.int32)
    sources = (block_ids[:, None] + 1 + orders.astype(jnp.int32)) % BLOCKS
    counts = jax.random.randint(count_key, (SECTORS, BLOCKS), 0, UPSTREAM + 1)
    fullest = jax.random.randint(pick_key, (), 0, BLOCKS)
    counts = jnp.where(block_ids[None, :] == fullest, UPSTREAM, counts)
    slot_ids = jnp.arange(UPSTREAM, dtype=jnp.int32)
    places = (jnp.arange(SECTORS, dtype=jnp.int32)[:, None] * UPSTREAM + slot_ids[None, :]) % others
    picked = jnp.transpose(sources[:, places], (1, 0, 2))
    return jnp.where(slot_ids[None, None, :] < counts[:, :, None], picked, -1).astype(jnp.int32)


def draw_sectors(key, part):
    base = jax.random.fold_in(key, 202)
    groups = SAMPLES // SAMP_DEV
    orders = jax.vmap(lambda single: jax.random.permutation(single, SAMP_DEV))(jax.random.split(base, groups))
    return (orders.astype(jnp.int32) % SECTORS).reshape(SAMPLES)


def draw_query_weight(key, part):
    single = jax.random.normal(jax.random.fold_in(key, 1), (D, D), jnp.float32) / math.sqrt(D)
    return jnp.clip(single, -2.0, 2.0).astype(jnp.bfloat16)


def draw_key_weight(key, part):
    single = jax.random.normal(jax.random.fold_in(key, 2), (D, D), jnp.float32) / math.sqrt(D)
    return jnp.clip(single, -2.0, 2.0).astype(jnp.bfloat16)


def block_levels(rng, shape, shards, low, high):
    def one(position, shards_of):
        heights = jax.random.uniform(jax.random.fold_in(jax.random.fold_in(rng, 6), position), (shards_of,), jnp.float32, low / len(shards), high / len(shards))
        return jnp.repeat(jnp.exp(heights), shape[position] // shards_of).reshape((-1,) + (1,) * (len(shape) - position - 1))

    gain = one(*shards[0])
    for cut in shards[1:]:
        gain = gain * one(*cut)
    return gain


def scatter_about(own_key, shape, spread, most, cuts=(), held_as=jnp.bfloat16):
    entries = jax.random.normal(own_key, shape, jnp.float32) * spread
    if len(cuts) > 0:
        entries = block_levels(own_key, shape, cuts, -0.22, 0.18) * entries
    return jnp.clip(entries, min=-most, max=most).astype(held_as)


def setup_inputs(seed: int = 0) -> dict:
    arg_keys = jax.random.split(jax.random.key(seed), 10)
    return {
        "inflow": scatter_about(arg_keys[0], (SAMPLES, TURBINES, D), 1.0, 6.0, ((0, 4), (1, 8))),
        "cotangent": scatter_about(arg_keys[1], (SAMPLES, TURBINES, D), 1.0, 6.0, ((0, 4), (1, 8))),
        "norm_gain": jnp.clip(1.0 + 0.15 * jax.random.normal(arg_keys[2], (D,), jnp.float32), 0.25, 1.75),
        "query_weight": draw_query_weight(jax.random.fold_in(arg_keys[9], 71), 0),
        "key_weight": draw_key_weight(jax.random.fold_in(arg_keys[9], 71), 0),
        "value_weight": scatter_about(arg_keys[5], (D, D), D ** -0.5, 0.25),
        "out_weight": scatter_about(arg_keys[6], (D, D), D ** -0.5, 0.25),
        "adjacency": draw_adjacency(jax.random.fold_in(arg_keys[9], 71), 0),
        "sectors": draw_sectors(jax.random.fold_in(arg_keys[9], 71), 0),
    }


epsilon = 1e-05

def normalize(row_block, norm_gain):
    widened = row_block.astype(jnp.float32)
    centred = widened - lax.optimization_barrier(jnp.mean(widened, axis=-1, keepdims=True))
    inverse = lax.rsqrt(lax.optimization_barrier(jnp.mean(centred * centred, axis=-1, keepdims=True)) + epsilon)
    scaled = centred * inverse
    return (scaled, inverse, (scaled * norm_gain).astype(jnp.bfloat16))

def attend(queries, key_rows, value_rows, key_usable, grad_attended):
    batch_count, query_count, model_width = queries.shape
    key_count = key_rows.shape[1]
    head_dim = model_width // HEADS
    score_scale = head_dim ** (-0.5)
    query_heads = queries.reshape(batch_count, query_count, HEADS, head_dim).astype(jnp.float32)
    key_heads = key_rows.reshape(batch_count, key_count, HEADS, head_dim).astype(jnp.float32)
    value_heads = value_rows.reshape(batch_count, key_count, HEADS, head_dim).astype(jnp.float32)
    grad_heads = grad_attended.reshape(batch_count, query_count, HEADS, head_dim).astype(jnp.float32)
    scores = jnp.einsum('nqhd,nkhd->nhqk', query_heads, key_heads) * score_scale
    scores = jnp.where(key_usable[:, None, None, :], scores, -1e+30)
    highest = lax.optimization_barrier(jnp.max(scores, axis=-1, keepdims=True))
    weights = jnp.exp(scores - highest)
    probabilities = weights / lax.optimization_barrier(jnp.sum(weights, axis=-1, keepdims=True))
    rounded = probabilities.astype(jnp.bfloat16)
    attended = jnp.einsum('nhqk,nkhd->nqhd', rounded.astype(jnp.float32), value_heads).astype(jnp.bfloat16)
    grad_probs = jnp.einsum('nqhd,nkhd->nhqk', grad_heads, value_heads)
    centred = grad_probs - lax.optimization_barrier(jnp.sum(probabilities * grad_probs, axis=-1, keepdims=True))
    grad_scores = (probabilities * centred * score_scale).astype(jnp.bfloat16)
    grad_queries = jnp.einsum('nhqk,nkhd->nqhd', grad_scores.astype(jnp.float32), key_heads).astype(jnp.bfloat16)
    grad_keys = jnp.einsum('nhqk,nqhd->nkhd', grad_scores.astype(jnp.float32), query_heads)
    grad_values = jnp.einsum('nhqk,nqhd->nkhd', rounded.astype(jnp.float32), grad_heads)
    pair_terms = jnp.concatenate([grad_keys.reshape(batch_count, key_count, model_width), grad_values.reshape(batch_count, key_count, model_width)], axis=-1)
    return (attended.reshape(batch_count, query_count, model_width), grad_queries.reshape(batch_count, query_count, model_width), pair_terms)

def reference(inflow, cotangent, norm_gain, query_weight, key_weight, value_weight, out_weight, adjacency, sectors):

    def one_sample(totals, pieces):
        input_rows, grad_rows, sector = pieces
        scaled, inverse, normed = normalize(input_rows, norm_gain)
        queries = jnp.dot(normed, query_weight, preferred_element_type=jnp.float32).astype(jnp.bfloat16)
        key_rows = jnp.dot(normed, key_weight, preferred_element_type=jnp.float32).astype(jnp.bfloat16)
        value_rows = jnp.dot(normed, value_weight, preferred_element_type=jnp.float32).astype(jnp.bfloat16)
        upstream = adjacency[sector]
        usable = upstream >= 0
        safe_lists = jnp.where(usable, upstream, 0)
        key_blocks = key_rows.reshape(BLOCKS, BLOCK, D)
        value_blocks = value_rows.reshape(BLOCKS, BLOCK, D)
        key_all = jnp.concatenate([key_blocks[:, None], key_blocks[safe_lists]], axis=1).reshape(BLOCKS, (1 + UPSTREAM) * BLOCK, D)
        value_all = jnp.concatenate([value_blocks[:, None], value_blocks[safe_lists]], axis=1).reshape(BLOCKS, (1 + UPSTREAM) * BLOCK, D)
        block_usable = jnp.concatenate([jnp.ones((BLOCKS, 1), dtype=jnp.bool_), usable], axis=1)
        key_usable = jnp.repeat(block_usable, BLOCK, axis=1)
        grad_attended = jnp.dot(grad_rows, out_weight.T, preferred_element_type=jnp.float32).astype(jnp.bfloat16)
        attended, grad_queries, pair_terms = attend(queries.reshape(BLOCKS, BLOCK, D), key_all, value_all, key_usable, grad_attended.reshape(BLOCKS, BLOCK, D))
        attended = attended.reshape(TURBINES, D)
        grad_queries = grad_queries.reshape(TURBINES, D)
        layer_output = (input_rows.astype(jnp.float32) + jnp.dot(attended, out_weight, preferred_element_type=jnp.float32)).astype(jnp.bfloat16)
        pair_terms = pair_terms.reshape(BLOCKS, 1 + UPSTREAM, BLOCK, 2 * D)
        sent_terms = lax.optimization_barrier(pair_terms[:, 1:].astype(jnp.bfloat16)).astype(jnp.float32)
        target = jnp.where(usable, upstream, BLOCKS).reshape(-1)
        combined = pair_terms[:, 0].at[target].add(sent_terms.reshape(BLOCKS * UPSTREAM, BLOCK, 2 * D), mode='drop')
        combined = combined.astype(jnp.bfloat16).reshape(TURBINES, 2 * D)
        grad_keys = combined[:, :D]
        grad_values = combined[:, D:]
        sum_query = jnp.dot(normed.T, grad_queries, preferred_element_type=jnp.float32)
        sum_key = jnp.dot(normed.T, grad_keys, preferred_element_type=jnp.float32)
        sum_value = jnp.dot(normed.T, grad_values, preferred_element_type=jnp.float32)
        sum_out = jnp.dot(attended.T, grad_rows, preferred_element_type=jnp.float32)
        grad_normed = jnp.dot(grad_queries, query_weight.T, preferred_element_type=jnp.float32)
        grad_normed = grad_normed + jnp.dot(grad_keys, key_weight.T, preferred_element_type=jnp.float32)
        grad_normed = grad_normed + jnp.dot(grad_values, value_weight.T, preferred_element_type=jnp.float32)
        sum_gain = lax.optimization_barrier(jnp.sum(grad_normed * scaled, axis=0))
        grad_scaled = grad_normed * norm_gain
        grad_input = inverse * (grad_scaled - lax.optimization_barrier(jnp.mean(grad_scaled, axis=-1, keepdims=True)) - scaled * lax.optimization_barrier(jnp.mean(grad_scaled * scaled, axis=-1, keepdims=True)))
        grad_inflow = (grad_rows.astype(jnp.float32) + grad_input).astype(jnp.bfloat16)
        new_totals = (totals[0] + sum_query, totals[1] + sum_key, totals[2] + sum_value, totals[3] + sum_out, totals[4] + sum_gain)
        return (new_totals, (layer_output, grad_inflow))
    zero_square = jnp.zeros((D, D), jnp.float32)
    start = (zero_square, zero_square, zero_square, zero_square, jnp.zeros((D,), jnp.float32))
    totals, outputs = lax.scan(one_sample, start, (inflow, cotangent, sectors))
    return (outputs[0], outputs[1], totals[0], totals[1], totals[2], totals[3], totals[4])
```

```python
import jax
import jax.numpy as jnp
from jax import lax
from jax.experimental import pallas as pl
from jax.experimental.pallas import tpu as pltpu
from jax.sharding import PartitionSpec as P

HEADS = 8
UPSTREAM = 3
SECTORS = 8
REPEAT = 1


epsilon = 1e-05


def normalize(row_block, norm_gain):
    widened = row_block.astype(jnp.float32)
    centred = widened - jnp.mean(widened, axis=-1, keepdims=True)
    inverse = lax.rsqrt(jnp.mean(centred * centred, axis=-1, keepdims=True) + epsilon)
    scaled = centred * inverse
    return (scaled, inverse, (scaled * norm_gain).astype(jnp.bfloat16))


def attend(pieces):
    queries, key_rows, value_rows, key_usable, grad_attended = pieces
    batch_count, query_count, model_width = queries.shape
    key_count = key_rows.shape[1]
    head_dim = model_width // HEADS
    score_scale = head_dim ** (-0.5)
    query_heads = queries.reshape(batch_count, query_count, HEADS, head_dim)
    key_heads = key_rows.reshape(batch_count, key_count, HEADS, head_dim)
    value_heads = value_rows.reshape(batch_count, key_count, HEADS, head_dim)
    grad_heads = grad_attended.reshape(batch_count, query_count, HEADS, head_dim)
    scores = (
        jnp.einsum("nqhd,nkhd->nhqk", query_heads, key_heads, preferred_element_type=jnp.float32)
        * score_scale
    )
    scores = jnp.where(key_usable[:, None, None, :], scores, -1e30)
    highest = jnp.max(scores, axis=-1, keepdims=True)
    weights = jnp.exp(scores - highest)
    probabilities = weights / jnp.sum(weights, axis=-1, keepdims=True)
    rounded = probabilities.astype(jnp.bfloat16)
    attended = jnp.einsum(
        "nhqk,nkhd->nqhd", rounded, value_heads, preferred_element_type=jnp.float32
    ).astype(jnp.bfloat16)
    grad_probs = jnp.einsum(
        "nqhd,nkhd->nhqk", grad_heads, value_heads, preferred_element_type=jnp.float32
    )
    centred = grad_probs - jnp.sum(probabilities * grad_probs, axis=-1, keepdims=True)
    grad_scores = (probabilities * centred * score_scale).astype(jnp.bfloat16)
    grad_queries = jnp.einsum(
        "nhqk,nkhd->nqhd", grad_scores, key_heads, preferred_element_type=jnp.float32
    ).astype(jnp.bfloat16)
    grad_keys = jnp.einsum(
        "nhqk,nqhd->nkhd", grad_scores, query_heads, preferred_element_type=jnp.float32
    )
    grad_values = jnp.einsum(
        "nhqk,nqhd->nkhd", rounded, grad_heads, preferred_element_type=jnp.float32
    )
    pair_terms = jnp.concatenate(
        [
            grad_keys.reshape(batch_count, key_count, model_width),
            grad_values.reshape(batch_count, key_count, model_width),
        ],
        axis=-1,
    )
    return (
        attended.reshape(batch_count, query_count, model_width),
        grad_queries.reshape(batch_count, query_count, model_width),
        pair_terms,
    )


def on_device(
    inflow,
    cotangent,
    norm_gain,
    query_weight,
    key_weight,
    value_weight,
    out_weight,
    adjacency,
    sectors,
):
    sample_count, block_rows, model_width = inflow.shape
    block_count = lax.axis_size("turb")
    own_block = lax.axis_index("turb")
    slot_count = REPEAT * ((SECTORS * UPSTREAM + block_count - 2) // (block_count - 1))
    flat_rows = sample_count * block_rows
    pair_width = 2 * model_width
    input_rows = inflow.reshape(flat_rows, model_width)
    grad_rows = cotangent.reshape(flat_rows, model_width)
    scaled, inverse, normed = normalize(input_rows, norm_gain)
    queries = jnp.dot(normed, query_weight, preferred_element_type=jnp.float32).astype(jnp.bfloat16)
    key_rows = jnp.dot(normed, key_weight, preferred_element_type=jnp.float32).astype(jnp.bfloat16)
    value_rows = jnp.dot(normed, value_weight, preferred_element_type=jnp.float32).astype(
        jnp.bfloat16
    )
    upstream = adjacency[sectors]
    needed = jnp.any(upstream == own_block, axis=2).astype(jnp.int32)
    earlier_need = jnp.cumsum(needed, axis=0) - needed
    slot_index = lax.broadcasted_iota(jnp.int32, (block_count, slot_count, sample_count), 1)
    chosen = (needed.T[:, None, :] == 1) & (earlier_need.T[:, None, :] == slot_index)
    selector = chosen.astype(jnp.bfloat16).reshape(block_count * slot_count, sample_count)
    own_lists = lax.dynamic_index_in_dim(upstream, own_block, axis=1, keepdims=False)
    usable = own_lists >= 0
    matches = jnp.any(own_lists[:, :, None, None] == own_lists[None, None, :, :], axis=3)
    sample_ids = lax.broadcasted_iota(jnp.int32, (sample_count, sample_count), 0)
    earlier = lax.broadcasted_iota(jnp.int32, (sample_count, sample_count), 1) < sample_ids
    position = jnp.sum((matches & earlier[:, None, :]).astype(jnp.int32), axis=2)
    flat_slot = own_lists * slot_count + position
    fetch_at = jnp.where(usable, flat_slot, 0)
    payload = jnp.concatenate([key_rows, value_rows], axis=1).reshape(
        sample_count, block_rows * pair_width
    )
    packed = jnp.dot(selector, payload, preferred_element_type=jnp.float32).astype(jnp.bfloat16)
    arrived = lax.all_to_all(
        packed.reshape(block_count, slot_count, block_rows, pair_width),
        "turb",
        split_axis=0,
        concat_axis=0,
        tiled=True,
    )
    fetched = arrived.reshape(block_count * slot_count, block_rows, pair_width)[fetch_at]
    upstream_keys = fetched[..., :model_width]
    upstream_values = fetched[..., model_width:]
    key_count = (1 + UPSTREAM) * block_rows
    key_all = jnp.concatenate(
        [key_rows.reshape(sample_count, 1, block_rows, model_width), upstream_keys], axis=1
    ).reshape(sample_count, key_count, model_width)
    value_all = jnp.concatenate(
        [value_rows.reshape(sample_count, 1, block_rows, model_width), upstream_values], axis=1
    ).reshape(sample_count, key_count, model_width)
    block_usable = jnp.concatenate([jnp.ones((sample_count, 1), dtype=jnp.bool_), usable], axis=1)
    key_usable = jnp.repeat(block_usable, block_rows, axis=1)
    grad_attended = jnp.dot(grad_rows, out_weight.T, preferred_element_type=jnp.float32).astype(
        jnp.bfloat16
    )
    group_size = min(sample_count, max(1, 512 // block_rows))
    while sample_count % group_size != 0:
        group_size = group_size - 1
    group_count = sample_count // group_size

    def grouped(tensor):
        return tensor.reshape((group_count, group_size) + tensor.shape[1:])

    attended, grad_queries, pair_terms = lax.map(
        attend,
        (
            grouped(queries.reshape(sample_count, block_rows, model_width)),
            grouped(key_all),
            grouped(value_all),
            grouped(key_usable),
            grouped(grad_attended.reshape(sample_count, block_rows, model_width)),
        ),
    )
    attended = attended.reshape(flat_rows, model_width)
    grad_queries = grad_queries.reshape(flat_rows, model_width)
    pair_terms = pair_terms.reshape(sample_count, 1 + UPSTREAM, block_rows, pair_width)
    layer_output = (
        (
            input_rows.astype(jnp.float32)
            + jnp.dot(attended, out_weight, preferred_element_type=jnp.float32)
        )
        .astype(jnp.bfloat16)
        .reshape(inflow.shape)
    )
    outgoing = (
        pair_terms[:, 1:]
        .astype(jnp.bfloat16)
        .reshape(sample_count * UPSTREAM, block_rows, pair_width)
    )
    target = jnp.where(usable, flat_slot, block_count * slot_count).reshape(-1)
    outbound = (
        jnp.zeros((block_count * slot_count, block_rows, pair_width), jnp.bfloat16)
        .at[target]
        .set(outgoing, mode="drop")
    )
    sum_out = jnp.dot(attended.T, grad_rows, preferred_element_type=jnp.float32)
    sum_query = jnp.dot(normed.T, grad_queries, preferred_element_type=jnp.float32)
    returned = lax.all_to_all(
        outbound.reshape(block_count, slot_count, block_rows, pair_width),
        "turb",
        split_axis=0,
        concat_axis=0,
        tiled=True,
    )
    remote = jnp.dot(
        selector.T,
        returned.reshape(block_count * slot_count, block_rows * pair_width),
        preferred_element_type=jnp.float32,
    )
    combined = (
        (pair_terms[:, 0].reshape(sample_count, block_rows * pair_width) + remote)
        .astype(jnp.bfloat16)
        .reshape(flat_rows, pair_width)
    )
    grad_keys = combined[:, :model_width]
    grad_values = combined[:, model_width:]
    sum_key = jnp.dot(normed.T, grad_keys, preferred_element_type=jnp.float32)
    sum_value = jnp.dot(normed.T, grad_values, preferred_element_type=jnp.float32)
    grad_normed = jnp.dot(grad_queries, query_weight.T, preferred_element_type=jnp.float32)
    grad_normed = grad_normed + jnp.dot(grad_keys, key_weight.T, preferred_element_type=jnp.float32)
    grad_normed = grad_normed + jnp.dot(
        grad_values, value_weight.T, preferred_element_type=jnp.float32
    )
    sum_gain = jnp.sum(grad_normed * scaled, axis=0)
    grad_scaled = grad_normed * norm_gain
    grad_input = inverse * (
        grad_scaled
        - jnp.mean(grad_scaled, axis=-1, keepdims=True)
        - scaled * jnp.mean(grad_scaled * scaled, axis=-1, keepdims=True)
    )
    grad_inflow = (
        (grad_rows.astype(jnp.float32) + grad_input).astype(jnp.bfloat16).reshape(inflow.shape)
    )
    sum_query, sum_key, sum_value, sum_out, sum_gain = lax.psum(
        (sum_query, sum_key, sum_value, sum_out, sum_gain), ("sample", "turb")
    )
    return (layer_output, grad_inflow, sum_query, sum_key, sum_value, sum_out, sum_gain)


HEAD_PAIR = 2
LOG2_E = 1.4426950408889634


def project_kernel(x_ref, gain_ref, wq_ref, wk_ref, wv_ref, wkt_ref, wvt_ref,
                   normed_ref, q_ref, k_ref, v_ref, kt_ref, vt_ref):
    _, _, normed = normalize(x_ref[...], gain_ref[...])
    normed_ref[...] = normed

    def straight(weight_ref):
        return jnp.dot(normed, weight_ref[...], preferred_element_type=jnp.float32).astype(
            jnp.bfloat16
        )

    def turned(weight_ref):
        return lax.dot_general(
            weight_ref[...], normed, (((1,), (1,)), ((), ())), preferred_element_type=jnp.float32
        ).astype(jnp.bfloat16)

    q_ref[...] = straight(wq_ref)
    k_ref[...] = straight(wk_ref)
    v_ref[...] = straight(wv_ref)
    kt_ref[...] = turned(wkt_ref)
    vt_ref[...] = turned(wvt_ref)


def project(rows, norm_gain, query_weight, key_weight, value_weight):
    row_count, width = rows.shape
    step = min(row_count, 256)
    whole = lambda shape: pl.BlockSpec(shape, lambda i: (0,) * len(shape))
    by_row = pl.BlockSpec((step, width), lambda i: (i, 0))
    by_column = pl.BlockSpec((width, step), lambda i: (0, i))
    flat = jax.ShapeDtypeStruct((row_count, width), jnp.bfloat16)
    turned = jax.ShapeDtypeStruct((width, row_count), jnp.bfloat16)
    return pl.pallas_call(
        project_kernel,
        grid=(row_count // step,),
        in_specs=[by_row, whole((1, width))] + [whole((width, width))] * 5,
        out_specs=[by_row] * 4 + [by_column] * 2,
        out_shape=[flat] * 4 + [turned] * 2,
        compiler_params=pltpu.CompilerParams(vmem_limit_bytes=32 * 2**20),
        cost_estimate=pl.CostEstimate(
            flops=10 * row_count * width * width,
            bytes_accessed=14 * row_count * width + 10 * width * width,
            transcendentals=0,
        ),
        name="project",
    )(rows, norm_gain.reshape(1, width), query_weight, key_weight, value_weight,
      key_weight.T, value_weight.T)


def pair_kernel(block_rows, block_count, head_dim, lists_ref, q_ref, k_ref, v_ref, kt_ref, vt_ref,
                cot_ref, wo_ref, att_ref, gq_ref, gk_ref, gv_ref, ga_ref, gk_acc, gv_acc):
    width = HEAD_PAIR * head_dim
    ga_ref[...] = lax.dot_general(
        cot_ref[...], wo_ref[...], (((1,), (1,)), ((), ())), preferred_element_type=jnp.float32
    ).astype(jnp.bfloat16)
    gk_acc[...] = jnp.zeros_like(gk_acc)
    gv_acc[...] = jnp.zeros_like(gv_acc)
    scale = head_dim ** (-0.5)

    def split_heads(rows):
        lane = lax.broadcasted_iota(jnp.int32, rows.shape, 1)
        wide = rows.astype(jnp.float32)
        return jnp.concatenate(
            [jnp.where(lane < head_dim, wide, 0.0), jnp.where(lane >= head_dim, wide, 0.0)], axis=0
        ).astype(jnp.bfloat16)

    def join_heads(wide):
        first = lax.broadcasted_iota(jnp.int32, (width, block_rows), 0) < head_dim
        return jnp.where(first, wide[:, :block_rows], wide[:, block_rows:]).astype(jnp.bfloat16)

    def attend_block(block, used):
        starts = [pl.multiple_of(block * block_rows, block_rows)]
        for slot in range(used):
            starts.append(
                pl.multiple_of(lists_ref[block * UPSTREAM + slot] * block_rows, block_rows)
            )
        own = pl.ds(starts[0], block_rows)

        def stacked(ref):
            return jnp.concatenate([ref[pl.ds(s, block_rows), :] for s in starts], axis=0)

        def beside(ref):
            return jnp.concatenate([ref[:, pl.ds(s, block_rows)] for s in starts], axis=1)

        queries = split_heads(q_ref[own, :])
        grads = split_heads(ga_ref[own, :])
        scores = lax.dot_general(
            stacked(k_ref), queries, (((1,), (1,)), ((), ())), preferred_element_type=jnp.float32
        )
        highest = jnp.max(scores, axis=0, keepdims=True)
        weights = jnp.exp2((scores - highest) * (scale * LOG2_E))
        probs = weights * (1.0 / jnp.sum(weights, axis=0, keepdims=True))
        probs_b = probs.astype(jnp.bfloat16)
        att_ref[:, own] = join_heads(
            jnp.dot(beside(vt_ref), probs_b, preferred_element_type=jnp.float32)
        )
        grad_probs = lax.dot_general(
            stacked(v_ref), grads * scale, (((1,), (1,)), ((), ())),
            preferred_element_type=jnp.float32,
        )
        total = jnp.sum(probs * grad_probs, axis=0, keepdims=True)
        grad_scores = (probs * (grad_probs - total)).astype(jnp.bfloat16)
        gq_ref[:, own] = join_heads(
            jnp.dot(beside(kt_ref), grad_scores, preferred_element_type=jnp.float32)
        )
        grad_keys = jnp.dot(grad_scores, queries, preferred_element_type=jnp.float32)
        grad_values = jnp.dot(probs_b, grads, preferred_element_type=jnp.float32)
        for slot, start in enumerate(starts):
            rows = pl.ds(start, block_rows)
            part = slice(slot * block_rows, (slot + 1) * block_rows)
            for acc, terms in ((gk_acc, grad_keys), (gv_acc, grad_values)):
                term = terms[part]
                if slot > 0:
                    term = term.astype(jnp.bfloat16).astype(jnp.float32)
                acc[rows, :] += term

    def step(block, carry):
        used = jnp.int32(0)
        for slot in range(UPSTREAM):
            used = used + (lists_ref[block * UPSTREAM + slot] >= 0).astype(jnp.int32)
        for count in range(UPSTREAM + 1):
            @pl.when(used == count)
            def _():
                attend_block(block, count)
        return carry

    lax.fori_loop(0, block_count, step, 0)
    gk_ref[...] = gk_acc[...].astype(jnp.bfloat16)
    gv_ref[...] = gv_acc[...].astype(jnp.bfloat16)


def attend_sample(lists, queries, keys, values, keys_t, values_t, cotangent, out_weight, block_rows):
    row_count, width = queries.shape
    head_dim = width // HEADS
    pair = HEAD_PAIR * head_dim
    block_count = row_count // block_rows
    by_column = pl.BlockSpec((row_count, pair), lambda p, lists: (0, p))
    by_row = pl.BlockSpec((pair, row_count), lambda p, lists: (p, 0))
    flat = jax.ShapeDtypeStruct((row_count, width), jnp.bfloat16)
    turned = jax.ShapeDtypeStruct((width, row_count), jnp.bfloat16)
    return pl.pallas_call(
        lambda *refs: pair_kernel(block_rows, block_count, head_dim, *refs),
        grid_spec=pltpu.PrefetchScalarGridSpec(
            num_scalar_prefetch=1,
            grid=(width // pair,),
            in_specs=[
                by_column, by_column, by_column, by_row, by_row,
                pl.BlockSpec((row_count, width), lambda p, lists: (0, 0)),
                pl.BlockSpec((pair, width), lambda p, lists: (p, 0)),
            ],
            out_specs=[by_row, by_row, by_column, by_column],
            scratch_shapes=[
                pltpu.VMEM((row_count, pair), jnp.bfloat16),
                pltpu.VMEM((row_count, pair), jnp.float32),
                pltpu.VMEM((row_count, pair), jnp.float32),
            ],
        ),
        out_shape=[turned, turned, flat, flat],
        compiler_params=pltpu.CompilerParams(vmem_limit_bytes=40 * 2**20),
        cost_estimate=pl.CostEstimate(
            flops=2 * row_count * width * width + 48 * row_count * block_rows * width,
            bytes_accessed=20 * row_count * width,
            transcendentals=row_count * 4 * block_rows * HEADS,
        ),
        name="attend",
    )(lists, queries, keys, values, keys_t, values_t, cotangent, out_weight)


def by_sample(
    inflow,
    cotangent,
    norm_gain,
    query_weight,
    key_weight,
    value_weight,
    out_weight,
    adjacency,
    sectors,
):
    sample_count, block_rows, width = inflow.shape
    sample_axis = lax.axis_size("sample")
    block_count = lax.axis_size("turb")
    row_count = block_count * block_rows
    sector = lax.dynamic_index_in_dim(sectors, lax.axis_index("turb"), keepdims=False)
    lists = lax.dynamic_index_in_dim(adjacency, sector, keepdims=False).reshape(-1)

    def exchange(tensor):
        return lax.all_to_all(tensor, "turb", split_axis=0, concat_axis=0, tiled=True)

    rows = exchange(inflow)
    rows, cotangent = lax.optimization_barrier((rows, cotangent))
    rows = rows.reshape(row_count, width)
    grad_rows = exchange(cotangent).reshape(row_count, width)
    normed, queries, keys, values, keys_t, values_t = project(
        rows, norm_gain, query_weight, key_weight, value_weight
    )
    attended_t, grad_queries_t, grad_keys, grad_values = attend_sample(
        lists, queries, keys, values, keys_t, values_t, grad_rows, out_weight, block_rows
    )

    def contract(left, right, left_dim, right_dim):
        return lax.dot_general(
            left, right, (((left_dim,), (right_dim,)), ((), ())), preferred_element_type=jnp.float32
        )

    layer_rows = (
        rows.astype(jnp.float32) + contract(attended_t, out_weight, 0, 0)
    ).astype(jnp.bfloat16)
    layer_output = exchange(layer_rows.reshape(inflow.shape))

    sums = jnp.concatenate(
        [
            contract(normed, grad_queries_t, 0, 1),
            contract(normed, grad_keys, 0, 0),
            contract(normed, grad_values, 0, 0),
            contract(attended_t, grad_rows, 1, 0),
        ],
        axis=0,
    ).astype(jnp.bfloat16)
    share = 4 * width // (sample_axis * block_count)
    sums = sums.reshape(sample_axis, block_count * share, width)
    sums = lax.all_to_all(sums, "sample", split_axis=0, concat_axis=0, tiled=True)
    sums = jnp.sum(sums.astype(jnp.float32), axis=0).astype(jnp.bfloat16)
    sums = sums.reshape(block_count, share, width)
    sums = lax.all_to_all(sums, "turb", split_axis=0, concat_axis=0, tiled=True)
    sums = jnp.sum(sums.astype(jnp.float32), axis=0).astype(jnp.bfloat16)
    sums = lax.all_gather(sums, ("sample", "turb"), axis=0, tiled=True).astype(jnp.float32)
    sum_query, sum_key, sum_value, sum_out = (
        sums[i * width : (i + 1) * width] for i in range(4)
    )

    grad_normed = contract(grad_queries_t, query_weight, 0, 1)
    grad_normed = grad_normed + contract(grad_keys, key_weight, 1, 1)
    grad_normed = grad_normed + contract(grad_values, value_weight, 1, 1)
    scaled, inverse, _ = normalize(rows, norm_gain)
    sum_gain = jnp.sum(grad_normed * scaled, axis=0)
    grad_scaled = grad_normed * norm_gain
    grad_input = inverse * (
        grad_scaled
        - jnp.mean(grad_scaled, axis=-1, keepdims=True)
        - scaled * jnp.mean(grad_scaled * scaled, axis=-1, keepdims=True)
    )
    grad_inflow = (grad_rows.astype(jnp.float32) + grad_input).astype(jnp.bfloat16)
    grad_inflow = exchange(grad_inflow.reshape(inflow.shape))
    sum_gain = jnp.sum(lax.all_gather(sum_gain, ("sample", "turb")), axis=0)
    return (layer_output, grad_inflow, sum_query, sum_key, sum_value, sum_out, sum_gain)


def solution(mesh):
    placed = (
        P("sample", "turb", None),
        P("sample", "turb", None),
        P(),
        P(),
        P(),
        P(),
        P(),
        P(),
        P("sample"),
    )

    def plan(*args):
        sample_count = args[0].shape[0]
        if sample_count == mesh.shape["turb"]:
            return by_sample(*args)
        return on_device(*args)

    return jax.shard_map(
        plan,
        mesh=mesh,
        in_specs=placed,
        out_specs=(P("sample", "turb", None), P("sample", "turb", None), P(), P(), P(), P(), P()),
        check_vma=False,
    )
```

```python
import jax
import jax.numpy as jnp
from jax import lax
from jax.experimental import pallas as pl
from jax.experimental.pallas import tpu as pltpu
from jax.sharding import PartitionSpec as P

HEADS = 8
UPSTREAM = 3
SECTORS = 8
REPEAT = 1


epsilon = 1e-05


def normalize(row_block, norm_gain):
    widened = row_block.astype(jnp.float32)
    centred = widened - jnp.mean(widened, axis=-1, keepdims=True)
    inverse = lax.rsqrt(jnp.mean(centred * centred, axis=-1, keepdims=True) + epsilon)
    scaled = centred * inverse
    return (scaled, inverse, (scaled * norm_gain).astype(jnp.bfloat16))


def attend(pieces):
    queries, key_rows, value_rows, key_usable, grad_attended = pieces
    batch_count, query_count, model_width = queries.shape
    key_count = key_rows.shape[1]
    head_dim = model_width // HEADS
    score_scale = head_dim ** (-0.5)
    query_heads = queries.reshape(batch_count, query_count, HEADS, head_dim)
    key_heads = key_rows.reshape(batch_count, key_count, HEADS, head_dim)
    value_heads = value_rows.reshape(batch_count, key_count, HEADS, head_dim)
    grad_heads = grad_attended.reshape(batch_count, query_count, HEADS, head_dim)
    scores = (
        jnp.einsum("nqhd,nkhd->nhqk", query_heads, key_heads, preferred_element_type=jnp.float32)
        * score_scale
    )
    scores = jnp.where(key_usable[:, None, None, :], scores, -1e30)
    highest = jnp.max(scores, axis=-1, keepdims=True)
    weights = jnp.exp(scores - highest)
    probabilities = weights / jnp.sum(weights, axis=-1, keepdims=True)
    rounded = probabilities.astype(jnp.bfloat16)
    attended = jnp.einsum(
        "nhqk,nkhd->nqhd", rounded, value_heads, preferred_element_type=jnp.float32
    ).astype(jnp.bfloat16)
    grad_probs = jnp.einsum(
        "nqhd,nkhd->nhqk", grad_heads, value_heads, preferred_element_type=jnp.float32
    )
    centred = grad_probs - jnp.sum(probabilities * grad_probs, axis=-1, keepdims=True)
    grad_scores = (probabilities * centred * score_scale).astype(jnp.bfloat16)
    grad_queries = jnp.einsum(
        "nhqk,nkhd->nqhd", grad_scores, key_heads, preferred_element_type=jnp.float32
    ).astype(jnp.bfloat16)
    grad_keys = jnp.einsum(
        "nhqk,nqhd->nkhd", grad_scores, query_heads, preferred_element_type=jnp.float32
    )
    grad_values = jnp.einsum(
        "nhqk,nqhd->nkhd", rounded, grad_heads, preferred_element_type=jnp.float32
    )
    pair_terms = jnp.concatenate(
        [
            grad_keys.reshape(batch_count, key_count, model_width),
            grad_values.reshape(batch_count, key_count, model_width),
        ],
        axis=-1,
    )
    return (
        attended.reshape(batch_count, query_count, model_width),
        grad_queries.reshape(batch_count, query_count, model_width),
        pair_terms,
    )


def on_device(
    inflow,
    cotangent,
    norm_gain,
    query_weight,
    key_weight,
    value_weight,
    out_weight,
    adjacency,
    sectors,
):
    sample_count, block_rows, model_width = inflow.shape
    block_count = lax.axis_size("turb")
    own_block = lax.axis_index("turb")
    slot_count = REPEAT * ((SECTORS * UPSTREAM + block_count - 2) // (block_count - 1))
    flat_rows = sample_count * block_rows
    pair_width = 2 * model_width
    input_rows = inflow.reshape(flat_rows, model_width)
    grad_rows = cotangent.reshape(flat_rows, model_width)
    scaled, inverse, normed = normalize(input_rows, norm_gain)
    queries = jnp.dot(normed, query_weight, preferred_element_type=jnp.float32).astype(jnp.bfloat16)
    key_rows = jnp.dot(normed, key_weight, preferred_element_type=jnp.float32).astype(jnp.bfloat16)
    value_rows = jnp.dot(normed, value_weight, preferred_element_type=jnp.float32).astype(
        jnp.bfloat16
    )
    upstream = adjacency[sectors]
    needed = jnp.any(upstream == own_block, axis=2).astype(jnp.int32)
    earlier_need = jnp.cumsum(needed, axis=0) - needed
    slot_index = lax.broadcasted_iota(jnp.int32, (block_count, slot_count, sample_count), 1)
    chosen = (needed.T[:, None, :] == 1) & (earlier_need.T[:, None, :] == slot_index)
    selector = chosen.astype(jnp.bfloat16).reshape(block_count * slot_count, sample_count)
    own_lists = lax.dynamic_index_in_dim(upstream, own_block, axis=1, keepdims=False)
    usable = own_lists >= 0
    matches = jnp.any(own_lists[:, :, None, None] == own_lists[None, None, :, :], axis=3)
    sample_ids = lax.broadcasted_iota(jnp.int32, (sample_count, sample_count), 0)
    earlier = lax.broadcasted_iota(jnp.int32, (sample_count, sample_count), 1) < sample_ids
    position = jnp.sum((matches & earlier[:, None, :]).astype(jnp.int32), axis=2)
    flat_slot = own_lists * slot_count + position
    fetch_at = jnp.where(usable, flat_slot, 0)
    payload = jnp.concatenate([key_rows, value_rows], axis=1).reshape(
        sample_count, block_rows * pair_width
    )
    packed = jnp.dot(selector, payload, preferred_element_type=jnp.float32).astype(jnp.bfloat16)
    arrived = lax.all_to_all(
        packed.reshape(block_count, slot_count, block_rows, pair_width),
        "turb",
        split_axis=0,
        concat_axis=0,
        tiled=True,
    )
    fetched = arrived.reshape(block_count * slot_count, block_rows, pair_width)[fetch_at]
    upstream_keys = fetched[..., :model_width]
    upstream_values = fetched[..., model_width:]
    key_count = (1 + UPSTREAM) * block_rows
    key_all = jnp.concatenate(
        [key_rows.reshape(sample_count, 1, block_rows, model_width), upstream_keys], axis=1
    ).reshape(sample_count, key_count, model_width)
    value_all = jnp.concatenate(
        [value_rows.reshape(sample_count, 1, block_rows, model_width), upstream_values], axis=1
    ).reshape(sample_count, key_count, model_width)
    block_usable = jnp.concatenate([jnp.ones((sample_count, 1), dtype=jnp.bool_), usable], axis=1)
    key_usable = jnp.repeat(block_usable, block_rows, axis=1)
    grad_attended = jnp.dot(grad_rows, out_weight.T, preferred_element_type=jnp.float32).astype(
        jnp.bfloat16
    )
    group_size = min(sample_count, max(1, 512 // block_rows))
    while sample_count % group_size != 0:
        group_size = group_size - 1
    group_count = sample_count // group_size

    def grouped(tensor):
        return tensor.reshape((group_count, group_size) + tensor.shape[1:])

    attended, grad_queries, pair_terms = lax.map(
        attend,
        (
            grouped(queries.reshape(sample_count, block_rows, model_width)),
            grouped(key_all),
            grouped(value_all),
            grouped(key_usable),
            grouped(grad_attended.reshape(sample_count, block_rows, model_width)),
        ),
    )
    attended = attended.reshape(flat_rows, model_width)
    grad_queries = grad_queries.reshape(flat_rows, model_width)
    pair_terms = pair_terms.reshape(sample_count, 1 + UPSTREAM, block_rows, pair_width)
    layer_output = (
        (
            input_rows.astype(jnp.float32)
            + jnp.dot(attended, out_weight, preferred_element_type=jnp.float32)
        )
        .astype(jnp.bfloat16)
        .reshape(inflow.shape)
    )
    outgoing = (
        pair_terms[:, 1:]
        .astype(jnp.bfloat16)
        .reshape(sample_count * UPSTREAM, block_rows, pair_width)
    )
    target = jnp.where(usable, flat_slot, block_count * slot_count).reshape(-1)
    outbound = (
        jnp.zeros((block_count * slot_count, block_rows, pair_width), jnp.bfloat16)
        .at[target]
        .set(outgoing, mode="drop")
    )
    sum_out = jnp.dot(attended.T, grad_rows, preferred_element_type=jnp.float32)
    sum_query = jnp.dot(normed.T, grad_queries, preferred_element_type=jnp.float32)
    returned = lax.all_to_all(
        outbound.reshape(block_count, slot_count, block_rows, pair_width),
        "turb",
        split_axis=0,
        concat_axis=0,
        tiled=True,
    )
    remote = jnp.dot(
        selector.T,
        returned.reshape(block_count * slot_count, block_rows * pair_width),
        preferred_element_type=jnp.float32,
    )
    combined = (
        (pair_terms[:, 0].reshape(sample_count, block_rows * pair_width) + remote)
        .astype(jnp.bfloat16)
        .reshape(flat_rows, pair_width)
    )
    grad_keys = combined[:, :model_width]
    grad_values = combined[:, model_width:]
    sum_key = jnp.dot(normed.T, grad_keys, preferred_element_type=jnp.float32)
    sum_value = jnp.dot(normed.T, grad_values, preferred_element_type=jnp.float32)
    grad_normed = jnp.dot(grad_queries, query_weight.T, preferred_element_type=jnp.float32)
    grad_normed = grad_normed + jnp.dot(grad_keys, key_weight.T, preferred_element_type=jnp.float32)
    grad_normed = grad_normed + jnp.dot(
        grad_values, value_weight.T, preferred_element_type=jnp.float32
    )
    sum_gain = jnp.sum(grad_normed * scaled, axis=0)
    grad_scaled = grad_normed * norm_gain
    grad_input = inverse * (
        grad_scaled
        - jnp.mean(grad_scaled, axis=-1, keepdims=True)
        - scaled * jnp.mean(grad_scaled * scaled, axis=-1, keepdims=True)
    )
    grad_inflow = (
        (grad_rows.astype(jnp.float32) + grad_input).astype(jnp.bfloat16).reshape(inflow.shape)
    )
    sum_query, sum_key, sum_value, sum_out, sum_gain = lax.psum(
        (sum_query, sum_key, sum_value, sum_out, sum_gain), ("sample", "turb")
    )
    return (layer_output, grad_inflow, sum_query, sum_key, sum_value, sum_out, sum_gain)


PAIR = 2
QUAD = 4
LOG2_E = 1.4426950408889634
VMEM_LIMIT = 58 * 2**20


def contract(left, right, left_dim, right_dim):
    return lax.dot_general(
        left, right, (((left_dim,), (right_dim,)), ((), ())), preferred_element_type=jnp.float32
    )


def split_heads(rows, head_dim):
    lane = lax.broadcasted_iota(jnp.int32, rows.shape, 1)
    wide = rows.astype(jnp.float32)
    return jnp.concatenate(
        [jnp.where(lane < head_dim, wide, 0.0), jnp.where(lane >= head_dim, wide, 0.0)], axis=0
    ).astype(jnp.bfloat16)


def join_heads(wide, head_dim):
    block_rows = wide.shape[1] // PAIR
    first = lax.broadcasted_iota(jnp.int32, (wide.shape[0], block_rows), 0) < head_dim
    return jnp.where(first, wide[:, :block_rows], wide[:, block_rows:])


def for_each_block(lists_ref, block_count, block_rows, work):
    def step(block, carry):
        used = jnp.int32(0)
        for slot in range(UPSTREAM):
            used = used + (lists_ref[block * UPSTREAM + slot] >= 0).astype(jnp.int32)
        for count in range(UPSTREAM + 1):

            @pl.when(used == count)
            def _():
                sources = [block] + [
                    lists_ref[block * UPSTREAM + slot] for slot in range(count)
                ]
                work(block, [pl.multiple_of(s * block_rows, block_rows) for s in sources])

        return carry

    lax.fori_loop(0, block_count, step, 0)


def stacked(ref, starts, block_rows, lanes):
    return jnp.concatenate([ref[pl.ds(s, block_rows), lanes] for s in starts], axis=0)


def beside(ref, starts, block_rows, rows):
    return jnp.concatenate([ref[rows, pl.ds(s, block_rows)] for s in starts], axis=1)


def forward_kernel(block_rows, head_dim, lists_ref, x_ref, gain_ref, wq_ref, wk_ref, wv_ref,
                   wkt_ref, wvt_ref, wo_ref, normed_t_ref, q_ref, k_ref, v_ref, kt_ref, att_ref,
                   top_ref, inverse_ref, out_ref, normed_ref, vt_ref, rows_ref, sum_ref):
    row_count = x_ref.shape[0]
    quad = pl.program_id(0)
    pair = PAIR * head_dim
    exponent = head_dim ** (-0.5) * LOG2_E
    chunk = min(row_count, 256)

    @pl.when(quad == 0)
    def _():
        for start in range(0, row_count, chunk):
            part = slice(start, start + chunk)
            scaled, _, normed = normalize(x_ref[part, :], gain_ref[...])
            normed_ref[part, :] = normed
            normed_t_ref[:, part] = (scaled * gain_ref[...]).T.astype(jnp.bfloat16)

    normed = normed_ref[...]
    q_ref[...] = contract(normed, wq_ref[...], 1, 0).astype(jnp.bfloat16)
    k_ref[...] = contract(normed, wk_ref[...], 1, 0).astype(jnp.bfloat16)
    v_ref[...] = contract(normed, wv_ref[...], 1, 0).astype(jnp.bfloat16)
    kt_ref[...] = contract(wkt_ref[...], normed, 1, 1).astype(jnp.bfloat16)
    vt_ref[...] = contract(wvt_ref[...], normed, 1, 1).astype(jnp.bfloat16)

    def work(block, starts):
        own = pl.ds(starts[0], block_rows)
        lanes = [slice(p * pair, (p + 1) * pair) for p in range(QUAD // PAIR)]
        scores = [
            contract(
                stacked(k_ref, starts, block_rows, lane), split_heads(q_ref[own, lane], head_dim), 1, 1
            )
            for lane in lanes
        ]
        for p, lane in enumerate(lanes):
            highest = jnp.max(scores[p], axis=0, keepdims=True)
            weights = jnp.exp2((scores[p] - highest) * exponent)
            inverse = 1.0 / jnp.sum(weights, axis=0, keepdims=True)
            probs = (weights * inverse).astype(jnp.bfloat16)
            top_ref[0, pl.ds(block * (QUAD // PAIR) + p, 1), :] = highest
            inverse_ref[0, pl.ds(block * (QUAD // PAIR) + p, 1), :] = inverse
            joined = join_heads(
                jnp.dot(
                    beside(vt_ref, starts, block_rows, lane),
                    probs,
                    preferred_element_type=jnp.float32,
                ),
                head_dim,
            )
            att_ref[lane, own] = joined.astype(jnp.bfloat16)
            rows_ref[own, lane] = joined.T.astype(jnp.bfloat16)

    for_each_block(lists_ref, row_count // block_rows, block_rows, work)
    part = contract(rows_ref[...], wo_ref[...], 1, 0)

    @pl.when(quad == 0)
    def _():
        sum_ref[...] = x_ref[...].astype(jnp.float32) + part

    @pl.when(quad > 0)
    def _():
        sum_ref[...] += part

    @pl.when(quad == pl.num_programs(0) - 1)
    def _():
        out_ref[...] = sum_ref[...].astype(jnp.bfloat16)


def forward(lists, rows, norm_gain, query_weight, key_weight, value_weight, out_weight, block_rows):
    row_count, width = rows.shape
    head_dim = width // HEADS
    quad = QUAD * head_dim
    quads = width // quad
    stat_rows = row_count // block_rows * (QUAD // PAIR)
    fixed = lambda *shape: pl.BlockSpec(shape, lambda p, lists: (0,) * len(shape))
    across = lambda size: pl.BlockSpec((size, quad), lambda p, lists: (0, p))
    down = lambda size: pl.BlockSpec((quad, size), lambda p, lists: (p, 0))
    stat = pl.BlockSpec((1, stat_rows, PAIR * block_rows), lambda p, lists: (p, 0, 0))
    flat = jax.ShapeDtypeStruct((row_count, width), jnp.bfloat16)
    turned = jax.ShapeDtypeStruct((width, row_count), jnp.bfloat16)
    stats = jax.ShapeDtypeStruct((quads, stat_rows, PAIR * block_rows), jnp.float32)
    return pl.pallas_call(
        lambda *refs: forward_kernel(block_rows, head_dim, *refs),
        grid_spec=pltpu.PrefetchScalarGridSpec(
            num_scalar_prefetch=1,
            grid=(quads,),
            in_specs=[fixed(row_count, width), fixed(1, width)]
            + [across(width)] * 3
            + [down(width)] * 3,
            out_specs=[fixed(width, row_count)]
            + [across(row_count)] * 3
            + [down(row_count)] * 2
            + [stat] * 2
            + [fixed(row_count, width)],
            scratch_shapes=[
                pltpu.VMEM((row_count, width), jnp.bfloat16),
                pltpu.VMEM((quad, row_count), jnp.bfloat16),
                pltpu.VMEM((row_count, quad), jnp.bfloat16),
                pltpu.VMEM((row_count, width), jnp.float32),
            ],
        ),
        out_shape=[turned, flat, flat, flat, turned, turned, stats, stats, flat],
        compiler_params=pltpu.CompilerParams(vmem_limit_bytes=VMEM_LIMIT),
        cost_estimate=pl.CostEstimate(
            flops=12 * row_count * width * width + 32 * row_count * block_rows * width,
            bytes_accessed=20 * row_count * width,
            transcendentals=row_count * 4 * block_rows * HEADS,
        ),
        name="forward",
    )(lists, rows, norm_gain.reshape(1, width), query_weight, key_weight, value_weight,
      key_weight.T, value_weight.T, out_weight)


def backward_kernel(block_rows, head_dim, lists_ref, cot_ref, wo_ref, normed_t_ref, q_ref, k_ref,
                    v_ref, kt_ref, att_ref, top_ref, inverse_ref, gq_ref, gk_ref, gv_ref, sums_ref,
                    ga_ref, gk_acc, gv_acc):
    row_count, width = cot_ref.shape
    pair = PAIR * head_dim
    quad = QUAD * head_dim
    scale = head_dim ** (-0.5)
    ga_ref[...] = contract(cot_ref[...], wo_ref[...], 1, 1).astype(jnp.bfloat16)
    gk_acc[...] = jnp.zeros_like(gk_acc)
    gv_acc[...] = jnp.zeros_like(gv_acc)

    def work(block, starts):
        own = pl.ds(starts[0], block_rows)
        lanes = [slice(p * pair, (p + 1) * pair) for p in range(QUAD // PAIR)]
        queries = [split_heads(q_ref[own, lane], head_dim) for lane in lanes]
        grads = [split_heads(ga_ref[own, lane], head_dim) for lane in lanes]
        scores = [
            contract(stacked(k_ref, starts, block_rows, lane), queries[p], 1, 1)
            for p, lane in enumerate(lanes)
        ]
        grad_probs = [
            contract(stacked(v_ref, starts, block_rows, lane), grads[p] * scale, 1, 1)
            for p, lane in enumerate(lanes)
        ]
        for p, lane in enumerate(lanes):
            stat = pl.ds(block * (QUAD // PAIR) + p, 1)
            probs = jnp.exp2((scores[p] - top_ref[0, stat, :]) * (scale * LOG2_E))
            probs = probs * inverse_ref[0, stat, :]
            total = jnp.sum(probs * grad_probs[p], axis=0, keepdims=True)
            grad_scores = (probs * (grad_probs[p] - total)).astype(jnp.bfloat16)
            probs_b = probs.astype(jnp.bfloat16)
            grad_values = jnp.dot(probs_b, grads[p], preferred_element_type=jnp.float32)
            grad_keys = jnp.dot(grad_scores, queries[p], preferred_element_type=jnp.float32)
            joined = join_heads(
                jnp.dot(
                    beside(kt_ref, starts, block_rows, lane),
                    grad_scores,
                    preferred_element_type=jnp.float32,
                ),
                head_dim,
            )
            gq_ref[own, lane] = joined.T.astype(jnp.bfloat16)
            for slot, start in enumerate(starts):
                rows = pl.ds(start, block_rows)
                part = slice(slot * block_rows, (slot + 1) * block_rows)
                for acc, terms in ((gk_acc, grad_keys), (gv_acc, grad_values)):
                    term = terms[part]
                    if slot > 0:
                        term = term.astype(jnp.bfloat16).astype(jnp.float32)
                    acc[rows, lane] += term

    for_each_block(lists_ref, row_count // block_rows, block_rows, work)
    gk_ref[...] = gk_acc[...].astype(jnp.bfloat16)
    gv_ref[...] = gv_acc[...].astype(jnp.bfloat16)
    for i, ref in enumerate((gq_ref, gk_ref, gv_ref)):
        sums_ref[i * width : (i + 1) * width, :] = contract(
            normed_t_ref[...], ref[...], 1, 0
        ).astype(jnp.bfloat16)
    for i in range(width // quad):
        start = 3 * width + i * quad
        sums_ref[start : start + quad, :] = contract(
            att_ref[...], cot_ref[:, i * quad : (i + 1) * quad], 1, 0
        ).astype(jnp.bfloat16)


def backward(lists, cotangent, out_weight, normed_t, queries, keys, values, keys_t, attended_t,
             tops, inverses, block_rows, which):
    row_count, width = cotangent.shape
    head_dim = width // HEADS
    quad = QUAD * head_dim
    fixed = lambda *shape: pl.BlockSpec(shape, lambda i, lists: (0,) * len(shape))
    across = pl.BlockSpec((row_count, quad), lambda i, lists: (0, which))
    down = lambda size: pl.BlockSpec((quad, size), lambda i, lists: (which, 0))
    stat = pl.BlockSpec((1,) + tops.shape[1:], lambda i, lists: (which, 0, 0))
    part = jax.ShapeDtypeStruct((row_count, quad), jnp.bfloat16)
    return pl.pallas_call(
        lambda *refs: backward_kernel(block_rows, head_dim, *refs),
        grid_spec=pltpu.PrefetchScalarGridSpec(
            num_scalar_prefetch=1,
            grid=(1,),
            in_specs=[fixed(row_count, width), down(width), fixed(width, row_count)]
            + [across] * 3
            + [down(row_count)] * 2
            + [stat] * 2,
            out_specs=[fixed(row_count, quad)] * 3 + [fixed(4 * width, quad)],
            scratch_shapes=[
                pltpu.VMEM((row_count, quad), jnp.bfloat16),
                pltpu.VMEM((row_count, quad), jnp.float32),
                pltpu.VMEM((row_count, quad), jnp.float32),
            ],
        ),
        out_shape=[part] * 3 + [jax.ShapeDtypeStruct((4 * width, quad), jnp.bfloat16)],
        compiler_params=pltpu.CompilerParams(vmem_limit_bytes=VMEM_LIMIT),
        cost_estimate=pl.CostEstimate(
            flops=10 * row_count * width * quad + 80 * row_count * block_rows * quad,
            bytes_accessed=14 * row_count * width,
            transcendentals=row_count * 4 * block_rows * QUAD,
        ),
        name="backward",
    )(lists, cotangent, out_weight, normed_t, queries, keys, values, keys_t, attended_t, tops,
      inverses)


def finish_kernel(quads, x_ref, cot_ref, gain_ref, wq_ref, wk_ref, wv_ref, *refs):
    grad_refs, (out_ref, sum_ref) = refs[:-2], refs[-2:]
    scaled, inverse, _ = normalize(x_ref[...], gain_ref[...])
    quad = grad_refs[0].shape[1]
    grad_normed = jnp.zeros(x_ref.shape, jnp.float32)
    for i in range(quads):
        lanes = slice(i * quad, (i + 1) * quad)
        for j, weight_ref in enumerate((wq_ref, wk_ref, wv_ref)):
            grad_normed += contract(grad_refs[3 * i + j][...], weight_ref[:, lanes], 1, 1)

    @pl.when(pl.program_id(0) == 0)
    def _():
        sum_ref[...] = jnp.zeros_like(sum_ref)

    sum_ref[...] += jnp.sum(grad_normed * scaled, axis=0, keepdims=True)
    grad_scaled = grad_normed * gain_ref[...]
    grad_input = inverse * (
        grad_scaled
        - jnp.mean(grad_scaled, axis=-1, keepdims=True)
        - scaled * jnp.mean(grad_scaled * scaled, axis=-1, keepdims=True)
    )
    out_ref[...] = (cot_ref[...].astype(jnp.float32) + grad_input).astype(jnp.bfloat16)


def finish(rows, cotangent, norm_gain, query_weight, key_weight, value_weight, grads):
    row_count, width = rows.shape
    quad = grads[0].shape[1]
    step = min(row_count, 256)
    fixed = lambda *shape: pl.BlockSpec(shape, lambda i: (0,) * len(shape))
    by_row = lambda size: pl.BlockSpec((step, size), lambda i: (i, 0))
    return pl.pallas_call(
        lambda *refs: finish_kernel(width // quad, *refs),
        grid=(row_count // step,),
        in_specs=[by_row(width)] * 2
        + [fixed(1, width)]
        + [fixed(width, width)] * 3
        + [by_row(quad)] * len(grads),
        out_specs=[by_row(width), fixed(1, width)],
        out_shape=[
            jax.ShapeDtypeStruct((row_count, width), jnp.bfloat16),
            jax.ShapeDtypeStruct((1, width), jnp.float32),
        ],
        compiler_params=pltpu.CompilerParams(vmem_limit_bytes=VMEM_LIMIT),
        cost_estimate=pl.CostEstimate(
            flops=6 * row_count * width * width,
            bytes_accessed=16 * row_count * width,
            transcendentals=0,
        ),
        name="finish",
    )(rows, cotangent, norm_gain.reshape(1, width), query_weight, key_weight, value_weight, *grads)


def swap(tensor, axis):
    return lax.all_to_all(tensor, axis, split_axis=0, concat_axis=0, tiled=True)


def reduce_sums(sums):
    row_count, width = sums.shape
    for axis in ("sample", "turb"):
        size = lax.axis_size(axis)
        sums = swap(sums.reshape(size, -1, width), axis)
        sums = jnp.sum(sums.astype(jnp.float32), axis=0).astype(jnp.bfloat16)
    for axis in ("turb", "sample"):
        size = lax.axis_size(axis)
        sums = swap(jnp.broadcast_to(sums, (size,) + sums.shape), axis).reshape(-1, width)
    return sums.astype(jnp.float32)


def by_sample(
    inflow,
    cotangent,
    norm_gain,
    query_weight,
    key_weight,
    value_weight,
    out_weight,
    adjacency,
    sectors,
):
    sample_count, block_rows, width = inflow.shape
    row_count = lax.axis_size("turb") * block_rows
    quads = HEADS // QUAD
    quad = width // quads
    sector = lax.dynamic_index_in_dim(sectors, lax.axis_index("turb"), keepdims=False)
    lists = lax.dynamic_index_in_dim(adjacency, sector, keepdims=False).reshape(-1)

    rows = swap(inflow, "turb")
    rows, cotangent = lax.optimization_barrier((rows, cotangent))
    rows = rows.reshape(row_count, width)
    grad_rows = swap(cotangent, "turb").reshape(row_count, width)
    *saved, layer_rows = forward(
        lists, rows, norm_gain, query_weight, key_weight, value_weight, out_weight, block_rows
    )
    layer_output = swap(layer_rows.reshape(inflow.shape), "turb")
    grads, sums = [], []
    for which in range(quads):
        *part, terms = backward(lists, grad_rows, out_weight, *saved, block_rows, which)
        grads += part
        sums.append(reduce_sums(terms))
    grad_rows, sum_gain = finish(
        rows, grad_rows, norm_gain, query_weight, key_weight, value_weight, grads
    )
    grad_inflow = swap(grad_rows.reshape(inflow.shape), "turb")
    sum_gain = jnp.sum(lax.all_gather(sum_gain.reshape(width), ("sample", "turb")), axis=0)
    projections = [
        jnp.concatenate([part[i * width : (i + 1) * width] for part in sums], axis=1)
        for i in range(3)
    ]
    sum_out = jnp.concatenate(
        [
            jnp.concatenate(
                [
                    part[3 * width + i * quad : 3 * width + (i + 1) * quad]
                    for i in range(quads)
                ],
                axis=1,
            )
            for part in sums
        ],
        axis=0,
    )
    return (layer_output, grad_inflow, *projections, sum_out, sum_gain)


def solution(mesh):
    placed = (
        P("sample", "turb", None),
        P("sample", "turb", None),
        P(),
        P(),
        P(),
        P(),
        P(),
        P(),
        P("sample"),
    )

    def plan(*args):
        sample_count = args[0].shape[0]
        if sample_count == mesh.shape["turb"]:
            return by_sample(*args)
        return on_device(*args)

    return jax.shard_map(
        plan,
        mesh=mesh,
        in_specs=placed,
        out_specs=(P("sample", "turb", None), P("sample", "turb", None), P(), P(), P(), P(), P()),
        check_vma=False,
    )
```

```python
import jax
import jax.numpy as jnp
from jax import lax
from jax.experimental import pallas as pl
from jax.experimental.pallas import tpu as pltpu
from jax.sharding import PartitionSpec as P

HEADS = 8
UPSTREAM = 3
SECTORS = 8
REPEAT = 1


epsilon = 1e-05


def normalize(row_block, norm_gain):
    widened = row_block.astype(jnp.float32)
    centred = widened - jnp.mean(widened, axis=-1, keepdims=True)
    inverse = lax.rsqrt(jnp.mean(centred * centred, axis=-1, keepdims=True) + epsilon)
    scaled = centred * inverse
    return (scaled, inverse, (scaled * norm_gain).astype(jnp.bfloat16))


def attend(pieces):
    queries, key_rows, value_rows, key_usable, grad_attended = pieces
    batch_count, query_count, model_width = queries.shape
    key_count = key_rows.shape[1]
    head_dim = model_width // HEADS
    score_scale = head_dim ** (-0.5)
    query_heads = queries.reshape(batch_count, query_count, HEADS, head_dim)
    key_heads = key_rows.reshape(batch_count, key_count, HEADS, head_dim)
    value_heads = value_rows.reshape(batch_count, key_count, HEADS, head_dim)
    grad_heads = grad_attended.reshape(batch_count, query_count, HEADS, head_dim)
    scores = (
        jnp.einsum("nqhd,nkhd->nhqk", query_heads, key_heads, preferred_element_type=jnp.float32)
        * score_scale
    )
    scores = jnp.where(key_usable[:, None, None, :], scores, -1e30)
    highest = jnp.max(scores, axis=-1, keepdims=True)
    weights = jnp.exp(scores - highest)
    probabilities = weights / jnp.sum(weights, axis=-1, keepdims=True)
    rounded = probabilities.astype(jnp.bfloat16)
    attended = jnp.einsum(
        "nhqk,nkhd->nqhd", rounded, value_heads, preferred_element_type=jnp.float32
    ).astype(jnp.bfloat16)
    grad_probs = jnp.einsum(
        "nqhd,nkhd->nhqk", grad_heads, value_heads, preferred_element_type=jnp.float32
    )
    centred = grad_probs - jnp.sum(probabilities * grad_probs, axis=-1, keepdims=True)
    grad_scores = (probabilities * centred * score_scale).astype(jnp.bfloat16)
    grad_queries = jnp.einsum(
        "nhqk,nkhd->nqhd", grad_scores, key_heads, preferred_element_type=jnp.float32
    ).astype(jnp.bfloat16)
    grad_keys = jnp.einsum(
        "nhqk,nqhd->nkhd", grad_scores, query_heads, preferred_element_type=jnp.float32
    )
    grad_values = jnp.einsum(
        "nhqk,nqhd->nkhd", rounded, grad_heads, preferred_element_type=jnp.float32
    )
    pair_terms = jnp.concatenate(
        [
            grad_keys.reshape(batch_count, key_count, model_width),
            grad_values.reshape(batch_count, key_count, model_width),
        ],
        axis=-1,
    )
    return (
        attended.reshape(batch_count, query_count, model_width),
        grad_queries.reshape(batch_count, query_count, model_width),
        pair_terms,
    )


def on_device(
    inflow,
    cotangent,
    norm_gain,
    query_weight,
    key_weight,
    value_weight,
    out_weight,
    adjacency,
    sectors,
):
    sample_count, block_rows, model_width = inflow.shape
    block_count = lax.axis_size("turb")
    own_block = lax.axis_index("turb")
    slot_count = REPEAT * ((SECTORS * UPSTREAM + block_count - 2) // (block_count - 1))
    flat_rows = sample_count * block_rows
    pair_width = 2 * model_width
    input_rows = inflow.reshape(flat_rows, model_width)
    grad_rows = cotangent.reshape(flat_rows, model_width)
    scaled, inverse, normed = normalize(input_rows, norm_gain)
    queries = jnp.dot(normed, query_weight, preferred_element_type=jnp.float32).astype(jnp.bfloat16)
    key_rows = jnp.dot(normed, key_weight, preferred_element_type=jnp.float32).astype(jnp.bfloat16)
    value_rows = jnp.dot(normed, value_weight, preferred_element_type=jnp.float32).astype(
        jnp.bfloat16
    )
    upstream = adjacency[sectors]
    needed = jnp.any(upstream == own_block, axis=2).astype(jnp.int32)
    earlier_need = jnp.cumsum(needed, axis=0) - needed
    slot_index = lax.broadcasted_iota(jnp.int32, (block_count, slot_count, sample_count), 1)
    chosen = (needed.T[:, None, :] == 1) & (earlier_need.T[:, None, :] == slot_index)
    selector = chosen.astype(jnp.bfloat16).reshape(block_count * slot_count, sample_count)
    own_lists = lax.dynamic_index_in_dim(upstream, own_block, axis=1, keepdims=False)
    usable = own_lists >= 0
    matches = jnp.any(own_lists[:, :, None, None] == own_lists[None, None, :, :], axis=3)
    sample_ids = lax.broadcasted_iota(jnp.int32, (sample_count, sample_count), 0)
    earlier = lax.broadcasted_iota(jnp.int32, (sample_count, sample_count), 1) < sample_ids
    position = jnp.sum((matches & earlier[:, None, :]).astype(jnp.int32), axis=2)
    flat_slot = own_lists * slot_count + position
    fetch_at = jnp.where(usable, flat_slot, 0)
    payload = jnp.concatenate([key_rows, value_rows], axis=1).reshape(
        sample_count, block_rows * pair_width
    )
    packed = jnp.dot(selector, payload, preferred_element_type=jnp.float32).astype(jnp.bfloat16)
    arrived = lax.all_to_all(
        packed.reshape(block_count, slot_count, block_rows, pair_width),
        "turb",
        split_axis=0,
        concat_axis=0,
        tiled=True,
    )
    fetched = arrived.reshape(block_count * slot_count, block_rows, pair_width)[fetch_at]
    upstream_keys = fetched[..., :model_width]
    upstream_values = fetched[..., model_width:]
    key_count = (1 + UPSTREAM) * block_rows
    key_all = jnp.concatenate(
        [key_rows.reshape(sample_count, 1, block_rows, model_width), upstream_keys], axis=1
    ).reshape(sample_count, key_count, model_width)
    value_all = jnp.concatenate(
        [value_rows.reshape(sample_count, 1, block_rows, model_width), upstream_values], axis=1
    ).reshape(sample_count, key_count, model_width)
    block_usable = jnp.concatenate([jnp.ones((sample_count, 1), dtype=jnp.bool_), usable], axis=1)
    key_usable = jnp.repeat(block_usable, block_rows, axis=1)
    grad_attended = jnp.dot(grad_rows, out_weight.T, preferred_element_type=jnp.float32).astype(
        jnp.bfloat16
    )
    group_size = min(sample_count, max(1, 512 // block_rows))
    while sample_count % group_size != 0:
        group_size = group_size - 1
    group_count = sample_count // group_size

    def grouped(tensor):
        return tensor.reshape((group_count, group_size) + tensor.shape[1:])

    attended, grad_queries, pair_terms = lax.map(
        attend,
        (
            grouped(queries.reshape(sample_count, block_rows, model_width)),
            grouped(key_all),
            grouped(value_all),
            grouped(key_usable),
            grouped(grad_attended.reshape(sample_count, block_rows, model_width)),
        ),
    )
    attended = attended.reshape(flat_rows, model_width)
    grad_queries = grad_queries.reshape(flat_rows, model_width)
    pair_terms = pair_terms.reshape(sample_count, 1 + UPSTREAM, block_rows, pair_width)
    layer_output = (
        (
            input_rows.astype(jnp.float32)
            + jnp.dot(attended, out_weight, preferred_element_type=jnp.float32)
        )
        .astype(jnp.bfloat16)
        .reshape(inflow.shape)
    )
    outgoing = (
        pair_terms[:, 1:]
        .astype(jnp.bfloat16)
        .reshape(sample_count * UPSTREAM, block_rows, pair_width)
    )
    target = jnp.where(usable, flat_slot, block_count * slot_count).reshape(-1)
    outbound = (
        jnp.zeros((block_count * slot_count, block_rows, pair_width), jnp.bfloat16)
        .at[target]
        .set(outgoing, mode="drop")
    )
    sum_out = jnp.dot(attended.T, grad_rows, preferred_element_type=jnp.float32)
    sum_query = jnp.dot(normed.T, grad_queries, preferred_element_type=jnp.float32)
    returned = lax.all_to_all(
        outbound.reshape(block_count, slot_count, block_rows, pair_width),
        "turb",
        split_axis=0,
        concat_axis=0,
        tiled=True,
    )
    remote = jnp.dot(
        selector.T,
        returned.reshape(block_count * slot_count, block_rows * pair_width),
        preferred_element_type=jnp.float32,
    )
    combined = (
        (pair_terms[:, 0].reshape(sample_count, block_rows * pair_width) + remote)
        .astype(jnp.bfloat16)
        .reshape(flat_rows, pair_width)
    )
    grad_keys = combined[:, :model_width]
    grad_values = combined[:, model_width:]
    sum_key = jnp.dot(normed.T, grad_keys, preferred_element_type=jnp.float32)
    sum_value = jnp.dot(normed.T, grad_values, preferred_element_type=jnp.float32)
    grad_normed = jnp.dot(grad_queries, query_weight.T, preferred_element_type=jnp.float32)
    grad_normed = grad_normed + jnp.dot(grad_keys, key_weight.T, preferred_element_type=jnp.float32)
    grad_normed = grad_normed + jnp.dot(
        grad_values, value_weight.T, preferred_element_type=jnp.float32
    )
    sum_gain = jnp.sum(grad_normed * scaled, axis=0)
    grad_scaled = grad_normed * norm_gain
    grad_input = inverse * (
        grad_scaled
        - jnp.mean(grad_scaled, axis=-1, keepdims=True)
        - scaled * jnp.mean(grad_scaled * scaled, axis=-1, keepdims=True)
    )
    grad_inflow = (
        (grad_rows.astype(jnp.float32) + grad_input).astype(jnp.bfloat16).reshape(inflow.shape)
    )
    sum_query, sum_key, sum_value, sum_out, sum_gain = lax.psum(
        (sum_query, sum_key, sum_value, sum_out, sum_gain), ("sample", "turb")
    )
    return (layer_output, grad_inflow, sum_query, sum_key, sum_value, sum_out, sum_gain)


PAIR = 2
QUAD = 4
LOG2_E = 1.4426950408889634
VMEM_LIMIT = 58 * 2**20


def contract(left, right, left_dim, right_dim):
    return lax.dot_general(
        left, right, (((left_dim,), (right_dim,)), ((), ())), preferred_element_type=jnp.float32
    )


def split_heads(rows, head_dim):
    lane = lax.broadcasted_iota(jnp.int32, rows.shape, 1)
    wide = rows.astype(jnp.float32)
    return jnp.concatenate(
        [jnp.where(lane < head_dim, wide, 0.0), jnp.where(lane >= head_dim, wide, 0.0)], axis=0
    ).astype(jnp.bfloat16)


def join_heads(wide, head_dim):
    block_rows = wide.shape[1] // PAIR
    first = lax.broadcasted_iota(jnp.int32, (wide.shape[0], block_rows), 0) < head_dim
    return jnp.where(first, wide[:, :block_rows], wide[:, block_rows:])


def for_each_block(lists_ref, block_count, block_rows, work):
    def step(block, carry):
        used = jnp.int32(0)
        for slot in range(UPSTREAM):
            used = used + (lists_ref[block * UPSTREAM + slot] >= 0).astype(jnp.int32)
        for count in range(UPSTREAM + 1):

            @pl.when(used == count)
            def _():
                sources = [block] + [
                    lists_ref[block * UPSTREAM + slot] for slot in range(count)
                ]
                work(block, [pl.multiple_of(s * block_rows, block_rows) for s in sources])

        return carry

    lax.fori_loop(0, block_count, step, 0)


def stacked(ref, starts, block_rows, lanes):
    return jnp.concatenate([ref[pl.ds(s, block_rows), lanes] for s in starts], axis=0)


def beside(ref, starts, block_rows, rows):
    return jnp.concatenate([ref[rows, pl.ds(s, block_rows)] for s in starts], axis=1)


def forward_kernel(block_rows, head_dim, lists_ref, x_ref, gain_ref, wq_ref, wk_ref, wv_ref,
                   wkt_ref, wvt_ref, wo_ref, normed_t_ref, q_ref, k_ref, v_ref, kt_ref, att_ref,
                   top_ref, inverse_ref, out_ref, normed_ref, vt_ref, rows_ref, sum_ref):
    row_count = x_ref.shape[0]
    quad = pl.program_id(0)
    pair = PAIR * head_dim
    exponent = head_dim ** (-0.5) * LOG2_E
    chunk = min(row_count, 256)

    @pl.when(quad == 0)
    def _():
        for start in range(0, row_count, chunk):
            part = slice(start, start + chunk)
            scaled, _, normed = normalize(x_ref[part, :], gain_ref[...])
            normed_ref[part, :] = normed
            normed_t_ref[:, part] = (scaled * gain_ref[...]).T.astype(jnp.bfloat16)

    normed = normed_ref[...]
    q_ref[...] = contract(normed, wq_ref[...], 1, 0).astype(jnp.bfloat16)
    k_ref[...] = contract(normed, wk_ref[...], 1, 0).astype(jnp.bfloat16)
    v_ref[...] = contract(normed, wv_ref[...], 1, 0).astype(jnp.bfloat16)
    kt_ref[...] = contract(wkt_ref[...], normed, 1, 1).astype(jnp.bfloat16)
    vt_ref[...] = contract(wvt_ref[...], normed, 1, 1).astype(jnp.bfloat16)

    def work(block, starts):
        own = pl.ds(starts[0], block_rows)
        lanes = [slice(p * pair, (p + 1) * pair) for p in range(QUAD // PAIR)]
        scores = [
            contract(
                stacked(k_ref, starts, block_rows, lane), split_heads(q_ref[own, lane], head_dim), 1, 1
            )
            for lane in lanes
        ]
        for p, lane in enumerate(lanes):
            highest = jnp.max(scores[p], axis=0, keepdims=True)
            weights = jnp.exp2((scores[p] - highest) * exponent)
            inverse = 1.0 / jnp.sum(weights, axis=0, keepdims=True)
            probs = (weights * inverse).astype(jnp.bfloat16)
            top_ref[0, pl.ds(block * (QUAD // PAIR) + p, 1), :] = highest
            inverse_ref[0, pl.ds(block * (QUAD // PAIR) + p, 1), :] = inverse
            joined = join_heads(
                jnp.dot(
                    beside(vt_ref, starts, block_rows, lane),
                    probs,
                    preferred_element_type=jnp.float32,
                ),
                head_dim,
            )
            att_ref[lane, own] = joined.astype(jnp.bfloat16)
            rows_ref[own, lane] = joined.T.astype(jnp.bfloat16)

    for_each_block(lists_ref, row_count // block_rows, block_rows, work)
    part = contract(rows_ref[...], wo_ref[...], 1, 0)

    @pl.when(quad == 0)
    def _():
        sum_ref[...] = x_ref[...].astype(jnp.float32) + part

    @pl.when(quad > 0)
    def _():
        sum_ref[...] += part

    @pl.when(quad == pl.num_programs(0) - 1)
    def _():
        out_ref[...] = sum_ref[...].astype(jnp.bfloat16)


def forward(lists, rows, norm_gain, query_weight, key_weight, value_weight, out_weight, block_rows):
    row_count, width = rows.shape
    head_dim = width // HEADS
    quad = QUAD * head_dim
    quads = width // quad
    stat_rows = row_count // block_rows * (QUAD // PAIR)
    fixed = lambda *shape: pl.BlockSpec(shape, lambda p, lists: (0,) * len(shape))
    across = lambda size: pl.BlockSpec((size, quad), lambda p, lists: (0, p))
    down = lambda size: pl.BlockSpec((quad, size), lambda p, lists: (p, 0))
    stat = pl.BlockSpec((1, stat_rows, PAIR * block_rows), lambda p, lists: (p, 0, 0))
    flat = jax.ShapeDtypeStruct((row_count, width), jnp.bfloat16)
    turned = jax.ShapeDtypeStruct((width, row_count), jnp.bfloat16)
    stats = jax.ShapeDtypeStruct((quads, stat_rows, PAIR * block_rows), jnp.float32)
    return pl.pallas_call(
        lambda *refs: forward_kernel(block_rows, head_dim, *refs),
        grid_spec=pltpu.PrefetchScalarGridSpec(
            num_scalar_prefetch=1,
            grid=(quads,),
            in_specs=[fixed(row_count, width), fixed(1, width)]
            + [across(width)] * 3
            + [down(width)] * 3,
            out_specs=[fixed(width, row_count)]
            + [across(row_count)] * 3
            + [down(row_count)] * 2
            + [stat] * 2
            + [fixed(row_count, width)],
            scratch_shapes=[
                pltpu.VMEM((row_count, width), jnp.bfloat16),
                pltpu.VMEM((quad, row_count), jnp.bfloat16),
                pltpu.VMEM((row_count, quad), jnp.bfloat16),
                pltpu.VMEM((row_count, width), jnp.float32),
            ],
        ),
        out_shape=[turned, flat, flat, flat, turned, turned, stats, stats, flat],
        compiler_params=pltpu.CompilerParams(vmem_limit_bytes=VMEM_LIMIT),
        cost_estimate=pl.CostEstimate(
            flops=12 * row_count * width * width + 32 * row_count * block_rows * width,
            bytes_accessed=20 * row_count * width,
            transcendentals=row_count * 4 * block_rows * HEADS,
        ),
        name="forward",
    )(lists, rows, norm_gain.reshape(1, width), query_weight, key_weight, value_weight,
      key_weight.T, value_weight.T, out_weight)


def backward_kernel(block_rows, head_dim, which, lists_ref, cot_ref, wo_ref, normed_t_ref, q_ref,
                    k_ref, v_ref, kt_ref, att_ref, top_ref, inverse_ref, gq_ref, gk_ref, gv_ref,
                    keep_ref, send_ref, ga_ref, gk_acc, gv_acc):
    row_count, width = cot_ref.shape
    block_count = row_count // block_rows
    pair = PAIR * head_dim
    quad = QUAD * head_dim
    scale = head_dim ** (-0.5)
    ga_ref[...] = contract(cot_ref[...], wo_ref[...], 1, 1).astype(jnp.bfloat16)
    gk_acc[...] = jnp.zeros_like(gk_acc)
    gv_acc[...] = jnp.zeros_like(gv_acc)

    def work(block, starts):
        own = pl.ds(starts[0], block_rows)
        lanes = [slice(p * pair, (p + 1) * pair) for p in range(QUAD // PAIR)]
        queries = [split_heads(q_ref[own, lane], head_dim) for lane in lanes]
        grads = [split_heads(ga_ref[own, lane], head_dim) for lane in lanes]
        scores = [
            contract(stacked(k_ref, starts, block_rows, lane), queries[p], 1, 1)
            for p, lane in enumerate(lanes)
        ]
        grad_probs = [
            contract(stacked(v_ref, starts, block_rows, lane), grads[p] * scale, 1, 1)
            for p, lane in enumerate(lanes)
        ]
        for p, lane in enumerate(lanes):
            stat = pl.ds(block * (QUAD // PAIR) + p, 1)
            probs = jnp.exp2((scores[p] - top_ref[0, stat, :]) * (scale * LOG2_E))
            probs = probs * inverse_ref[0, stat, :]
            total = jnp.sum(probs * grad_probs[p], axis=0, keepdims=True)
            grad_scores = (probs * (grad_probs[p] - total)).astype(jnp.bfloat16)
            probs_b = probs.astype(jnp.bfloat16)
            grad_values = jnp.dot(probs_b, grads[p], preferred_element_type=jnp.float32)
            grad_keys = jnp.dot(grad_scores, queries[p], preferred_element_type=jnp.float32)
            joined = join_heads(
                jnp.dot(
                    beside(kt_ref, starts, block_rows, lane),
                    grad_scores,
                    preferred_element_type=jnp.float32,
                ),
                head_dim,
            )
            gq_ref[own, lane] = joined.T.astype(jnp.bfloat16)
            for slot, start in enumerate(starts):
                rows = pl.ds(start, block_rows)
                part = slice(slot * block_rows, (slot + 1) * block_rows)
                for acc, terms in ((gk_acc, grad_keys), (gv_acc, grad_values)):
                    term = terms[part]
                    if slot > 0:
                        term = term.astype(jnp.bfloat16).astype(jnp.float32)
                    acc[rows, lane] += term

    for_each_block(lists_ref, block_count, block_rows, work)
    gk_ref[...] = gk_acc[...].astype(jnp.bfloat16)
    gv_ref[...] = gv_acc[...].astype(jnp.bfloat16)
    products = [(normed_t_ref, ref, slice(None)) for ref in (gq_ref, gk_ref, gv_ref)]
    products.append((att_ref, cot_ref, slice(which * quad, (which + 1) * quad)))
    share = keep_ref.shape[1]
    turbs = keep_ref.shape[0] // 2
    offset = block_count * UPSTREAM
    own_sample, own_turb = lists_ref[offset], lists_ref[offset + 1]
    piece = 0
    for left, right, lanes in products:
        terms = contract(left[...], right[:, lanes], 1, 0)
        for start in range(0, width, share):
            apart = (piece // turbs) ^ own_sample
            place = (apart // 2) * turbs + ((piece % turbs) ^ own_turb)
            term = terms[start : start + share]

            @pl.when(apart % 2 == 0)
            def _():
                keep_ref[place] = term

            @pl.when(apart % 2 == 1)
            def _():
                send_ref[place] = term

            piece += 1


def backward(lists, cotangent, out_weight, normed_t, queries, keys, values, keys_t, attended_t,
             tops, inverses, block_rows, which, sample_axis):
    row_count, width = cotangent.shape
    block_count = row_count // block_rows
    head_dim = width // HEADS
    quad = QUAD * head_dim
    fixed = lambda *shape: pl.BlockSpec(shape, lambda i, lists: (0,) * len(shape))
    across = pl.BlockSpec((row_count, quad), lambda i, lists: (0, which))
    down = lambda size: pl.BlockSpec((quad, size), lambda i, lists: (which, 0))
    stat = pl.BlockSpec((1,) + tops.shape[1:], lambda i, lists: (which, 0, 0))
    part = jax.ShapeDtypeStruct((row_count, quad), jnp.bfloat16)
    share = 4 * width // (sample_axis * block_count)
    pieces = (sample_axis * block_count // 2, share, quad)
    return pl.pallas_call(
        lambda *refs: backward_kernel(block_rows, head_dim, which, *refs),
        grid_spec=pltpu.PrefetchScalarGridSpec(
            num_scalar_prefetch=1,
            grid=(1,),
            in_specs=[fixed(row_count, width), down(width), fixed(width, row_count)]
            + [across] * 3
            + [down(row_count), fixed(width, row_count)]
            + [stat] * 2,
            out_specs=[fixed(row_count, quad)] * 3 + [fixed(*pieces)] * 2,
            scratch_shapes=[
                pltpu.VMEM((row_count, quad), jnp.bfloat16),
                pltpu.VMEM((row_count, quad), jnp.float32),
                pltpu.VMEM((row_count, quad), jnp.float32),
            ],
        ),
        out_shape=[part] * 3 + [jax.ShapeDtypeStruct(pieces, jnp.float32)] * 2,
        compiler_params=pltpu.CompilerParams(vmem_limit_bytes=VMEM_LIMIT),
        cost_estimate=pl.CostEstimate(
            flops=10 * row_count * width * quad + 80 * row_count * block_rows * quad,
            bytes_accessed=14 * row_count * width,
            transcendentals=row_count * 4 * block_rows * QUAD,
        ),
        name="backward",
    )(lists, cotangent, out_weight, normed_t, queries, keys, values, keys_t, attended_t, tops,
      inverses)


def finish_kernel(quads, x_ref, cot_ref, gain_ref, wq_ref, wk_ref, wv_ref, *refs):
    grad_refs, (out_ref, sum_ref) = refs[:-2], refs[-2:]
    scaled, inverse, _ = normalize(x_ref[...], gain_ref[...])
    quad = grad_refs[0].shape[1]
    grad_normed = jnp.zeros(x_ref.shape, jnp.float32)
    for i in range(quads):
        lanes = slice(i * quad, (i + 1) * quad)
        for j, weight_ref in enumerate((wq_ref, wk_ref, wv_ref)):
            grad_normed += contract(grad_refs[3 * i + j][...], weight_ref[:, lanes], 1, 1)

    @pl.when(pl.program_id(0) == 0)
    def _():
        sum_ref[...] = jnp.zeros_like(sum_ref)

    sum_ref[...] += jnp.sum(grad_normed * scaled, axis=0, keepdims=True)
    grad_scaled = grad_normed * gain_ref[...]
    grad_input = inverse * (
        grad_scaled
        - jnp.mean(grad_scaled, axis=-1, keepdims=True)
        - scaled * jnp.mean(grad_scaled * scaled, axis=-1, keepdims=True)
    )
    out_ref[...] = (cot_ref[...].astype(jnp.float32) + grad_input).astype(jnp.bfloat16)


def finish(rows, cotangent, norm_gain, query_weight, key_weight, value_weight, grads):
    row_count, width = rows.shape
    quad = grads[0].shape[1]
    step = min(row_count, 256)
    fixed = lambda *shape: pl.BlockSpec(shape, lambda i: (0,) * len(shape))
    by_row = lambda size: pl.BlockSpec((step, size), lambda i: (i, 0))
    return pl.pallas_call(
        lambda *refs: finish_kernel(width // quad, *refs),
        grid=(row_count // step,),
        in_specs=[by_row(width)] * 2
        + [fixed(1, width)]
        + [fixed(width, width)] * 3
        + [by_row(quad)] * len(grads),
        out_specs=[by_row(width), fixed(1, width)],
        out_shape=[
            jax.ShapeDtypeStruct((row_count, width), jnp.bfloat16),
            jax.ShapeDtypeStruct((1, width), jnp.float32),
        ],
        compiler_params=pltpu.CompilerParams(vmem_limit_bytes=VMEM_LIMIT),
        cost_estimate=pl.CostEstimate(
            flops=6 * row_count * width * width,
            bytes_accessed=16 * row_count * width,
            transcendentals=0,
        ),
        name="finish",
    )(rows, cotangent, norm_gain.reshape(1, width), query_weight, key_weight, value_weight, *grads)


def swap(tensor, axis):
    return lax.all_to_all(tensor, axis, split_axis=0, concat_axis=0, tiled=True)


def across(tensor, axis, distance):
    size = lax.axis_size(axis)
    return lax.ppermute(tensor, axis, [(i, i ^ distance) for i in range(size)])


def reduce_sums(keep, send):
    turbs = lax.axis_size("turb")
    sums = keep + across(send, "sample", 1)
    arrived = across(sums[turbs:].astype(jnp.bfloat16), "sample", 2)
    sums = sums[:turbs] + arrived.astype(jnp.float32)
    total = sums[0]
    for distance in range(1, turbs):
        total = total + across(sums[distance].astype(jnp.bfloat16), "turb", distance).astype(
            jnp.float32
        )
    own = total.astype(jnp.bfloat16)
    row = jnp.stack([own] + [across(own, "turb", distance) for distance in range(1, turbs)])
    both = [row, across(row, "sample", 2)]
    return both + [across(part, "sample", 1) for part in both]


def place_kernel(place_ref, *refs):
    (*pieces, query_ref, key_ref, value_ref, out_ref, all_ref) = refs
    own_sample, own_turb = place_ref[0], place_ref[1]
    groups = len(pieces) // 4
    for i, ref in enumerate(pieces):
        which, part = divmod(i, 4)
        turbs, share, quad = ref.shape
        sample = own_sample ^ ((part % 2) * 2 + part // 2)
        for j in range(turbs):
            start = pl.multiple_of((sample * turbs + (own_turb ^ j)) * share, share)
            all_ref[pl.ds(start, share), which * quad : (which + 1) * quad] = ref[j].astype(
                jnp.float32
            )
    width = query_ref.shape[0]
    for i, ref in enumerate((query_ref, key_ref, value_ref, out_ref)):
        ref[...] = all_ref[i * width : (i + 1) * width, :]


def place_sums(place, pieces, width):
    whole = jax.ShapeDtypeStruct((width, width), jnp.float32)
    return pl.pallas_call(
        place_kernel,
        in_specs=[pl.BlockSpec(memory_space=pltpu.SMEM)]
        + [pl.BlockSpec(memory_space=pltpu.VMEM)] * len(pieces),
        out_specs=[pl.BlockSpec(memory_space=pltpu.VMEM)] * 4,
        out_shape=[whole] * 4,
        scratch_shapes=[pltpu.VMEM((4 * width, width), jnp.float32)],
        compiler_params=pltpu.CompilerParams(vmem_limit_bytes=VMEM_LIMIT),
        cost_estimate=pl.CostEstimate(
            flops=0, bytes_accessed=24 * width * width, transcendentals=0
        ),
        name="place",
    )(place, *pieces)


def by_sample(
    inflow,
    cotangent,
    norm_gain,
    query_weight,
    key_weight,
    value_weight,
    out_weight,
    adjacency,
    sectors,
):
    sample_count, block_rows, width = inflow.shape
    sample_axis = lax.axis_size("sample")
    row_count = lax.axis_size("turb") * block_rows
    own_turb = lax.axis_index("turb")
    place = jnp.stack([lax.axis_index("sample"), own_turb]).astype(jnp.int32)
    sector = lax.dynamic_index_in_dim(sectors, own_turb, keepdims=False)
    lists = lax.dynamic_index_in_dim(adjacency, sector, keepdims=False).reshape(-1)
    lists = jnp.concatenate([lists, place])

    rows = swap(inflow, "turb")
    rows, cotangent = lax.optimization_barrier((rows, cotangent))
    rows = rows.reshape(row_count, width)
    grad_rows = swap(cotangent, "turb").reshape(row_count, width)
    *saved, layer_rows = forward(
        lists, rows, norm_gain, query_weight, key_weight, value_weight, out_weight, block_rows
    )
    layer_output = swap(layer_rows.reshape(inflow.shape), "turb")
    grads, pieces = [], []
    for which in range(HEADS // QUAD):
        *part, keep, send = backward(
            lists, grad_rows, out_weight, *saved, block_rows, which, sample_axis
        )
        grads += part
        pieces += reduce_sums(keep, send)
    grad_rows, sum_gain = finish(
        rows, grad_rows, norm_gain, query_weight, key_weight, value_weight, grads
    )
    grad_inflow = swap(grad_rows.reshape(inflow.shape), "turb")
    for axis in ("sample", "turb"):
        distance = 1
        while distance < lax.axis_size(axis):
            sum_gain = sum_gain + across(sum_gain, axis, distance)
            distance *= 2
    sums = place_sums(place, pieces, width)
    return (layer_output, grad_inflow, *sums, sum_gain.reshape(width))


def solution(mesh):
    placed = (
        P("sample", "turb", None),
        P("sample", "turb", None),
        P(),
        P(),
        P(),
        P(),
        P(),
        P(),
        P("sample"),
    )

    def plan(*args):
        sample_count = args[0].shape[0]
        if sample_count == mesh.shape["turb"] and mesh.shape["sample"] == 4:
            return by_sample(*args)
        return on_device(*args)

    return jax.shard_map(
        plan,
        mesh=mesh,
        in_specs=placed,
        out_specs=(P("sample", "turb", None), P("sample", "turb", None), P(), P(), P(), P(), P()),
        check_vma=False,
    )
```

```python
import jax
import jax.numpy as jnp
from jax import lax
from jax.experimental import pallas as pl
from jax.experimental.pallas import tpu as pltpu
from jax.sharding import PartitionSpec as P

HEADS = 8
UPSTREAM = 3
SECTORS = 8
REPEAT = 1


epsilon = 1e-05


def normalize(row_block, norm_gain):
    widened = row_block.astype(jnp.float32)
    centred = widened - jnp.mean(widened, axis=-1, keepdims=True)
    inverse = lax.rsqrt(jnp.mean(centred * centred, axis=-1, keepdims=True) + epsilon)
    scaled = centred * inverse
    return (scaled, inverse, (scaled * norm_gain).astype(jnp.bfloat16))


def attend(pieces):
    queries, key_rows, value_rows, key_usable, grad_attended = pieces
    batch_count, query_count, model_width = queries.shape
    key_count = key_rows.shape[1]
    head_dim = model_width // HEADS
    score_scale = head_dim ** (-0.5)
    query_heads = queries.reshape(batch_count, query_count, HEADS, head_dim)
    key_heads = key_rows.reshape(batch_count, key_count, HEADS, head_dim)
    value_heads = value_rows.reshape(batch_count, key_count, HEADS, head_dim)
    grad_heads = grad_attended.reshape(batch_count, query_count, HEADS, head_dim)
    scores = (
        jnp.einsum("nqhd,nkhd->nhqk", query_heads, key_heads, preferred_element_type=jnp.float32)
        * score_scale
    )
    scores = jnp.where(key_usable[:, None, None, :], scores, -1e30)
    highest = jnp.max(scores, axis=-1, keepdims=True)
    weights = jnp.exp(scores - highest)
    probabilities = weights / jnp.sum(weights, axis=-1, keepdims=True)
    rounded = probabilities.astype(jnp.bfloat16)
    attended = jnp.einsum(
        "nhqk,nkhd->nqhd", rounded, value_heads, preferred_element_type=jnp.float32
    ).astype(jnp.bfloat16)
    grad_probs = jnp.einsum(
        "nqhd,nkhd->nhqk", grad_heads, value_heads, preferred_element_type=jnp.float32
    )
    centred = grad_probs - jnp.sum(probabilities * grad_probs, axis=-1, keepdims=True)
    grad_scores = (probabilities * centred * score_scale).astype(jnp.bfloat16)
    grad_queries = jnp.einsum(
        "nhqk,nkhd->nqhd", grad_scores, key_heads, preferred_element_type=jnp.float32
    ).astype(jnp.bfloat16)
    grad_keys = jnp.einsum(
        "nhqk,nqhd->nkhd", grad_scores, query_heads, preferred_element_type=jnp.float32
    )
    grad_values = jnp.einsum(
        "nhqk,nqhd->nkhd", rounded, grad_heads, preferred_element_type=jnp.float32
    )
    pair_terms = jnp.concatenate(
        [
            grad_keys.reshape(batch_count, key_count, model_width),
            grad_values.reshape(batch_count, key_count, model_width),
        ],
        axis=-1,
    )
    return (
        attended.reshape(batch_count, query_count, model_width),
        grad_queries.reshape(batch_count, query_count, model_width),
        pair_terms,
    )


def on_device(
    inflow,
    cotangent,
    norm_gain,
    query_weight,
    key_weight,
    value_weight,
    out_weight,
    adjacency,
    sectors,
):
    sample_count, block_rows, model_width = inflow.shape
    block_count = lax.axis_size("turb")
    own_block = lax.axis_index("turb")
    slot_count = REPEAT * ((SECTORS * UPSTREAM + block_count - 2) // (block_count - 1))
    flat_rows = sample_count * block_rows
    pair_width = 2 * model_width
    input_rows = inflow.reshape(flat_rows, model_width)
    grad_rows = cotangent.reshape(flat_rows, model_width)
    scaled, inverse, normed = normalize(input_rows, norm_gain)
    queries = jnp.dot(normed, query_weight, preferred_element_type=jnp.float32).astype(jnp.bfloat16)
    key_rows = jnp.dot(normed, key_weight, preferred_element_type=jnp.float32).astype(jnp.bfloat16)
    value_rows = jnp.dot(normed, value_weight, preferred_element_type=jnp.float32).astype(
        jnp.bfloat16
    )
    upstream = adjacency[sectors]
    needed = jnp.any(upstream == own_block, axis=2).astype(jnp.int32)
    earlier_need = jnp.cumsum(needed, axis=0) - needed
    slot_index = lax.broadcasted_iota(jnp.int32, (block_count, slot_count, sample_count), 1)
    chosen = (needed.T[:, None, :] == 1) & (earlier_need.T[:, None, :] == slot_index)
    selector = chosen.astype(jnp.bfloat16).reshape(block_count * slot_count, sample_count)
    own_lists = lax.dynamic_index_in_dim(upstream, own_block, axis=1, keepdims=False)
    usable = own_lists >= 0
    matches = jnp.any(own_lists[:, :, None, None] == own_lists[None, None, :, :], axis=3)
    sample_ids = lax.broadcasted_iota(jnp.int32, (sample_count, sample_count), 0)
    earlier = lax.broadcasted_iota(jnp.int32, (sample_count, sample_count), 1) < sample_ids
    position = jnp.sum((matches & earlier[:, None, :]).astype(jnp.int32), axis=2)
    flat_slot = own_lists * slot_count + position
    fetch_at = jnp.where(usable, flat_slot, 0)
    payload = jnp.concatenate([key_rows, value_rows], axis=1).reshape(
        sample_count, block_rows * pair_width
    )
    packed = jnp.dot(selector, payload, preferred_element_type=jnp.float32).astype(jnp.bfloat16)
    arrived = lax.all_to_all(
        packed.reshape(block_count, slot_count, block_rows, pair_width),
        "turb",
        split_axis=0,
        concat_axis=0,
        tiled=True,
    )
    fetched = arrived.reshape(block_count * slot_count, block_rows, pair_width)[fetch_at]
    upstream_keys = fetched[..., :model_width]
    upstream_values = fetched[..., model_width:]
    key_count = (1 + UPSTREAM) * block_rows
    key_all = jnp.concatenate(
        [key_rows.reshape(sample_count, 1, block_rows, model_width), upstream_keys], axis=1
    ).reshape(sample_count, key_count, model_width)
    value_all = jnp.concatenate(
        [value_rows.reshape(sample_count, 1, block_rows, model_width), upstream_values], axis=1
    ).reshape(sample_count, key_count, model_width)
    block_usable = jnp.concatenate([jnp.ones((sample_count, 1), dtype=jnp.bool_), usable], axis=1)
    key_usable = jnp.repeat(block_usable, block_rows, axis=1)
    grad_attended = jnp.dot(grad_rows, out_weight.T, preferred_element_type=jnp.float32).astype(
        jnp.bfloat16
    )
    group_size = min(sample_count, max(1, 512 // block_rows))
    while sample_count % group_size != 0:
        group_size = group_size - 1
    group_count = sample_count // group_size

    def grouped(tensor):
        return tensor.reshape((group_count, group_size) + tensor.shape[1:])

    attended, grad_queries, pair_terms = lax.map(
        attend,
        (
            grouped(queries.reshape(sample_count, block_rows, model_width)),
            grouped(key_all),
            grouped(value_all),
            grouped(key_usable),
            grouped(grad_attended.reshape(sample_count, block_rows, model_width)),
        ),
    )
    attended = attended.reshape(flat_rows, model_width)
    grad_queries = grad_queries.reshape(flat_rows, model_width)
    pair_terms = pair_terms.reshape(sample_count, 1 + UPSTREAM, block_rows, pair_width)
    layer_output = (
        (
            input_rows.astype(jnp.float32)
            + jnp.dot(attended, out_weight, preferred_element_type=jnp.float32)
        )
        .astype(jnp.bfloat16)
        .reshape(inflow.shape)
    )
    outgoing = (
        pair_terms[:, 1:]
        .astype(jnp.bfloat16)
        .reshape(sample_count * UPSTREAM, block_rows, pair_width)
    )
    target = jnp.where(usable, flat_slot, block_count * slot_count).reshape(-1)
    outbound = (
        jnp.zeros((block_count * slot_count, block_rows, pair_width), jnp.bfloat16)
        .at[target]
        .set(outgoing, mode="drop")
    )
    sum_out = jnp.dot(attended.T, grad_rows, preferred_element_type=jnp.float32)
    sum_query = jnp.dot(normed.T, grad_queries, preferred_element_type=jnp.float32)
    returned = lax.all_to_all(
        outbound.reshape(block_count, slot_count, block_rows, pair_width),
        "turb",
        split_axis=0,
        concat_axis=0,
        tiled=True,
    )
    remote = jnp.dot(
        selector.T,
        returned.reshape(block_count * slot_count, block_rows * pair_width),
        preferred_element_type=jnp.float32,
    )
    combined = (
        (pair_terms[:, 0].reshape(sample_count, block_rows * pair_width) + remote)
        .astype(jnp.bfloat16)
        .reshape(flat_rows, pair_width)
    )
    grad_keys = combined[:, :model_width]
    grad_values = combined[:, model_width:]
    sum_key = jnp.dot(normed.T, grad_keys, preferred_element_type=jnp.float32)
    sum_value = jnp.dot(normed.T, grad_values, preferred_element_type=jnp.float32)
    grad_normed = jnp.dot(grad_queries, query_weight.T, preferred_element_type=jnp.float32)
    grad_normed = grad_normed + jnp.dot(grad_keys, key_weight.T, preferred_element_type=jnp.float32)
    grad_normed = grad_normed + jnp.dot(
        grad_values, value_weight.T, preferred_element_type=jnp.float32
    )
    sum_gain = jnp.sum(grad_normed * scaled, axis=0)
    grad_scaled = grad_normed * norm_gain
    grad_input = inverse * (
        grad_scaled
        - jnp.mean(grad_scaled, axis=-1, keepdims=True)
        - scaled * jnp.mean(grad_scaled * scaled, axis=-1, keepdims=True)
    )
    grad_inflow = (
        (grad_rows.astype(jnp.float32) + grad_input).astype(jnp.bfloat16).reshape(inflow.shape)
    )
    sum_query, sum_key, sum_value, sum_out, sum_gain = lax.psum(
        (sum_query, sum_key, sum_value, sum_out, sum_gain), ("sample", "turb")
    )
    return (layer_output, grad_inflow, sum_query, sum_key, sum_value, sum_out, sum_gain)


PAIR = 2
QUAD = 4
LOG2_E = 1.4426950408889634
VMEM_LIMIT = 58 * 2**20
GAIN_ROWS = 8


def contract(left, right, left_dim, right_dim):
    return lax.dot_general(
        left, right, (((left_dim,), (right_dim,)), ((), ())), preferred_element_type=jnp.float32
    )


def split_heads(rows, head_dim):
    lane = lax.broadcasted_iota(jnp.int32, rows.shape, 1)
    wide = rows.astype(jnp.float32)
    return jnp.concatenate(
        [jnp.where(lane < head_dim, wide, 0.0), jnp.where(lane >= head_dim, wide, 0.0)], axis=0
    ).astype(jnp.bfloat16)


def join_heads(wide, head_dim):
    block_rows = wide.shape[1] // PAIR
    first = lax.broadcasted_iota(jnp.int32, (wide.shape[0], block_rows), 0) < head_dim
    return jnp.where(first, wide[:, :block_rows], wide[:, block_rows:])


def for_each_block(sectors_ref, lists_ref, block_count, block_rows, work):
    sector = sectors_ref[lax.axis_index("turb")]

    def step(block, carry):
        used = jnp.int32(0)
        for slot in range(UPSTREAM):
            used = used + (lists_ref[sector, block, slot] >= 0).astype(jnp.int32)
        for count in range(UPSTREAM + 1):

            @pl.when(used == count)
            def _():
                sources = [block] + [
                    lists_ref[sector, block, slot] for slot in range(count)
                ]
                work(block, [pl.multiple_of(s * block_rows, block_rows) for s in sources])

        return carry

    lax.fori_loop(0, block_count, step, 0)


def stacked(ref, starts, block_rows, lanes):
    return jnp.concatenate([ref[pl.ds(s, block_rows), lanes] for s in starts], axis=0)


def beside(ref, starts, block_rows, rows):
    return jnp.concatenate([ref[rows, pl.ds(s, block_rows)] for s in starts], axis=1)


def forward_kernel(block_rows, head_dim, sectors_ref, lists_ref, x_ref, gain_ref, wq_ref, wk_ref,
                   wv_ref, wo_ref, normed_t_ref, q_ref, k_ref, v_ref, kt_ref, att_ref,
                   top_ref, inverse_ref, out_ref, normed_ref, vt_ref, rows_ref, sum_ref):
    row_count = x_ref.shape[0]
    quad = pl.program_id(0)
    pair = PAIR * head_dim
    exponent = head_dim ** (-0.5) * LOG2_E
    chunk = min(row_count, 256)

    @pl.when(quad == 0)
    def _():
        for start in range(0, row_count, chunk):
            part = slice(start, start + chunk)
            scaled, _, normed = normalize(x_ref[part, :], gain_ref[...])
            normed_ref[part, :] = normed
            normed_t_ref[:, part] = (scaled * gain_ref[...]).T.astype(jnp.bfloat16)

    normed = normed_ref[...]
    q_ref[...] = contract(normed, wq_ref[...], 1, 0).astype(jnp.bfloat16)
    k_ref[...] = contract(normed, wk_ref[...], 1, 0).astype(jnp.bfloat16)
    v_ref[...] = contract(normed, wv_ref[...], 1, 0).astype(jnp.bfloat16)
    kt_ref[...] = contract(wk_ref[...], normed, 0, 1).astype(jnp.bfloat16)
    vt_ref[...] = contract(wv_ref[...], normed, 0, 1).astype(jnp.bfloat16)

    def work(block, starts):
        own = pl.ds(starts[0], block_rows)
        lanes = [slice(p * pair, (p + 1) * pair) for p in range(QUAD // PAIR)]
        scores = [
            contract(
                stacked(k_ref, starts, block_rows, lane), split_heads(q_ref[own, lane], head_dim), 1, 1
            )
            for lane in lanes
        ]
        for p, lane in enumerate(lanes):
            highest = jnp.max(scores[p], axis=0, keepdims=True)
            weights = jnp.exp2((scores[p] - highest) * exponent)
            inverse = 1.0 / jnp.sum(weights, axis=0, keepdims=True)
            probs = (weights * inverse).astype(jnp.bfloat16)
            top_ref[0, pl.ds(block * (QUAD // PAIR) + p, 1), :] = highest
            inverse_ref[0, pl.ds(block * (QUAD // PAIR) + p, 1), :] = inverse
            joined = join_heads(
                jnp.dot(
                    beside(vt_ref, starts, block_rows, lane),
                    probs,
                    preferred_element_type=jnp.float32,
                ),
                head_dim,
            )
            att_ref[lane, own] = joined.astype(jnp.bfloat16)
            rows_ref[own, lane] = joined.T.astype(jnp.bfloat16)

    for_each_block(sectors_ref, lists_ref, row_count // block_rows, block_rows, work)
    part = contract(rows_ref[...], wo_ref[...], 1, 0)

    @pl.when(quad == 0)
    def _():
        sum_ref[...] = x_ref[...].astype(jnp.float32) + part

    @pl.when(quad > 0)
    def _():
        sum_ref[...] += part

    @pl.when(quad == pl.num_programs(0) - 1)
    def _():
        out_ref[...] = sum_ref[...].astype(jnp.bfloat16)


def forward(sectors, adjacency, rows, norm_gain, query_weight, key_weight, value_weight, out_weight, block_rows):
    row_count, width = rows.shape
    head_dim = width // HEADS
    quad = QUAD * head_dim
    quads = width // quad
    stat_rows = row_count // block_rows * (QUAD // PAIR)
    fixed = lambda *shape: pl.BlockSpec(shape, lambda p, *lists: (0,) * len(shape))
    across = lambda size: pl.BlockSpec((size, quad), lambda p, *lists: (0, p))
    down = lambda size: pl.BlockSpec((quad, size), lambda p, *lists: (p, 0))
    stat = pl.BlockSpec((1, stat_rows, PAIR * block_rows), lambda p, *lists: (p, 0, 0))
    flat = jax.ShapeDtypeStruct((row_count, width), jnp.bfloat16)
    turned = jax.ShapeDtypeStruct((width, row_count), jnp.bfloat16)
    stats = jax.ShapeDtypeStruct((quads, stat_rows, PAIR * block_rows), jnp.float32)
    return pl.pallas_call(
        lambda *refs: forward_kernel(block_rows, head_dim, *refs),
        grid_spec=pltpu.PrefetchScalarGridSpec(
            num_scalar_prefetch=2,
            grid=(quads,),
            in_specs=[fixed(row_count, width), fixed(1, width)]
            + [across(width)] * 3
            + [down(width)],
            out_specs=[fixed(width, row_count)]
            + [across(row_count)] * 3
            + [down(row_count)] * 2
            + [stat] * 2
            + [fixed(row_count, width)],
            scratch_shapes=[
                pltpu.VMEM((row_count, width), jnp.bfloat16),
                pltpu.VMEM((quad, row_count), jnp.bfloat16),
                pltpu.VMEM((row_count, quad), jnp.bfloat16),
                pltpu.VMEM((row_count, width), jnp.float32),
            ],
        ),
        out_shape=[turned, flat, flat, flat, turned, turned, stats, stats, flat],
        compiler_params=pltpu.CompilerParams(vmem_limit_bytes=VMEM_LIMIT),
        cost_estimate=pl.CostEstimate(
            flops=12 * row_count * width * width + 32 * row_count * block_rows * width,
            bytes_accessed=20 * row_count * width,
            transcendentals=row_count * 4 * block_rows * HEADS,
        ),
        name="forward",
    )(sectors, adjacency, rows, norm_gain.reshape(1, width), query_weight, key_weight, value_weight,
      out_weight)


def backward_kernel(block_rows, head_dim, which, last, sectors_ref, lists_ref, cot_ref, wo_ref,
                    normed_t_ref, q_ref, k_ref, v_ref, kt_ref, att_ref, top_ref, inverse_ref, *refs):
    if last:
        x_ref, gain_ref, wq_ref, wk_ref, wv_ref, *refs = refs
        before, refs = refs[: 3 * which], refs[3 * which :]
        grad_ref, keep_ref, send_ref, gq_ref, gk_ref, gv_ref, ga_ref, gk_acc, gv_acc, sum_ref = refs
    else:
        gq_ref, gk_ref, gv_ref, whole_ref, ga_ref, gk_acc, gv_acc = refs
    row_count, width = cot_ref.shape
    block_count = row_count // block_rows
    pair = PAIR * head_dim
    quad = QUAD * head_dim
    scale = head_dim ** (-0.5)
    ga_ref[...] = contract(cot_ref[...], wo_ref[...], 1, 1).astype(jnp.bfloat16)
    gk_acc[...] = jnp.zeros_like(gk_acc)
    gv_acc[...] = jnp.zeros_like(gv_acc)

    def work(block, starts):
        own = pl.ds(starts[0], block_rows)
        lanes = [slice(p * pair, (p + 1) * pair) for p in range(QUAD // PAIR)]
        queries = [split_heads(q_ref[own, lane], head_dim) for lane in lanes]
        grads = [split_heads(ga_ref[own, lane], head_dim) for lane in lanes]
        scores = [
            contract(stacked(k_ref, starts, block_rows, lane), queries[p], 1, 1)
            for p, lane in enumerate(lanes)
        ]
        grad_probs = [
            contract(stacked(v_ref, starts, block_rows, lane), grads[p] * scale, 1, 1)
            for p, lane in enumerate(lanes)
        ]
        for p, lane in enumerate(lanes):
            stat = pl.ds(block * (QUAD // PAIR) + p, 1)
            probs = jnp.exp2((scores[p] - top_ref[0, stat, :]) * (scale * LOG2_E))
            probs = probs * inverse_ref[0, stat, :]
            total = jnp.sum(probs * grad_probs[p], axis=0, keepdims=True)
            grad_scores = (probs * (grad_probs[p] - total)).astype(jnp.bfloat16)
            probs_b = probs.astype(jnp.bfloat16)
            grad_values = jnp.dot(probs_b, grads[p], preferred_element_type=jnp.float32)
            grad_keys = jnp.dot(grad_scores, queries[p], preferred_element_type=jnp.float32)
            joined = join_heads(
                jnp.dot(
                    beside(kt_ref, starts, block_rows, lane),
                    grad_scores,
                    preferred_element_type=jnp.float32,
                ),
                head_dim,
            )
            gq_ref[own, lane] = joined.T.astype(jnp.bfloat16)
            for slot, start in enumerate(starts):
                rows = pl.ds(start, block_rows)
                part = slice(slot * block_rows, (slot + 1) * block_rows)
                for acc, terms in ((gk_acc, grad_keys), (gv_acc, grad_values)):
                    term = terms[part]
                    if slot > 0:
                        term = term.astype(jnp.bfloat16).astype(jnp.float32)
                    acc[rows, lane] += term

    for_each_block(sectors_ref, lists_ref, block_count, block_rows, work)
    gk_ref[...] = gk_acc[...].astype(jnp.bfloat16)
    gv_ref[...] = gv_acc[...].astype(jnp.bfloat16)
    products = [(normed_t_ref, ref, slice(None)) for ref in (gq_ref, gk_ref, gv_ref)]
    products.append((att_ref, cot_ref, slice(which * quad, (which + 1) * quad)))
    for i, (left, right, lanes) in enumerate(products):
        terms = contract(left[...], right[:, lanes], 1, 0)
        if not last:
            whole_ref[i * width : (i + 1) * width, :] = terms
            continue
        apart = i ^ lax.axis_index("sample")

        @pl.when(apart % 2 == 0)
        def _():
            keep_ref[apart // 2, :width] = terms

        @pl.when(apart % 2 == 1)
        def _():
            send_ref[apart // 2, :width] = terms

    if not last:
        return
    chunk = min(row_count, 256)
    sum_ref[...] = jnp.zeros_like(sum_ref)
    for start in range(0, row_count, chunk):
        rows = slice(start, start + chunk)
        scaled, inverse, _ = normalize(x_ref[rows, :], gain_ref[...])
        grad_normed = jnp.zeros((chunk, width), jnp.float32)
        for i in range(width // quad):
            parts = before[3 * i : 3 * i + 3] if i < which else (gq_ref, gk_ref, gv_ref)
            for ref, weight_ref in zip(parts, (wq_ref, wk_ref, wv_ref)):
                grad_normed += contract(
                    ref[rows, :], weight_ref[:, i * quad : (i + 1) * quad], 1, 1
                )
        sum_ref[...] += jnp.sum(grad_normed * scaled, axis=0, keepdims=True)
        grad_scaled = grad_normed * gain_ref[...]
        grad_input = inverse * (
            grad_scaled
            - jnp.mean(grad_scaled, axis=-1, keepdims=True)
            - scaled * jnp.mean(grad_scaled * scaled, axis=-1, keepdims=True)
        )
        grad_ref[rows, :] = (cot_ref[rows, :].astype(jnp.float32) + grad_input).astype(jnp.bfloat16)
    for ref in (keep_ref, send_ref):
        for i in range(width // quad):
            start = width + i * GAIN_ROWS
            ref[:, start : start + GAIN_ROWS, :] = jnp.broadcast_to(
                sum_ref[:, i * quad : (i + 1) * quad], (ref.shape[0], GAIN_ROWS, quad)
            )


def backward(sectors, adjacency, cotangent, out_weight, normed_t, queries, keys, values, keys_t,
             attended_t, tops, inverses, block_rows, which, *ending):
    row_count, width = cotangent.shape
    block_count = row_count // block_rows
    head_dim = width // HEADS
    quad = QUAD * head_dim
    fixed = lambda *shape: pl.BlockSpec(shape, lambda i, *lists: (0,) * len(shape))
    across = pl.BlockSpec((row_count, quad), lambda i, *lists: (0, which))
    down = lambda size: pl.BlockSpec((quad, size), lambda i, *lists: (which, 0))
    stat = pl.BlockSpec((1,) + tops.shape[1:], lambda i, *lists: (which, 0, 0))
    part = jax.ShapeDtypeStruct((row_count, quad), jnp.bfloat16)
    halves = (2, width + GAIN_ROWS * (width // quad), quad)
    scratch = [
        pltpu.VMEM((row_count, quad), jnp.bfloat16),
        pltpu.VMEM((row_count, quad), jnp.float32),
        pltpu.VMEM((row_count, quad), jnp.float32),
    ]
    if ending:
        out_shape = [jax.ShapeDtypeStruct((row_count, width), jnp.bfloat16)]
        out_shape += [jax.ShapeDtypeStruct(halves, jnp.float32)] * 2
        scratch = [pltpu.VMEM((row_count, quad), jnp.bfloat16)] * 3 + scratch
        scratch.append(pltpu.VMEM((1, width), jnp.float32))
    else:
        out_shape = [part] * 3 + [jax.ShapeDtypeStruct((4 * width, quad), jnp.float32)]
    return pl.pallas_call(
        lambda *refs: backward_kernel(block_rows, head_dim, which, bool(ending), *refs),
        grid_spec=pltpu.PrefetchScalarGridSpec(
            num_scalar_prefetch=2,
            grid=(1,),
            in_specs=[fixed(row_count, width), down(width), fixed(width, row_count)]
            + [across] * 3
            + [down(row_count), fixed(width, row_count)]
            + [stat] * 2
            + [fixed(*array.shape) for array in ending],
            out_specs=[fixed(*struct.shape) for struct in out_shape],
            scratch_shapes=scratch,
        ),
        out_shape=out_shape,
        compiler_params=pltpu.CompilerParams(vmem_limit_bytes=VMEM_LIMIT),
        cost_estimate=pl.CostEstimate(
            flops=10 * row_count * width * quad
            + 80 * row_count * block_rows * quad
            + 6 * row_count * width * width * bool(ending),
            bytes_accessed=14 * row_count * width,
            transcendentals=row_count * 4 * block_rows * QUAD,
        ),
        name="backward",
    )(sectors, adjacency, cotangent, out_weight, normed_t, queries, keys, values, keys_t, attended_t,
      tops, inverses, *ending)


def swap(tensor, axis):
    return lax.all_to_all(tensor, axis, split_axis=0, concat_axis=0, tiled=True)


def across(tensor, axis, distance):
    size = lax.axis_size(axis)
    return lax.ppermute(tensor, axis, [(i, i ^ distance) for i in range(size)])


def across(tensor, axis, distance):
    size = lax.axis_size(axis)
    return lax.ppermute(tensor, axis, [(i, i ^ distance) for i in range(size)])


def reduce_halves(keep, send, width):
    sums = keep + across(send, "sample", 1)
    sums = sums[0] + across(sums[1].astype(jnp.bfloat16), "sample", 2).astype(jnp.float32)
    sums = lax.psum(sums, "turb")
    gain = sums[width:].reshape(-1, GAIN_ROWS, sums.shape[1])[:, 0].reshape(width)
    own = sums[:width].astype(jnp.bfloat16)
    both = [own, across(own, "sample", 2)]
    return both + [across(part, "sample", 1) for part in both], gain


def place_kernel(whole_ref, *refs):
    (*parts, query_ref, key_ref, value_ref, out_ref, all_ref) = refs
    own = lax.axis_index("sample")
    width, quad = parts[0].shape
    for i, ref in enumerate(parts):
        all_ref[own ^ ((i % 2) * 2 + i // 2)] = ref[...].astype(jnp.float32)
    for i, ref in enumerate((query_ref, key_ref, value_ref, out_ref)):
        ref[:, :quad] = whole_ref[i * width : (i + 1) * width, :]
        ref[:, quad:] = all_ref[i]


def place_sums(whole, parts):
    width, quad = parts[0].shape
    return pl.pallas_call(
        place_kernel,
        in_specs=[pl.BlockSpec(memory_space=pltpu.VMEM)] * (1 + len(parts)),
        out_specs=[pl.BlockSpec(memory_space=pltpu.VMEM)] * 4,
        out_shape=[jax.ShapeDtypeStruct((width, 2 * quad), jnp.float32)] * 4,
        scratch_shapes=[pltpu.VMEM((4, width, quad), jnp.float32)],
        compiler_params=pltpu.CompilerParams(vmem_limit_bytes=VMEM_LIMIT),
        cost_estimate=pl.CostEstimate(
            flops=0, bytes_accessed=28 * width * width, transcendentals=0
        ),
        name="place",
    )(whole, *parts)


def by_sample(
    inflow,
    cotangent,
    norm_gain,
    query_weight,
    key_weight,
    value_weight,
    out_weight,
    adjacency,
    sectors,
):
    sample_count, block_rows, width = inflow.shape
    row_count = lax.axis_size("turb") * block_rows
    rows = swap(inflow, "turb")
    rows, cotangent = lax.optimization_barrier((rows, cotangent))
    rows = rows.reshape(row_count, width)
    grad_rows = swap(cotangent, "turb").reshape(row_count, width)
    *saved, layer_rows = forward(
        sectors, adjacency, rows, norm_gain, query_weight, key_weight, value_weight, out_weight,
        block_rows,
    )
    layer_output = swap(layer_rows.reshape(inflow.shape), "turb")
    *grads, whole = backward(
        sectors, adjacency, grad_rows, out_weight, *saved, block_rows, 0
    )
    whole = lax.psum(whole, ("sample", "turb"))
    grad_rows, keep, send = backward(
        sectors, adjacency, grad_rows, out_weight, *saved, block_rows, 1,
        rows, norm_gain.reshape(1, width), query_weight, key_weight, value_weight, *grads,
    )
    grad_inflow = swap(grad_rows.reshape(inflow.shape), "turb")
    parts, sum_gain = reduce_halves(keep, send, width)
    sums = place_sums(whole, parts)
    return (layer_output, grad_inflow, *sums, sum_gain)


def solution(mesh):
    placed = (
        P("sample", "turb", None),
        P("sample", "turb", None),
        P(),
        P(),
        P(),
        P(),
        P(),
        P(),
        P("sample"),
    )

    def plan(*args):
        sample_count = args[0].shape[0]
        if sample_count == mesh.shape["turb"] and mesh.shape["sample"] == 4:
            return by_sample(*args)
        return on_device(*args)

    return jax.shard_map(
        plan,
        mesh=mesh,
        in_specs=placed,
        out_specs=(P("sample", "turb", None), P("sample", "turb", None), P(), P(), P(), P(), P()),
        check_vma=False,
    )
```

```python
import jax
import jax.numpy as jnp
from jax import lax
from jax.experimental import pallas as pl
from jax.experimental.pallas import tpu as pltpu
from jax.sharding import PartitionSpec as P

HEADS = 8
UPSTREAM = 3
SECTORS = 8
REPEAT = 1


epsilon = 1e-05


def normalize(row_block, norm_gain):
    widened = row_block.astype(jnp.float32)
    centred = widened - jnp.mean(widened, axis=-1, keepdims=True)
    inverse = lax.rsqrt(jnp.mean(centred * centred, axis=-1, keepdims=True) + epsilon)
    scaled = centred * inverse
    return (scaled, inverse, (scaled * norm_gain).astype(jnp.bfloat16))


def attend(pieces):
    queries, key_rows, value_rows, key_usable, grad_attended = pieces
    batch_count, query_count, model_width = queries.shape
    key_count = key_rows.shape[1]
    head_dim = model_width // HEADS
    score_scale = head_dim ** (-0.5)
    query_heads = queries.reshape(batch_count, query_count, HEADS, head_dim)
    key_heads = key_rows.reshape(batch_count, key_count, HEADS, head_dim)
    value_heads = value_rows.reshape(batch_count, key_count, HEADS, head_dim)
    grad_heads = grad_attended.reshape(batch_count, query_count, HEADS, head_dim)
    scores = (
        jnp.einsum("nqhd,nkhd->nhqk", query_heads, key_heads, preferred_element_type=jnp.float32)
        * score_scale
    )
    scores = jnp.where(key_usable[:, None, None, :], scores, -1e30)
    highest = jnp.max(scores, axis=-1, keepdims=True)
    weights = jnp.exp(scores - highest)
    probabilities = weights / jnp.sum(weights, axis=-1, keepdims=True)
    rounded = probabilities.astype(jnp.bfloat16)
    attended = jnp.einsum(
        "nhqk,nkhd->nqhd", rounded, value_heads, preferred_element_type=jnp.float32
    ).astype(jnp.bfloat16)
    grad_probs = jnp.einsum(
        "nqhd,nkhd->nhqk", grad_heads, value_heads, preferred_element_type=jnp.float32
    )
    centred = grad_probs - jnp.sum(probabilities * grad_probs, axis=-1, keepdims=True)
    grad_scores = (probabilities * centred * score_scale).astype(jnp.bfloat16)
    grad_queries = jnp.einsum(
        "nhqk,nkhd->nqhd", grad_scores, key_heads, preferred_element_type=jnp.float32
    ).astype(jnp.bfloat16)
    grad_keys = jnp.einsum(
        "nhqk,nqhd->nkhd", grad_scores, query_heads, preferred_element_type=jnp.float32
    )
    grad_values = jnp.einsum(
        "nhqk,nqhd->nkhd", rounded, grad_heads, preferred_element_type=jnp.float32
    )
    pair_terms = jnp.concatenate(
        [
            grad_keys.reshape(batch_count, key_count, model_width),
            grad_values.reshape(batch_count, key_count, model_width),
        ],
        axis=-1,
    )
    return (
        attended.reshape(batch_count, query_count, model_width),
        grad_queries.reshape(batch_count, query_count, model_width),
        pair_terms,
    )


def on_device(
    inflow,
    cotangent,
    norm_gain,
    query_weight,
    key_weight,
    value_weight,
    out_weight,
    adjacency,
    sectors,
):
    sample_count, block_rows, model_width = inflow.shape
    block_count = lax.axis_size("turb")
    own_block = lax.axis_index("turb")
    slot_count = REPEAT * ((SECTORS * UPSTREAM + block_count - 2) // (block_count - 1))
    flat_rows = sample_count * block_rows
    pair_width = 2 * model_width
    input_rows = inflow.reshape(flat_rows, model_width)
    grad_rows = cotangent.reshape(flat_rows, model_width)
    scaled, inverse, normed = normalize(input_rows, norm_gain)
    queries = jnp.dot(normed, query_weight, preferred_element_type=jnp.float32).astype(jnp.bfloat16)
    key_rows = jnp.dot(normed, key_weight, preferred_element_type=jnp.float32).astype(jnp.bfloat16)
    value_rows = jnp.dot(normed, value_weight, preferred_element_type=jnp.float32).astype(
        jnp.bfloat16
    )
    upstream = adjacency[sectors]
    needed = jnp.any(upstream == own_block, axis=2).astype(jnp.int32)
    earlier_need = jnp.cumsum(needed, axis=0) - needed
    slot_index = lax.broadcasted_iota(jnp.int32, (block_count, slot_count, sample_count), 1)
    chosen = (needed.T[:, None, :] == 1) & (earlier_need.T[:, None, :] == slot_index)
    selector = chosen.astype(jnp.bfloat16).reshape(block_count * slot_count, sample_count)
    own_lists = lax.dynamic_index_in_dim(upstream, own_block, axis=1, keepdims=False)
    usable = own_lists >= 0
    matches = jnp.any(own_lists[:, :, None, None] == own_lists[None, None, :, :], axis=3)
    sample_ids = lax.broadcasted_iota(jnp.int32, (sample_count, sample_count), 0)
    earlier = lax.broadcasted_iota(jnp.int32, (sample_count, sample_count), 1) < sample_ids
    position = jnp.sum((matches & earlier[:, None, :]).astype(jnp.int32), axis=2)
    flat_slot = own_lists * slot_count + position
    fetch_at = jnp.where(usable, flat_slot, 0)
    payload = jnp.concatenate([key_rows, value_rows], axis=1).reshape(
        sample_count, block_rows * pair_width
    )
    packed = jnp.dot(selector, payload, preferred_element_type=jnp.float32).astype(jnp.bfloat16)
    arrived = lax.all_to_all(
        packed.reshape(block_count, slot_count, block_rows, pair_width),
        "turb",
        split_axis=0,
        concat_axis=0,
        tiled=True,
    )
    fetched = arrived.reshape(block_count * slot_count, block_rows, pair_width)[fetch_at]
    upstream_keys = fetched[..., :model_width]
    upstream_values = fetched[..., model_width:]
    key_count = (1 + UPSTREAM) * block_rows
    key_all = jnp.concatenate(
        [key_rows.reshape(sample_count, 1, block_rows, model_width), upstream_keys], axis=1
    ).reshape(sample_count, key_count, model_width)
    value_all = jnp.concatenate(
        [value_rows.reshape(sample_count, 1, block_rows, model_width), upstream_values], axis=1
    ).reshape(sample_count, key_count, model_width)
    block_usable = jnp.concatenate([jnp.ones((sample_count, 1), dtype=jnp.bool_), usable], axis=1)
    key_usable = jnp.repeat(block_usable, block_rows, axis=1)
    grad_attended = jnp.dot(grad_rows, out_weight.T, preferred_element_type=jnp.float32).astype(
        jnp.bfloat16
    )
    group_size = min(sample_count, max(1, 512 // block_rows))
    while sample_count % group_size != 0:
        group_size = group_size - 1
    group_count = sample_count // group_size

    def grouped(tensor):
        return tensor.reshape((group_count, group_size) + tensor.shape[1:])

    attended, grad_queries, pair_terms = lax.map(
        attend,
        (
            grouped(queries.reshape(sample_count, block_rows, model_width)),
            grouped(key_all),
            grouped(value_all),
            grouped(key_usable),
            grouped(grad_attended.reshape(sample_count, block_rows, model_width)),
        ),
    )
    attended = attended.reshape(flat_rows, model_width)
    grad_queries = grad_queries.reshape(flat_rows, model_width)
    pair_terms = pair_terms.reshape(sample_count, 1 + UPSTREAM, block_rows, pair_width)
    layer_output = (
        (
            input_rows.astype(jnp.float32)
            + jnp.dot(attended, out_weight, preferred_element_type=jnp.float32)
        )
        .astype(jnp.bfloat16)
        .reshape(inflow.shape)
    )
    outgoing = (
        pair_terms[:, 1:]
        .astype(jnp.bfloat16)
        .reshape(sample_count * UPSTREAM, block_rows, pair_width)
    )
    target = jnp.where(usable, flat_slot, block_count * slot_count).reshape(-1)
    outbound = (
        jnp.zeros((block_count * slot_count, block_rows, pair_width), jnp.bfloat16)
        .at[target]
        .set(outgoing, mode="drop")
    )
    sum_out = jnp.dot(attended.T, grad_rows, preferred_element_type=jnp.float32)
    sum_query = jnp.dot(normed.T, grad_queries, preferred_element_type=jnp.float32)
    returned = lax.all_to_all(
        outbound.reshape(block_count, slot_count, block_rows, pair_width),
        "turb",
        split_axis=0,
        concat_axis=0,
        tiled=True,
    )
    remote = jnp.dot(
        selector.T,
        returned.reshape(block_count * slot_count, block_rows * pair_width),
        preferred_element_type=jnp.float32,
    )
    combined = (
        (pair_terms[:, 0].reshape(sample_count, block_rows * pair_width) + remote)
        .astype(jnp.bfloat16)
        .reshape(flat_rows, pair_width)
    )
    grad_keys = combined[:, :model_width]
    grad_values = combined[:, model_width:]
    sum_key = jnp.dot(normed.T, grad_keys, preferred_element_type=jnp.float32)
    sum_value = jnp.dot(normed.T, grad_values, preferred_element_type=jnp.float32)
    grad_normed = jnp.dot(grad_queries, query_weight.T, preferred_element_type=jnp.float32)
    grad_normed = grad_normed + jnp.dot(grad_keys, key_weight.T, preferred_element_type=jnp.float32)
    grad_normed = grad_normed + jnp.dot(
        grad_values, value_weight.T, preferred_element_type=jnp.float32
    )
    sum_gain = jnp.sum(grad_normed * scaled, axis=0)
    grad_scaled = grad_normed * norm_gain
    grad_input = inverse * (
        grad_scaled
        - jnp.mean(grad_scaled, axis=-1, keepdims=True)
        - scaled * jnp.mean(grad_scaled * scaled, axis=-1, keepdims=True)
    )
    grad_inflow = (
        (grad_rows.astype(jnp.float32) + grad_input).astype(jnp.bfloat16).reshape(inflow.shape)
    )
    sum_query, sum_key, sum_value, sum_out, sum_gain = lax.psum(
        (sum_query, sum_key, sum_value, sum_out, sum_gain), ("sample", "turb")
    )
    return (layer_output, grad_inflow, sum_query, sum_key, sum_value, sum_out, sum_gain)


PAIR = 2
QUAD = 4
LOG2_E = 1.4426950408889634
VMEM_LIMIT = 58 * 2**20
GAIN_ROWS = 4
SAMPLES = 4
TURBS = 8


def turb_place(apart):
    return (apart % 2) * 4 + (apart // 4) * 2 + (apart // 2) % 2


def contract(left, right, left_dim, right_dim):
    return lax.dot_general(
        left, right, (((left_dim,), (right_dim,)), ((), ())), preferred_element_type=jnp.float32
    )


def split_heads(rows, head_dim):
    lane = lax.broadcasted_iota(jnp.int32, rows.shape, 1)
    wide = rows.astype(jnp.float32)
    return jnp.concatenate(
        [jnp.where(lane < head_dim, wide, 0.0), jnp.where(lane >= head_dim, wide, 0.0)], axis=0
    ).astype(jnp.bfloat16)


def join_heads(wide, head_dim):
    block_rows = wide.shape[1] // PAIR
    first = lax.broadcasted_iota(jnp.int32, (wide.shape[0], block_rows), 0) < head_dim
    return jnp.where(first, wide[:, :block_rows], wide[:, block_rows:])


def for_each_block(sectors_ref, lists_ref, block_count, block_rows, work):
    sector = sectors_ref[lax.axis_index("turb")]

    def step(block, carry):
        used = jnp.int32(0)
        for slot in range(UPSTREAM):
            used = used + (lists_ref[sector, block, slot] >= 0).astype(jnp.int32)
        for count in range(UPSTREAM + 1):

            @pl.when(used == count)
            def _():
                sources = [block] + [
                    lists_ref[sector, block, slot] for slot in range(count)
                ]
                work(block, [pl.multiple_of(s * block_rows, block_rows) for s in sources])

        return carry

    lax.fori_loop(0, block_count, step, 0)


def stacked(ref, starts, block_rows, lanes):
    return jnp.concatenate([ref[pl.ds(s, block_rows), lanes] for s in starts], axis=0)


def beside(ref, starts, block_rows, rows):
    return jnp.concatenate([ref[rows, pl.ds(s, block_rows)] for s in starts], axis=1)


def forward_kernel(block_rows, head_dim, sectors_ref, lists_ref, x_ref, gain_ref, wq_ref, wk_ref,
                   wv_ref, wo_ref, normed_t_ref, q_ref, k_ref, v_ref, kt_ref, att_ref,
                   top_ref, inverse_ref, out_ref, normed_ref, vt_ref, rows_ref, sum_ref):
    row_count = x_ref.shape[0]
    quad = pl.program_id(0)
    pair = PAIR * head_dim
    exponent = head_dim ** (-0.5) * LOG2_E
    chunk = min(row_count, 256)

    @pl.when(quad == 0)
    def _():
        for start in range(0, row_count, chunk):
            part = slice(start, start + chunk)
            scaled, _, normed = normalize(x_ref[part, :], gain_ref[...])
            normed_ref[part, :] = normed
            normed_t_ref[:, part] = (scaled * gain_ref[...]).T.astype(jnp.bfloat16)

    normed = normed_ref[...]
    q_ref[...] = contract(normed, wq_ref[...], 1, 0).astype(jnp.bfloat16)
    k_ref[...] = contract(normed, wk_ref[...], 1, 0).astype(jnp.bfloat16)
    v_ref[...] = contract(normed, wv_ref[...], 1, 0).astype(jnp.bfloat16)
    kt_ref[...] = contract(wk_ref[...], normed, 0, 1).astype(jnp.bfloat16)
    vt_ref[...] = contract(wv_ref[...], normed, 0, 1).astype(jnp.bfloat16)

    def work(block, starts):
        own = pl.ds(starts[0], block_rows)
        lanes = [slice(p * pair, (p + 1) * pair) for p in range(QUAD // PAIR)]
        scores = [
            contract(
                stacked(k_ref, starts, block_rows, lane), split_heads(q_ref[own, lane], head_dim), 1, 1
            )
            for lane in lanes
        ]
        for p, lane in enumerate(lanes):
            highest = jnp.max(scores[p], axis=0, keepdims=True)
            weights = jnp.exp2((scores[p] - highest) * exponent)
            inverse = 1.0 / jnp.sum(weights, axis=0, keepdims=True)
            probs = (weights * inverse).astype(jnp.bfloat16)
            top_ref[0, pl.ds(block * (QUAD // PAIR) + p, 1), :] = highest
            inverse_ref[0, pl.ds(block * (QUAD // PAIR) + p, 1), :] = inverse
            joined = join_heads(
                jnp.dot(
                    beside(vt_ref, starts, block_rows, lane),
                    probs,
                    preferred_element_type=jnp.float32,
                ),
                head_dim,
            )
            att_ref[lane, own] = joined.astype(jnp.bfloat16)
            rows_ref[own, lane] = joined.T.astype(jnp.bfloat16)

    for_each_block(sectors_ref, lists_ref, row_count // block_rows, block_rows, work)
    part = contract(rows_ref[...], wo_ref[...], 1, 0)

    @pl.when(quad == 0)
    def _():
        sum_ref[...] = x_ref[...].astype(jnp.float32) + part

    @pl.when(quad > 0)
    def _():
        sum_ref[...] += part

    @pl.when(quad == pl.num_programs(0) - 1)
    def _():
        out_ref[...] = sum_ref[...].astype(jnp.bfloat16)


def forward(sectors, adjacency, rows, norm_gain, query_weight, key_weight, value_weight, out_weight, block_rows):
    row_count, width = rows.shape
    head_dim = width // HEADS
    quad = QUAD * head_dim
    quads = width // quad
    stat_rows = row_count // block_rows * (QUAD // PAIR)
    fixed = lambda *shape: pl.BlockSpec(shape, lambda p, *lists: (0,) * len(shape))
    across = lambda size: pl.BlockSpec((size, quad), lambda p, *lists: (0, p))
    down = lambda size: pl.BlockSpec((quad, size), lambda p, *lists: (p, 0))
    stat = pl.BlockSpec((1, stat_rows, PAIR * block_rows), lambda p, *lists: (p, 0, 0))
    flat = jax.ShapeDtypeStruct((row_count, width), jnp.bfloat16)
    turned = jax.ShapeDtypeStruct((width, row_count), jnp.bfloat16)
    stats = jax.ShapeDtypeStruct((quads, stat_rows, PAIR * block_rows), jnp.float32)
    return pl.pallas_call(
        lambda *refs: forward_kernel(block_rows, head_dim, *refs),
        grid_spec=pltpu.PrefetchScalarGridSpec(
            num_scalar_prefetch=2,
            grid=(quads,),
            in_specs=[fixed(row_count, width), fixed(1, width)]
            + [across(width)] * 3
            + [down(width)],
            out_specs=[fixed(width, row_count)]
            + [across(row_count)] * 3
            + [down(row_count)] * 2
            + [stat] * 2
            + [fixed(row_count, width)],
            scratch_shapes=[
                pltpu.VMEM((row_count, width), jnp.bfloat16),
                pltpu.VMEM((quad, row_count), jnp.bfloat16),
                pltpu.VMEM((row_count, quad), jnp.bfloat16),
                pltpu.VMEM((row_count, width), jnp.float32),
            ],
        ),
        out_shape=[turned, flat, flat, flat, turned, turned, stats, stats, flat],
        compiler_params=pltpu.CompilerParams(vmem_limit_bytes=VMEM_LIMIT),
        cost_estimate=pl.CostEstimate(
            flops=12 * row_count * width * width + 32 * row_count * block_rows * width,
            bytes_accessed=20 * row_count * width,
            transcendentals=row_count * 4 * block_rows * HEADS,
        ),
        name="forward",
    )(sectors, adjacency, rows, norm_gain.reshape(1, width), query_weight, key_weight, value_weight,
      out_weight)


def backward_kernel(block_rows, head_dim, which, last, sectors_ref, lists_ref, cot_ref, wo_ref,
                    normed_t_ref, q_ref, k_ref, v_ref, kt_ref, att_ref, top_ref, inverse_ref, *refs):
    if last:
        x_ref, gain_ref, wq_ref, wk_ref, wv_ref, *refs = refs
        before, refs = refs[: 3 * which], refs[3 * which :]
        grad_ref, keep_ref, send_ref, gq_ref, gk_ref, gv_ref, ga_ref, gk_acc, gv_acc, sum_ref = refs
    else:
        gq_ref, gk_ref, gv_ref, keep_ref, send_ref, ga_ref, gk_acc, gv_acc = refs
    row_count, width = cot_ref.shape
    block_count = row_count // block_rows
    pair = PAIR * head_dim
    quad = QUAD * head_dim
    scale = head_dim ** (-0.5)
    ga_ref[...] = contract(cot_ref[...], wo_ref[...], 1, 1).astype(jnp.bfloat16)
    gk_acc[...] = jnp.zeros_like(gk_acc)
    gv_acc[...] = jnp.zeros_like(gv_acc)

    def work(block, starts):
        own = pl.ds(starts[0], block_rows)
        lanes = [slice(p * pair, (p + 1) * pair) for p in range(QUAD // PAIR)]
        queries = [split_heads(q_ref[own, lane], head_dim) for lane in lanes]
        grads = [split_heads(ga_ref[own, lane], head_dim) for lane in lanes]
        scores = [
            contract(stacked(k_ref, starts, block_rows, lane), queries[p], 1, 1)
            for p, lane in enumerate(lanes)
        ]
        grad_probs = [
            contract(stacked(v_ref, starts, block_rows, lane), grads[p] * scale, 1, 1)
            for p, lane in enumerate(lanes)
        ]
        for p, lane in enumerate(lanes):
            stat = pl.ds(block * (QUAD // PAIR) + p, 1)
            probs = jnp.exp2((scores[p] - top_ref[0, stat, :]) * (scale * LOG2_E))
            probs = probs * inverse_ref[0, stat, :]
            total = jnp.sum(probs * grad_probs[p], axis=0, keepdims=True)
            grad_scores = (probs * (grad_probs[p] - total)).astype(jnp.bfloat16)
            probs_b = probs.astype(jnp.bfloat16)
            grad_values = jnp.dot(probs_b, grads[p], preferred_element_type=jnp.float32)
            grad_keys = jnp.dot(grad_scores, queries[p], preferred_element_type=jnp.float32)
            joined = join_heads(
                jnp.dot(
                    beside(kt_ref, starts, block_rows, lane),
                    grad_scores,
                    preferred_element_type=jnp.float32,
                ),
                head_dim,
            )
            gq_ref[own, lane] = joined.T.astype(jnp.bfloat16)
            for slot, start in enumerate(starts):
                rows = pl.ds(start, block_rows)
                part = slice(slot * block_rows, (slot + 1) * block_rows)
                for acc, terms in ((gk_acc, grad_keys), (gv_acc, grad_values)):
                    term = terms[part]
                    if slot > 0:
                        term = term.astype(jnp.bfloat16).astype(jnp.float32)
                    acc[rows, lane] += term

    for_each_block(sectors_ref, lists_ref, block_count, block_rows, work)
    gk_ref[...] = gk_acc[...].astype(jnp.bfloat16)
    gv_ref[...] = gv_acc[...].astype(jnp.bfloat16)
    products = [(normed_t_ref, ref, slice(None)) for ref in (gq_ref, gk_ref, gv_ref)]
    products.append((att_ref, cot_ref, slice(which * quad, (which + 1) * quad)))
    own_sample, own_turb = lax.axis_index("sample"), lax.axis_index("turb")
    share = width // TURBS
    for i, (left, right, lanes) in enumerate(products):
        terms = contract(left[...], right[:, lanes], 1, 0)
        apart = i ^ own_sample
        first, second = (apart % 2, apart // 2) if last else (apart // 2, apart % 2)

        def store(ref):
            for turb in range(TURBS):
                start = pl.multiple_of(second * width + turb_place(turb ^ own_turb) * share, share)
                ref[pl.ds(start, share), :] = terms[turb * share : (turb + 1) * share].astype(
                    ref.dtype
                )

        @pl.when(first == 0)
        def _():
            store(keep_ref)

        @pl.when(first == 1)
        def _():
            store(send_ref)

    if not last:
        return
    chunk = min(row_count, 256)
    sum_ref[...] = jnp.zeros_like(sum_ref)
    for start in range(0, row_count, chunk):
        rows = slice(start, start + chunk)
        scaled, inverse, _ = normalize(x_ref[rows, :], gain_ref[...])
        grad_normed = jnp.zeros((chunk, width), jnp.float32)
        for i in range(width // quad):
            parts = before[3 * i : 3 * i + 3] if i < which else (gq_ref, gk_ref, gv_ref)
            for ref, weight_ref in zip(parts, (wq_ref, wk_ref, wv_ref)):
                grad_normed += contract(
                    ref[rows, :], weight_ref[:, i * quad : (i + 1) * quad], 1, 1
                )
        sum_ref[...] += jnp.sum(grad_normed * scaled, axis=0, keepdims=True)
        grad_scaled = grad_normed * gain_ref[...]
        grad_input = inverse * (
            grad_scaled
            - jnp.mean(grad_scaled, axis=-1, keepdims=True)
            - scaled * jnp.mean(grad_scaled * scaled, axis=-1, keepdims=True)
        )
        grad_ref[rows, :] = (cot_ref[rows, :].astype(jnp.float32) + grad_input).astype(jnp.bfloat16)
    for ref in (keep_ref, send_ref):
        for i in range(width // quad):
            start = 2 * width + i * GAIN_ROWS
            ref[start : start + GAIN_ROWS, :] = jnp.broadcast_to(
                sum_ref[:, i * quad : (i + 1) * quad], (GAIN_ROWS, quad)
            )


def backward(sectors, adjacency, cotangent, out_weight, normed_t, queries, keys, values, keys_t,
             attended_t, tops, inverses, block_rows, which, *ending):
    row_count, width = cotangent.shape
    block_count = row_count // block_rows
    head_dim = width // HEADS
    quad = QUAD * head_dim
    fixed = lambda *shape: pl.BlockSpec(shape, lambda i, *lists: (0,) * len(shape))
    across = pl.BlockSpec((row_count, quad), lambda i, *lists: (0, which))
    down = lambda size: pl.BlockSpec((quad, size), lambda i, *lists: (which, 0))
    stat = pl.BlockSpec((1,) + tops.shape[1:], lambda i, *lists: (which, 0, 0))
    part = jax.ShapeDtypeStruct((row_count, quad), jnp.bfloat16)
    gain_rows = GAIN_ROWS * (width // quad)
    scratch = [
        pltpu.VMEM((row_count, quad), jnp.bfloat16),
        pltpu.VMEM((row_count, quad), jnp.float32),
        pltpu.VMEM((row_count, quad), jnp.float32),
    ]
    if ending:
        out_shape = [jax.ShapeDtypeStruct((row_count, width), jnp.bfloat16)]
        out_shape += [jax.ShapeDtypeStruct((2 * width + gain_rows, quad), jnp.float32)] * 2
        scratch = [pltpu.VMEM((row_count, quad), jnp.bfloat16)] * 3 + scratch
        scratch.append(pltpu.VMEM((1, width), jnp.float32))
    else:
        out_shape = [part] * 3 + [
            jax.ShapeDtypeStruct((2 * width, quad), dtype) for dtype in (jnp.float32, jnp.bfloat16)
        ]
    return pl.pallas_call(
        lambda *refs: backward_kernel(block_rows, head_dim, which, bool(ending), *refs),
        grid_spec=pltpu.PrefetchScalarGridSpec(
            num_scalar_prefetch=2,
            grid=(1,),
            in_specs=[fixed(row_count, width), down(width), fixed(width, row_count)]
            + [across] * 3
            + [down(row_count), fixed(width, row_count)]
            + [stat] * 2
            + [fixed(*array.shape) for array in ending],
            out_specs=[fixed(*struct.shape) for struct in out_shape],
            scratch_shapes=scratch,
        ),
        out_shape=out_shape,
        compiler_params=pltpu.CompilerParams(vmem_limit_bytes=VMEM_LIMIT),
        cost_estimate=pl.CostEstimate(
            flops=10 * row_count * width * quad
            + 80 * row_count * block_rows * quad
            + 6 * row_count * width * width * bool(ending),
            bytes_accessed=14 * row_count * width,
            transcendentals=row_count * 4 * block_rows * QUAD,
        ),
        name="backward",
    )(sectors, adjacency, cotangent, out_weight, normed_t, queries, keys, values, keys_t, attended_t,
      tops, inverses, *ending)


def swap(tensor, axis):
    return lax.all_to_all(tensor, axis, split_axis=0, concat_axis=0, tiled=True)


def across(tensor, axis, distance):
    size = lax.axis_size(axis)
    return lax.ppermute(tensor, axis, [(i, i ^ distance) for i in range(size)])


def across(tensor, axis, distance):
    size = lax.axis_size(axis)
    return lax.ppermute(tensor, axis, [(i, i ^ distance) for i in range(size)])


def reduce_sums(early, late, width):
    quad = early[0].shape[1]
    wide = jnp.float32

    def pack(gain):
        high = gain.astype(jnp.bfloat16)
        low = (gain - high.astype(wide)).astype(jnp.bfloat16)
        return jnp.concatenate([high, low, jnp.zeros((16 - 2 * gain.shape[0], quad), jnp.bfloat16)])

    def unpack(rows, count):
        return rows[:count].astype(wide) + rows[count : 2 * count].astype(wide)

    keep, arrived = early
    first = keep + arrived.astype(wide)
    first = first[:width] + across(first[width:], "sample", 1)
    keep, arrived = late
    second = keep + arrived
    gain = second[2 * width :: GAIN_ROWS]
    count = gain.shape[0]
    arrived = across(
        jnp.concatenate([second[width : 2 * width].astype(jnp.bfloat16), pack(gain)]), "sample", 2
    )
    second = second[:width] + arrived[:width].astype(wide)
    gain = gain + unpack(arrived[width:], count)
    for distance in (1, 4, 2):
        half = first.shape[0] // 2
        halves = [part[half:].astype(jnp.bfloat16) for part in (first, second)]
        arrived = across(jnp.concatenate(halves + [pack(gain)]), "turb", distance)
        first = first[:half] + arrived[:half].astype(wide)
        second = second[:half] + arrived[half : 2 * half].astype(wide)
        gain = gain + unpack(arrived[2 * half :], count)
    total = jnp.stack([first, second]).astype(jnp.bfloat16)[None]
    for distance in (2, 4, 1):
        total = jnp.concatenate([total, across(total, "turb", distance)])
    both = [total, across(total, "sample", 2)]
    return both + [across(part, "sample", 1) for part in both], gain.reshape(width)


def place_kernel(*refs):
    (*parts, query_ref, key_ref, value_ref, out_ref, all_ref) = refs
    own_sample, own_turb = lax.axis_index("sample"), lax.axis_index("turb")
    turbs, quads, share, quad = parts[0].shape
    for i, ref in enumerate(parts):
        product = own_sample ^ ((i % 2) * 2 + i // 2)
        for apart in range(turbs):
            rows = pl.ds(pl.multiple_of((apart ^ own_turb) * share, share), share)
            for j in range(quads):
                all_ref[product, rows, j * quad : (j + 1) * quad] = ref[
                    turb_place(apart), j
                ].astype(jnp.float32)
    for i, ref in enumerate((query_ref, key_ref, value_ref, out_ref)):
        ref[...] = all_ref[i]


def place_sums(parts, width):
    return pl.pallas_call(
        place_kernel,
        in_specs=[pl.BlockSpec(memory_space=pltpu.VMEM)] * len(parts),
        out_specs=[pl.BlockSpec(memory_space=pltpu.VMEM)] * 4,
        out_shape=[jax.ShapeDtypeStruct((width, width), jnp.float32)] * 4,
        scratch_shapes=[pltpu.VMEM((4, width, width), jnp.float32)],
        compiler_params=pltpu.CompilerParams(vmem_limit_bytes=VMEM_LIMIT),
        cost_estimate=pl.CostEstimate(
            flops=0, bytes_accessed=24 * width * width, transcendentals=0
        ),
        name="place",
    )(*parts)


def by_sample(
    inflow,
    cotangent,
    norm_gain,
    query_weight,
    key_weight,
    value_weight,
    out_weight,
    adjacency,
    sectors,
):
    sample_count, block_rows, width = inflow.shape
    row_count = lax.axis_size("turb") * block_rows
    rows = swap(inflow, "turb")
    rows, cotangent = lax.optimization_barrier((rows, cotangent))
    rows = rows.reshape(row_count, width)
    grad_rows = swap(cotangent, "turb").reshape(row_count, width)
    *saved, layer_rows = forward(
        sectors, adjacency, rows, norm_gain, query_weight, key_weight, value_weight, out_weight,
        block_rows,
    )
    layer_output = swap(layer_rows.reshape(inflow.shape), "turb")
    *grads, keep, send = backward(
        sectors, adjacency, grad_rows, out_weight, *saved, block_rows, 0
    )
    early = (keep, across(send, "sample", 2))
    grad_rows, keep, send = backward(
        sectors, adjacency, grad_rows, out_weight, *saved, block_rows, 1,
        rows, norm_gain.reshape(1, width), query_weight, key_weight, value_weight, *grads,
    )
    late = (keep, across(send, "sample", 1))
    grad_inflow = swap(grad_rows.reshape(inflow.shape), "turb")
    parts, sum_gain = reduce_sums(early, late, width)
    sums = place_sums(parts, width)
    return (layer_output, grad_inflow, *sums, sum_gain)


def solution(mesh):
    placed = (
        P("sample", "turb", None),
        P("sample", "turb", None),
        P(),
        P(),
        P(),
        P(),
        P(),
        P(),
        P("sample"),
    )

    def plan(*args):
        sample_count = args[0].shape[0]
        if sample_count == mesh.shape["turb"] == TURBS and mesh.shape["sample"] == SAMPLES:
            return by_sample(*args)
        return on_device(*args)

    return jax.shard_map(
        plan,
        mesh=mesh,
        in_specs=placed,
        out_specs=(P("sample", "turb", None), P("sample", "turb", None), P(), P(), P(), P(), P()),
        check_vma=False,
    )
```

```python
import jax
import jax.numpy as jnp
from jax import lax
from jax.experimental import pallas as pl
from jax.experimental.pallas import tpu as pltpu
from jax.sharding import PartitionSpec as P

HEADS = 8
UPSTREAM = 3
SECTORS = 8
REPEAT = 1


epsilon = 1e-05


def normalize(row_block, norm_gain):
    widened = row_block.astype(jnp.float32)
    centred = widened - jnp.mean(widened, axis=-1, keepdims=True)
    inverse = lax.rsqrt(jnp.mean(centred * centred, axis=-1, keepdims=True) + epsilon)
    scaled = centred * inverse
    return (scaled, inverse, (scaled * norm_gain).astype(jnp.bfloat16))


def attend(pieces):
    queries, key_rows, value_rows, key_usable, grad_attended = pieces
    batch_count, query_count, model_width = queries.shape
    key_count = key_rows.shape[1]
    head_dim = model_width // HEADS
    score_scale = head_dim ** (-0.5)
    query_heads = queries.reshape(batch_count, query_count, HEADS, head_dim)
    key_heads = key_rows.reshape(batch_count, key_count, HEADS, head_dim)
    value_heads = value_rows.reshape(batch_count, key_count, HEADS, head_dim)
    grad_heads = grad_attended.reshape(batch_count, query_count, HEADS, head_dim)
    scores = (
        jnp.einsum("nqhd,nkhd->nhqk", query_heads, key_heads, preferred_element_type=jnp.float32)
        * score_scale
    )
    scores = jnp.where(key_usable[:, None, None, :], scores, -1e30)
    highest = jnp.max(scores, axis=-1, keepdims=True)
    weights = jnp.exp(scores - highest)
    probabilities = weights / jnp.sum(weights, axis=-1, keepdims=True)
    rounded = probabilities.astype(jnp.bfloat16)
    attended = jnp.einsum(
        "nhqk,nkhd->nqhd", rounded, value_heads, preferred_element_type=jnp.float32
    ).astype(jnp.bfloat16)
    grad_probs = jnp.einsum(
        "nqhd,nkhd->nhqk", grad_heads, value_heads, preferred_element_type=jnp.float32
    )
    centred = grad_probs - jnp.sum(probabilities * grad_probs, axis=-1, keepdims=True)
    grad_scores = (probabilities * centred * score_scale).astype(jnp.bfloat16)
    grad_queries = jnp.einsum(
        "nhqk,nkhd->nqhd", grad_scores, key_heads, preferred_element_type=jnp.float32
    ).astype(jnp.bfloat16)
    grad_keys = jnp.einsum(
        "nhqk,nqhd->nkhd", grad_scores, query_heads, preferred_element_type=jnp.float32
    )
    grad_values = jnp.einsum(
        "nhqk,nqhd->nkhd", rounded, grad_heads, preferred_element_type=jnp.float32
    )
    pair_terms = jnp.concatenate(
        [
            grad_keys.reshape(batch_count, key_count, model_width),
            grad_values.reshape(batch_count, key_count, model_width),
        ],
        axis=-1,
    )
    return (
        attended.reshape(batch_count, query_count, model_width),
        grad_queries.reshape(batch_count, query_count, model_width),
        pair_terms,
    )


def on_device(
    inflow,
    cotangent,
    norm_gain,
    query_weight,
    key_weight,
    value_weight,
    out_weight,
    adjacency,
    sectors,
):
    sample_count, block_rows, model_width = inflow.shape
    block_count = lax.axis_size("turb")
    own_block = lax.axis_index("turb")
    slot_count = REPEAT * ((SECTORS * UPSTREAM + block_count - 2) // (block_count - 1))
    flat_rows = sample_count * block_rows
    pair_width = 2 * model_width
    input_rows = inflow.reshape(flat_rows, model_width)
    grad_rows = cotangent.reshape(flat_rows, model_width)
    scaled, inverse, normed = normalize(input_rows, norm_gain)
    queries = jnp.dot(normed, query_weight, preferred_element_type=jnp.float32).astype(jnp.bfloat16)
    key_rows = jnp.dot(normed, key_weight, preferred_element_type=jnp.float32).astype(jnp.bfloat16)
    value_rows = jnp.dot(normed, value_weight, preferred_element_type=jnp.float32).astype(
        jnp.bfloat16
    )
    upstream = adjacency[sectors]
    needed = jnp.any(upstream == own_block, axis=2).astype(jnp.int32)
    earlier_need = jnp.cumsum(needed, axis=0) - needed
    slot_index = lax.broadcasted_iota(jnp.int32, (block_count, slot_count, sample_count), 1)
    chosen = (needed.T[:, None, :] == 1) & (earlier_need.T[:, None, :] == slot_index)
    selector = chosen.astype(jnp.bfloat16).reshape(block_count * slot_count, sample_count)
    own_lists = lax.dynamic_index_in_dim(upstream, own_block, axis=1, keepdims=False)
    usable = own_lists >= 0
    matches = jnp.any(own_lists[:, :, None, None] == own_lists[None, None, :, :], axis=3)
    sample_ids = lax.broadcasted_iota(jnp.int32, (sample_count, sample_count), 0)
    earlier = lax.broadcasted_iota(jnp.int32, (sample_count, sample_count), 1) < sample_ids
    position = jnp.sum((matches & earlier[:, None, :]).astype(jnp.int32), axis=2)
    flat_slot = own_lists * slot_count + position
    fetch_at = jnp.where(usable, flat_slot, 0)
    payload = jnp.concatenate([key_rows, value_rows], axis=1).reshape(
        sample_count, block_rows * pair_width
    )
    packed = jnp.dot(selector, payload, preferred_element_type=jnp.float32).astype(jnp.bfloat16)
    arrived = lax.all_to_all(
        packed.reshape(block_count, slot_count, block_rows, pair_width),
        "turb",
        split_axis=0,
        concat_axis=0,
        tiled=True,
    )
    fetched = arrived.reshape(block_count * slot_count, block_rows, pair_width)[fetch_at]
    upstream_keys = fetched[..., :model_width]
    upstream_values = fetched[..., model_width:]
    key_count = (1 + UPSTREAM) * block_rows
    key_all = jnp.concatenate(
        [key_rows.reshape(sample_count, 1, block_rows, model_width), upstream_keys], axis=1
    ).reshape(sample_count, key_count, model_width)
    value_all = jnp.concatenate(
        [value_rows.reshape(sample_count, 1, block_rows, model_width), upstream_values], axis=1
    ).reshape(sample_count, key_count, model_width)
    block_usable = jnp.concatenate([jnp.ones((sample_count, 1), dtype=jnp.bool_), usable], axis=1)
    key_usable = jnp.repeat(block_usable, block_rows, axis=1)
    grad_attended = jnp.dot(grad_rows, out_weight.T, preferred_element_type=jnp.float32).astype(
        jnp.bfloat16
    )
    group_size = min(sample_count, max(1, 512 // block_rows))
    while sample_count % group_size != 0:
        group_size = group_size - 1
    group_count = sample_count // group_size

    def grouped(tensor):
        return tensor.reshape((group_count, group_size) + tensor.shape[1:])

    attended, grad_queries, pair_terms = lax.map(
        attend,
        (
            grouped(queries.reshape(sample_count, block_rows, model_width)),
            grouped(key_all),
            grouped(value_all),
            grouped(key_usable),
            grouped(grad_attended.reshape(sample_count, block_rows, model_width)),
        ),
    )
    attended = attended.reshape(flat_rows, model_width)
    grad_queries = grad_queries.reshape(flat_rows, model_width)
    pair_terms = pair_terms.reshape(sample_count, 1 + UPSTREAM, block_rows, pair_width)
    layer_output = (
        (
            input_rows.astype(jnp.float32)
            + jnp.dot(attended, out_weight, preferred_element_type=jnp.float32)
        )
        .astype(jnp.bfloat16)
        .reshape(inflow.shape)
    )
    outgoing = (
        pair_terms[:, 1:]
        .astype(jnp.bfloat16)
        .reshape(sample_count * UPSTREAM, block_rows, pair_width)
    )
    target = jnp.where(usable, flat_slot, block_count * slot_count).reshape(-1)
    outbound = (
        jnp.zeros((block_count * slot_count, block_rows, pair_width), jnp.bfloat16)
        .at[target]
        .set(outgoing, mode="drop")
    )
    sum_out = jnp.dot(attended.T, grad_rows, preferred_element_type=jnp.float32)
    sum_query = jnp.dot(normed.T, grad_queries, preferred_element_type=jnp.float32)
    returned = lax.all_to_all(
        outbound.reshape(block_count, slot_count, block_rows, pair_width),
        "turb",
        split_axis=0,
        concat_axis=0,
        tiled=True,
    )
    remote = jnp.dot(
        selector.T,
        returned.reshape(block_count * slot_count, block_rows * pair_width),
        preferred_element_type=jnp.float32,
    )
    combined = (
        (pair_terms[:, 0].reshape(sample_count, block_rows * pair_width) + remote)
        .astype(jnp.bfloat16)
        .reshape(flat_rows, pair_width)
    )
    grad_keys = combined[:, :model_width]
    grad_values = combined[:, model_width:]
    sum_key = jnp.dot(normed.T, grad_keys, preferred_element_type=jnp.float32)
    sum_value = jnp.dot(normed.T, grad_values, preferred_element_type=jnp.float32)
    grad_normed = jnp.dot(grad_queries, query_weight.T, preferred_element_type=jnp.float32)
    grad_normed = grad_normed + jnp.dot(grad_keys, key_weight.T, preferred_element_type=jnp.float32)
    grad_normed = grad_normed + jnp.dot(
        grad_values, value_weight.T, preferred_element_type=jnp.float32
    )
    sum_gain = jnp.sum(grad_normed * scaled, axis=0)
    grad_scaled = grad_normed * norm_gain
    grad_input = inverse * (
        grad_scaled
        - jnp.mean(grad_scaled, axis=-1, keepdims=True)
        - scaled * jnp.mean(grad_scaled * scaled, axis=-1, keepdims=True)
    )
    grad_inflow = (
        (grad_rows.astype(jnp.float32) + grad_input).astype(jnp.bfloat16).reshape(inflow.shape)
    )
    sum_query, sum_key, sum_value, sum_out, sum_gain = lax.psum(
        (sum_query, sum_key, sum_value, sum_out, sum_gain), ("sample", "turb")
    )
    return (layer_output, grad_inflow, sum_query, sum_key, sum_value, sum_out, sum_gain)


PAIR = 2
QUAD = 4
LOG2_E = 1.4426950408889634
VMEM_LIMIT = 58 * 2**20
GAIN_ROWS = 4
SAMPLES = 4
TURBS = 8


def turb_place(apart):
    return (apart % 2) * 4 + (apart // 4) * 2 + (apart // 2) % 2


def contract(left, right, left_dim, right_dim):
    return lax.dot_general(
        left, right, (((left_dim,), (right_dim,)), ((), ())), preferred_element_type=jnp.float32
    )


def split_heads(rows, head_dim):
    lane = lax.broadcasted_iota(jnp.int32, rows.shape, 1)
    wide = rows.astype(jnp.float32)
    return jnp.concatenate(
        [jnp.where(lane < head_dim, wide, 0.0), jnp.where(lane >= head_dim, wide, 0.0)], axis=0
    ).astype(jnp.bfloat16)


def join_heads(wide, head_dim):
    block_rows = wide.shape[1] // PAIR
    first = lax.broadcasted_iota(jnp.int32, (wide.shape[0], block_rows), 0) < head_dim
    return jnp.where(first, wide[:, :block_rows], wide[:, block_rows:])


def for_each_block(sectors_ref, lists_ref, block_count, block_rows, work):
    sector = sectors_ref[lax.axis_index("turb")]

    def step(block, carry):
        used = jnp.int32(0)
        for slot in range(UPSTREAM):
            used = used + (lists_ref[sector, block, slot] >= 0).astype(jnp.int32)
        for count in range(UPSTREAM + 1):

            @pl.when(used == count)
            def _():
                sources = [block] + [
                    lists_ref[sector, block, slot] for slot in range(count)
                ]
                work(block, [pl.multiple_of(s * block_rows, block_rows) for s in sources])

        return carry

    lax.fori_loop(0, block_count, step, 0)


def stacked(ref, starts, block_rows, lanes):
    return jnp.concatenate([ref[pl.ds(s, block_rows), lanes] for s in starts], axis=0)


def beside(ref, starts, block_rows, rows):
    return jnp.concatenate([ref[rows, pl.ds(s, block_rows)] for s in starts], axis=1)


def forward_kernel(block_rows, head_dim, sectors_ref, lists_ref, x_ref, gain_ref, wq_ref, wk_ref,
                   wv_ref, wo_ref, normed_t_ref, q_ref, k_ref, v_ref, kt_ref, att_ref,
                   top_ref, inverse_ref, out_ref, normed_ref, vt_ref, rows_ref, sum_ref):
    row_count = x_ref.shape[0]
    quad = pl.program_id(0)
    pair = PAIR * head_dim
    exponent = head_dim ** (-0.5) * LOG2_E
    chunk = min(row_count, 256)

    @pl.when(quad == 0)
    def _():
        for start in range(0, row_count, chunk):
            part = slice(start, start + chunk)
            scaled, _, normed = normalize(x_ref[part, :], gain_ref[...])
            normed_ref[part, :] = normed
            normed_t_ref[:, part] = (scaled * gain_ref[...]).T.astype(jnp.bfloat16)

    normed = normed_ref[...]
    q_ref[...] = contract(normed, wq_ref[...], 1, 0).astype(jnp.bfloat16)
    k_ref[...] = contract(normed, wk_ref[...], 1, 0).astype(jnp.bfloat16)
    v_ref[...] = contract(normed, wv_ref[...], 1, 0).astype(jnp.bfloat16)
    kt_ref[...] = contract(wk_ref[...], normed, 0, 1).astype(jnp.bfloat16)
    vt_ref[...] = contract(wv_ref[...], normed, 0, 1).astype(jnp.bfloat16)

    def work(block, starts):
        own = pl.ds(starts[0], block_rows)
        lanes = [slice(p * pair, (p + 1) * pair) for p in range(QUAD // PAIR)]
        scores = [
            contract(
                stacked(k_ref, starts, block_rows, lane), split_heads(q_ref[own, lane], head_dim), 1, 1
            )
            for lane in lanes
        ]
        for p, lane in enumerate(lanes):
            highest = jnp.max(scores[p], axis=0, keepdims=True)
            weights = jnp.exp2((scores[p] - highest) * exponent)
            inverse = 1.0 / jnp.sum(weights, axis=0, keepdims=True)
            probs = (weights * inverse).astype(jnp.bfloat16)
            top_ref[0, pl.ds(block * (QUAD // PAIR) + p, 1), :] = highest
            inverse_ref[0, pl.ds(block * (QUAD // PAIR) + p, 1), :] = inverse
            joined = join_heads(
                jnp.dot(
                    beside(vt_ref, starts, block_rows, lane),
                    probs,
                    preferred_element_type=jnp.float32,
                ),
                head_dim,
            )
            att_ref[lane, own] = joined.astype(jnp.bfloat16)
            rows_ref[own, lane] = joined.T.astype(jnp.bfloat16)

    for_each_block(sectors_ref, lists_ref, row_count // block_rows, block_rows, work)
    part = contract(rows_ref[...], wo_ref[...], 1, 0)

    @pl.when(quad == 0)
    def _():
        sum_ref[...] = x_ref[...].astype(jnp.float32) + part

    @pl.when(quad > 0)
    def _():
        sum_ref[...] += part

    @pl.when(quad == pl.num_programs(0) - 1)
    def _():
        out_ref[...] = sum_ref[...].astype(jnp.bfloat16)


def forward(sectors, adjacency, rows, norm_gain, query_weight, key_weight, value_weight, out_weight, block_rows):
    row_count, width = rows.shape
    head_dim = width // HEADS
    quad = QUAD * head_dim
    quads = width // quad
    stat_rows = row_count // block_rows * (QUAD // PAIR)
    fixed = lambda *shape: pl.BlockSpec(shape, lambda p, *lists: (0,) * len(shape))
    across = lambda size: pl.BlockSpec((size, quad), lambda p, *lists: (0, p))
    down = lambda size: pl.BlockSpec((quad, size), lambda p, *lists: (p, 0))
    stat = pl.BlockSpec((1, stat_rows, PAIR * block_rows), lambda p, *lists: (p, 0, 0))
    flat = jax.ShapeDtypeStruct((row_count, width), jnp.bfloat16)
    turned = jax.ShapeDtypeStruct((width, row_count), jnp.bfloat16)
    stats = jax.ShapeDtypeStruct((quads, stat_rows, PAIR * block_rows), jnp.float32)
    return pl.pallas_call(
        lambda *refs: forward_kernel(block_rows, head_dim, *refs),
        grid_spec=pltpu.PrefetchScalarGridSpec(
            num_scalar_prefetch=2,
            grid=(quads,),
            in_specs=[fixed(row_count, width), fixed(1, width)]
            + [across(width)] * 3
            + [down(width)],
            out_specs=[fixed(width, row_count)]
            + [across(row_count)] * 3
            + [down(row_count)] * 2
            + [stat] * 2
            + [fixed(row_count, width)],
            scratch_shapes=[
                pltpu.VMEM((row_count, width), jnp.bfloat16),
                pltpu.VMEM((quad, row_count), jnp.bfloat16),
                pltpu.VMEM((row_count, quad), jnp.bfloat16),
                pltpu.VMEM((row_count, width), jnp.float32),
            ],
        ),
        out_shape=[turned, flat, flat, flat, turned, turned, stats, stats, flat],
        compiler_params=pltpu.CompilerParams(vmem_limit_bytes=VMEM_LIMIT),
        cost_estimate=pl.CostEstimate(
            flops=12 * row_count * width * width + 32 * row_count * block_rows * width,
            bytes_accessed=20 * row_count * width,
            transcendentals=row_count * 4 * block_rows * HEADS,
        ),
        name="forward",
    )(sectors, adjacency, rows, norm_gain.reshape(1, width), query_weight, key_weight, value_weight,
      out_weight)


def backward_kernel(block_rows, head_dim, which, last, sectors_ref, lists_ref, cot_ref, wo_ref,
                    normed_t_ref, q_ref, k_ref, v_ref, kt_ref, att_ref, top_ref, inverse_ref, *refs):
    if last:
        x_ref, gain_ref, wq_ref, wk_ref, wv_ref, *refs = refs
        before, refs = refs[: 3 * which], refs[3 * which :]
        grad_ref, keep_ref, send_ref, gq_ref, gk_ref, gv_ref, ga_ref, gk_acc, gv_acc, sum_ref = refs
    else:
        gq_ref, gk_ref, gv_ref, keep_ref, send_ref, ga_ref, gk_acc, gv_acc = refs
    row_count, width = cot_ref.shape
    block_count = row_count // block_rows
    pair = PAIR * head_dim
    quad = QUAD * head_dim
    scale = head_dim ** (-0.5)
    ga_ref[...] = contract(cot_ref[...], wo_ref[...], 1, 1).astype(jnp.bfloat16)
    gk_acc[...] = jnp.zeros_like(gk_acc)
    gv_acc[...] = jnp.zeros_like(gv_acc)

    def work(block, starts):
        own = pl.ds(starts[0], block_rows)
        lanes = [slice(p * pair, (p + 1) * pair) for p in range(QUAD // PAIR)]
        queries = [split_heads(q_ref[own, lane], head_dim) for lane in lanes]
        grads = [split_heads(ga_ref[own, lane], head_dim) for lane in lanes]
        scores = [
            contract(stacked(k_ref, starts, block_rows, lane), queries[p], 1, 1)
            for p, lane in enumerate(lanes)
        ]
        grad_probs = [
            contract(stacked(v_ref, starts, block_rows, lane), grads[p] * scale, 1, 1)
            for p, lane in enumerate(lanes)
        ]
        for p, lane in enumerate(lanes):
            stat = pl.ds(block * (QUAD // PAIR) + p, 1)
            probs = jnp.exp2((scores[p] - top_ref[0, stat, :]) * (scale * LOG2_E))
            probs = probs * inverse_ref[0, stat, :]
            total = jnp.sum(probs * grad_probs[p], axis=0, keepdims=True)
            grad_scores = (probs * (grad_probs[p] - total)).astype(jnp.bfloat16)
            probs_b = probs.astype(jnp.bfloat16)
            grad_values = jnp.dot(probs_b, grads[p], preferred_element_type=jnp.float32)
            grad_keys = jnp.dot(grad_scores, queries[p], preferred_element_type=jnp.float32)
            joined = join_heads(
                jnp.dot(
                    beside(kt_ref, starts, block_rows, lane),
                    grad_scores,
                    preferred_element_type=jnp.float32,
                ),
                head_dim,
            )
            gq_ref[own, lane] = joined.T.astype(jnp.bfloat16)
            for slot, start in enumerate(starts):
                rows = pl.ds(start, block_rows)
                part = slice(slot * block_rows, (slot + 1) * block_rows)
                for acc, terms in ((gk_acc, grad_keys), (gv_acc, grad_values)):
                    term = terms[part]
                    if slot > 0:
                        term = term.astype(jnp.bfloat16).astype(jnp.float32)
                    acc[rows, lane] += term

    for_each_block(sectors_ref, lists_ref, block_count, block_rows, work)
    gk_ref[...] = gk_acc[...].astype(jnp.bfloat16)
    gv_ref[...] = gv_acc[...].astype(jnp.bfloat16)
    products = [(normed_t_ref, ref, slice(None)) for ref in (gq_ref, gk_ref, gv_ref)]
    products.append((att_ref, cot_ref, slice(which * quad, (which + 1) * quad)))
    own_sample, own_turb = lax.axis_index("sample"), lax.axis_index("turb")
    share = width // TURBS
    for i, (left, right, lanes) in enumerate(products):
        terms = contract(left[...], right[:, lanes], 1, 0)
        apart = i ^ own_sample
        first, second = (apart % 2, apart // 2) if last else (apart // 2, apart % 2)

        def store(ref):
            for turb in range(TURBS):
                start = pl.multiple_of(second * width + turb_place(turb ^ own_turb) * share, share)
                ref[pl.ds(start, share), :] = terms[turb * share : (turb + 1) * share].astype(
                    ref.dtype
                )

        @pl.when(first == 0)
        def _():
            store(keep_ref)

        @pl.when(first == 1)
        def _():
            store(send_ref)

    if not last:
        return
    chunk = min(row_count, 256)
    sum_ref[...] = jnp.zeros_like(sum_ref)
    for start in range(0, row_count, chunk):
        rows = slice(start, start + chunk)
        scaled, inverse, _ = normalize(x_ref[rows, :], gain_ref[...])
        grad_normed = jnp.zeros((chunk, width), jnp.float32)
        for i in range(width // quad):
            parts = before[3 * i : 3 * i + 3] if i < which else (gq_ref, gk_ref, gv_ref)
            for ref, weight_ref in zip(parts, (wq_ref, wk_ref, wv_ref)):
                grad_normed += contract(
                    ref[rows, :], weight_ref[:, i * quad : (i + 1) * quad], 1, 1
                )
        sum_ref[...] += jnp.sum(grad_normed * scaled, axis=0, keepdims=True)
        grad_scaled = grad_normed * gain_ref[...]
        grad_input = inverse * (
            grad_scaled
            - jnp.mean(grad_scaled, axis=-1, keepdims=True)
            - scaled * jnp.mean(grad_scaled * scaled, axis=-1, keepdims=True)
        )
        grad_ref[rows, :] = (cot_ref[rows, :].astype(jnp.float32) + grad_input).astype(jnp.bfloat16)
    for ref in (keep_ref, send_ref):
        for i in range(width // quad):
            start = 2 * width + i * GAIN_ROWS
            ref[start : start + GAIN_ROWS, :] = jnp.broadcast_to(
                sum_ref[:, i * quad : (i + 1) * quad], (GAIN_ROWS, quad)
            )


def backward(sectors, adjacency, cotangent, out_weight, normed_t, queries, keys, values, keys_t,
             attended_t, tops, inverses, block_rows, which, *ending):
    row_count, width = cotangent.shape
    block_count = row_count // block_rows
    head_dim = width // HEADS
    quad = QUAD * head_dim
    fixed = lambda *shape: pl.BlockSpec(shape, lambda i, *lists: (0,) * len(shape))
    across = pl.BlockSpec((row_count, quad), lambda i, *lists: (0, which))
    down = lambda size: pl.BlockSpec((quad, size), lambda i, *lists: (which, 0))
    stat = pl.BlockSpec((1,) + tops.shape[1:], lambda i, *lists: (which, 0, 0))
    part = jax.ShapeDtypeStruct((row_count, quad), jnp.bfloat16)
    gain_rows = GAIN_ROWS * (width // quad)
    scratch = [
        pltpu.VMEM((row_count, quad), jnp.bfloat16),
        pltpu.VMEM((row_count, quad), jnp.float32),
        pltpu.VMEM((row_count, quad), jnp.float32),
    ]
    if ending:
        out_shape = [jax.ShapeDtypeStruct((row_count, width), jnp.bfloat16)]
        out_shape += [jax.ShapeDtypeStruct((2 * width + gain_rows, quad), jnp.float32)] * 2
        scratch = [pltpu.VMEM((row_count, quad), jnp.bfloat16)] * 3 + scratch
        scratch.append(pltpu.VMEM((1, width), jnp.float32))
    else:
        out_shape = [part] * 3 + [
            jax.ShapeDtypeStruct((2 * width, quad), dtype) for dtype in (jnp.float32, jnp.bfloat16)
        ]
    return pl.pallas_call(
        lambda *refs: backward_kernel(block_rows, head_dim, which, bool(ending), *refs),
        grid_spec=pltpu.PrefetchScalarGridSpec(
            num_scalar_prefetch=2,
            grid=(1,),
            in_specs=[fixed(row_count, width), down(width), fixed(width, row_count)]
            + [across] * 3
            + [down(row_count), fixed(width, row_count)]
            + [stat] * 2
            + [fixed(*array.shape) for array in ending],
            out_specs=[fixed(*struct.shape) for struct in out_shape],
            scratch_shapes=scratch,
        ),
        out_shape=out_shape,
        compiler_params=pltpu.CompilerParams(vmem_limit_bytes=VMEM_LIMIT),
        cost_estimate=pl.CostEstimate(
            flops=10 * row_count * width * quad
            + 80 * row_count * block_rows * quad
            + 6 * row_count * width * width * bool(ending),
            bytes_accessed=14 * row_count * width,
            transcendentals=row_count * 4 * block_rows * QUAD,
        ),
        name="backward",
    )(sectors, adjacency, cotangent, out_weight, normed_t, queries, keys, values, keys_t, attended_t,
      tops, inverses, *ending)


def swap(tensor, axis):
    return lax.all_to_all(tensor, axis, split_axis=0, concat_axis=0, tiled=True)


def across(tensor, axis, distance):
    size = lax.axis_size(axis)
    return lax.ppermute(tensor, axis, [(i, i ^ distance) for i in range(size)])


def across(tensor, axis, distance):
    size = lax.axis_size(axis)
    return lax.ppermute(tensor, axis, [(i, i ^ distance) for i in range(size)])


def reduce_sums(early, late, width, beside):
    quad = early[0].shape[1]
    wide = jnp.float32

    def pack(gain):
        high = gain.astype(jnp.bfloat16)
        low = (gain - high.astype(wide)).astype(jnp.bfloat16)
        return jnp.concatenate([high, low, jnp.zeros((16 - 2 * gain.shape[0], quad), jnp.bfloat16)])

    def unpack(rows, count):
        return rows[:count].astype(wide) + rows[count : 2 * count].astype(wide)

    keep, arrived = early
    first = keep + arrived.astype(wide)
    first = first[:width] + across(first[width:], "sample", 1)
    keep, arrived = late
    second = keep + arrived
    gain = second[2 * width :: GAIN_ROWS]
    count = gain.shape[0]
    arrived = across(
        jnp.concatenate([second[width : 2 * width].astype(jnp.bfloat16), pack(gain)]), "sample", 2
    )
    second = second[:width] + arrived[:width].astype(wide)
    gain = gain + unpack(arrived[width:], count)
    for distance in (1, 4, 2):
        half = first.shape[0] // 2
        halves = [part[half:].astype(jnp.bfloat16) for part in (first, second)]
        arrived = across(jnp.concatenate(halves + [pack(gain)]), "turb", distance)
        first = first[:half] + arrived[:half].astype(wide)
        second = second[:half] + arrived[half : 2 * half].astype(wide)
        gain = gain + unpack(arrived[2 * half :], count)
    total = jnp.stack([first, second]).astype(jnp.bfloat16)[None]
    total, beside = lax.optimization_barrier((total, beside))
    for distance in (2, 4, 1):
        total = jnp.concatenate([total, across(total, "turb", distance)])
    both = [total, across(total, "sample", 2)]
    both += [across(part, "sample", 1) for part in both]
    return both, gain.reshape(width), beside


def place_kernel(from_ref, from_grad_ref, *refs):
    (*parts, to_ref, to_grad_ref, query_ref, key_ref, value_ref, out_ref, all_ref, sems) = refs
    copies = [
        pltpu.make_async_copy(from_ref, to_ref, sems.at[0]),
        pltpu.make_async_copy(from_grad_ref, to_grad_ref, sems.at[1]),
    ]
    for copy in copies:
        copy.start()
    own_sample, own_turb = lax.axis_index("sample"), lax.axis_index("turb")
    turbs, quads, share, quad = parts[0].shape
    for i, ref in enumerate(parts):
        product = own_sample ^ ((i % 2) * 2 + i // 2)
        for apart in range(turbs):
            rows = pl.ds(pl.multiple_of((apart ^ own_turb) * share, share), share)
            for j in range(quads):
                all_ref[product, rows, j * quad : (j + 1) * quad] = ref[
                    turb_place(apart), j
                ].astype(jnp.float32)
    for i, ref in enumerate((query_ref, key_ref, value_ref, out_ref)):
        ref[...] = all_ref[i]
    for copy in copies:
        copy.wait()


def place_sums(rows, parts, width):
    return pl.pallas_call(
        place_kernel,
        in_specs=[pl.BlockSpec(memory_space=pl.ANY)] * 2
        + [pl.BlockSpec(memory_space=pltpu.VMEM)] * len(parts),
        out_specs=[pl.BlockSpec(memory_space=pl.ANY)] * 2
        + [pl.BlockSpec(memory_space=pltpu.VMEM)] * 4,
        out_shape=[jax.ShapeDtypeStruct(array.shape, array.dtype) for array in rows]
        + [jax.ShapeDtypeStruct((width, width), jnp.float32)] * 4,
        scratch_shapes=[
            pltpu.VMEM((4, width, width), jnp.float32),
            pltpu.SemaphoreType.DMA((2,)),
        ],
        compiler_params=pltpu.CompilerParams(vmem_limit_bytes=VMEM_LIMIT),
        cost_estimate=pl.CostEstimate(
            flops=0, bytes_accessed=24 * width * width, transcendentals=0
        ),
        name="place",
    )(*rows, *parts)


def by_sample(
    inflow,
    cotangent,
    norm_gain,
    query_weight,
    key_weight,
    value_weight,
    out_weight,
    adjacency,
    sectors,
):
    sample_count, block_rows, width = inflow.shape
    row_count = lax.axis_size("turb") * block_rows
    rows = swap(inflow, "turb")
    rows, cotangent = lax.optimization_barrier((rows, cotangent))
    rows = rows.reshape(row_count, width)
    grad_rows = swap(cotangent, "turb").reshape(row_count, width)
    *saved, layer_rows = forward(
        sectors, adjacency, rows, norm_gain, query_weight, key_weight, value_weight, out_weight,
        block_rows,
    )
    layer_output = swap(layer_rows.reshape(inflow.shape), "turb")
    *grads, keep, send = backward(
        sectors, adjacency, grad_rows, out_weight, *saved, block_rows, 0
    )
    early = across(send, "sample", 2)
    *late, grad_rows = backward(
        sectors, adjacency, grad_rows, out_weight, *saved, block_rows, 1,
        rows, norm_gain.reshape(1, width), query_weight, key_weight, value_weight, *grads,
    )[::-1]
    late, grad_rows, early, layer_output = lax.optimization_barrier(
        (late, grad_rows, early, layer_output)
    )
    send, second = late
    late = (second, across(send, "sample", 1))
    grad_inflow = swap(grad_rows.reshape(inflow.shape), "turb")
    parts, sum_gain, grad_inflow = reduce_sums((keep, early), late, width, grad_inflow)
    layer_output, grad_inflow, *sums = place_sums((layer_output, grad_inflow), parts, width)
    return (layer_output, grad_inflow, *sums, sum_gain)


def solution(mesh):
    placed = (
        P("sample", "turb", None),
        P("sample", "turb", None),
        P(),
        P(),
        P(),
        P(),
        P(),
        P(),
        P("sample"),
    )

    def plan(*args):
        sample_count = args[0].shape[0]
        if sample_count == mesh.shape["turb"] == TURBS and mesh.shape["sample"] == SAMPLES:
            return by_sample(*args)
        return on_device(*args)

    return jax.shard_map(
        plan,
        mesh=mesh,
        in_specs=placed,
        out_specs=(P("sample", "turb", None), P("sample", "turb", None), P(), P(), P(), P(), P()),
        check_vma=False,
    )
```

```python
import jax
import jax.numpy as jnp
from jax import lax
from jax.experimental import pallas as pl
from jax.experimental.pallas import tpu as pltpu
from jax.sharding import PartitionSpec as P

HEADS = 8
UPSTREAM = 3
SECTORS = 8
REPEAT = 1


epsilon = 1e-05


def normalize(row_block, norm_gain):
    widened = row_block.astype(jnp.float32)
    centred = widened - jnp.mean(widened, axis=-1, keepdims=True)
    inverse = lax.rsqrt(jnp.mean(centred * centred, axis=-1, keepdims=True) + epsilon)
    scaled = centred * inverse
    return (scaled, inverse, (scaled * norm_gain).astype(jnp.bfloat16))


def attend(pieces):
    queries, key_rows, value_rows, key_usable, grad_attended = pieces
    batch_count, query_count, model_width = queries.shape
    key_count = key_rows.shape[1]
    head_dim = model_width // HEADS
    score_scale = head_dim ** (-0.5)
    query_heads = queries.reshape(batch_count, query_count, HEADS, head_dim)
    key_heads = key_rows.reshape(batch_count, key_count, HEADS, head_dim)
    value_heads = value_rows.reshape(batch_count, key_count, HEADS, head_dim)
    grad_heads = grad_attended.reshape(batch_count, query_count, HEADS, head_dim)
    scores = (
        jnp.einsum("nqhd,nkhd->nhqk", query_heads, key_heads, preferred_element_type=jnp.float32)
        * score_scale
    )
    scores = jnp.where(key_usable[:, None, None, :], scores, -1e30)
    highest = jnp.max(scores, axis=-1, keepdims=True)
    weights = jnp.exp(scores - highest)
    probabilities = weights / jnp.sum(weights, axis=-1, keepdims=True)
    rounded = probabilities.astype(jnp.bfloat16)
    attended = jnp.einsum(
        "nhqk,nkhd->nqhd", rounded, value_heads, preferred_element_type=jnp.float32
    ).astype(jnp.bfloat16)
    grad_probs = jnp.einsum(
        "nqhd,nkhd->nhqk", grad_heads, value_heads, preferred_element_type=jnp.float32
    )
    centred = grad_probs - jnp.sum(probabilities * grad_probs, axis=-1, keepdims=True)
    grad_scores = (probabilities * centred * score_scale).astype(jnp.bfloat16)
    grad_queries = jnp.einsum(
        "nhqk,nkhd->nqhd", grad_scores, key_heads, preferred_element_type=jnp.float32
    ).astype(jnp.bfloat16)
    grad_keys = jnp.einsum(
        "nhqk,nqhd->nkhd", grad_scores, query_heads, preferred_element_type=jnp.float32
    )
    grad_values = jnp.einsum(
        "nhqk,nqhd->nkhd", rounded, grad_heads, preferred_element_type=jnp.float32
    )
    pair_terms = jnp.concatenate(
        [
            grad_keys.reshape(batch_count, key_count, model_width),
            grad_values.reshape(batch_count, key_count, model_width),
        ],
        axis=-1,
    )
    return (
        attended.reshape(batch_count, query_count, model_width),
        grad_queries.reshape(batch_count, query_count, model_width),
        pair_terms,
    )


def on_device(
    inflow,
    cotangent,
    norm_gain,
    query_weight,
    key_weight,
    value_weight,
    out_weight,
    adjacency,
    sectors,
):
    sample_count, block_rows, model_width = inflow.shape
    block_count = lax.axis_size("turb")
    own_block = lax.axis_index("turb")
    slot_count = REPEAT * ((SECTORS * UPSTREAM + block_count - 2) // (block_count - 1))
    flat_rows = sample_count * block_rows
    pair_width = 2 * model_width
    input_rows = inflow.reshape(flat_rows, model_width)
    grad_rows = cotangent.reshape(flat_rows, model_width)
    scaled, inverse, normed = normalize(input_rows, norm_gain)
    queries = jnp.dot(normed, query_weight, preferred_element_type=jnp.float32).astype(jnp.bfloat16)
    key_rows = jnp.dot(normed, key_weight, preferred_element_type=jnp.float32).astype(jnp.bfloat16)
    value_rows = jnp.dot(normed, value_weight, preferred_element_type=jnp.float32).astype(
        jnp.bfloat16
    )
    upstream = adjacency[sectors]
    needed = jnp.any(upstream == own_block, axis=2).astype(jnp.int32)
    earlier_need = jnp.cumsum(needed, axis=0) - needed
    slot_index = lax.broadcasted_iota(jnp.int32, (block_count, slot_count, sample_count), 1)
    chosen = (needed.T[:, None, :] == 1) & (earlier_need.T[:, None, :] == slot_index)
    selector = chosen.astype(jnp.bfloat16).reshape(block_count * slot_count, sample_count)
    own_lists = lax.dynamic_index_in_dim(upstream, own_block, axis=1, keepdims=False)
    usable = own_lists >= 0
    matches = jnp.any(own_lists[:, :, None, None] == own_lists[None, None, :, :], axis=3)
    sample_ids = lax.broadcasted_iota(jnp.int32, (sample_count, sample_count), 0)
    earlier = lax.broadcasted_iota(jnp.int32, (sample_count, sample_count), 1) < sample_ids
    position = jnp.sum((matches & earlier[:, None, :]).astype(jnp.int32), axis=2)
    flat_slot = own_lists * slot_count + position
    fetch_at = jnp.where(usable, flat_slot, 0)
    payload = jnp.concatenate([key_rows, value_rows], axis=1).reshape(
        sample_count, block_rows * pair_width
    )
    packed = jnp.dot(selector, payload, preferred_element_type=jnp.float32).astype(jnp.bfloat16)
    arrived = lax.all_to_all(
        packed.reshape(block_count, slot_count, block_rows, pair_width),
        "turb",
        split_axis=0,
        concat_axis=0,
        tiled=True,
    )
    fetched = arrived.reshape(block_count * slot_count, block_rows, pair_width)[fetch_at]
    upstream_keys = fetched[..., :model_width]
    upstream_values = fetched[..., model_width:]
    key_count = (1 + UPSTREAM) * block_rows
    key_all = jnp.concatenate(
        [key_rows.reshape(sample_count, 1, block_rows, model_width), upstream_keys], axis=1
    ).reshape(sample_count, key_count, model_width)
    value_all = jnp.concatenate(
        [value_rows.reshape(sample_count, 1, block_rows, model_width), upstream_values], axis=1
    ).reshape(sample_count, key_count, model_width)
    block_usable = jnp.concatenate([jnp.ones((sample_count, 1), dtype=jnp.bool_), usable], axis=1)
    key_usable = jnp.repeat(block_usable, block_rows, axis=1)
    grad_attended = jnp.dot(grad_rows, out_weight.T, preferred_element_type=jnp.float32).astype(
        jnp.bfloat16
    )
    group_size = min(sample_count, max(1, 512 // block_rows))
    while sample_count % group_size != 0:
        group_size = group_size - 1
    group_count = sample_count // group_size

    def grouped(tensor):
        return tensor.reshape((group_count, group_size) + tensor.shape[1:])

    attended, grad_queries, pair_terms = lax.map(
        attend,
        (
            grouped(queries.reshape(sample_count, block_rows, model_width)),
            grouped(key_all),
            grouped(value_all),
            grouped(key_usable),
            grouped(grad_attended.reshape(sample_count, block_rows, model_width)),
        ),
    )
    attended = attended.reshape(flat_rows, model_width)
    grad_queries = grad_queries.reshape(flat_rows, model_width)
    pair_terms = pair_terms.reshape(sample_count, 1 + UPSTREAM, block_rows, pair_width)
    layer_output = (
        (
            input_rows.astype(jnp.float32)
            + jnp.dot(attended, out_weight, preferred_element_type=jnp.float32)
        )
        .astype(jnp.bfloat16)
        .reshape(inflow.shape)
    )
    outgoing = (
        pair_terms[:, 1:]
        .astype(jnp.bfloat16)
        .reshape(sample_count * UPSTREAM, block_rows, pair_width)
    )
    target = jnp.where(usable, flat_slot, block_count * slot_count).reshape(-1)
    outbound = (
        jnp.zeros((block_count * slot_count, block_rows, pair_width), jnp.bfloat16)
        .at[target]
        .set(outgoing, mode="drop")
    )
    sum_out = jnp.dot(attended.T, grad_rows, preferred_element_type=jnp.float32)
    sum_query = jnp.dot(normed.T, grad_queries, preferred_element_type=jnp.float32)
    returned = lax.all_to_all(
        outbound.reshape(block_count, slot_count, block_rows, pair_width),
        "turb",
        split_axis=0,
        concat_axis=0,
        tiled=True,
    )
    remote = jnp.dot(
        selector.T,
        returned.reshape(block_count * slot_count, block_rows * pair_width),
        preferred_element_type=jnp.float32,
    )
    combined = (
        (pair_terms[:, 0].reshape(sample_count, block_rows * pair_width) + remote)
        .astype(jnp.bfloat16)
        .reshape(flat_rows, pair_width)
    )
    grad_keys = combined[:, :model_width]
    grad_values = combined[:, model_width:]
    sum_key = jnp.dot(normed.T, grad_keys, preferred_element_type=jnp.float32)
    sum_value = jnp.dot(normed.T, grad_values, preferred_element_type=jnp.float32)
    grad_normed = jnp.dot(grad_queries, query_weight.T, preferred_element_type=jnp.float32)
    grad_normed = grad_normed + jnp.dot(grad_keys, key_weight.T, preferred_element_type=jnp.float32)
    grad_normed = grad_normed + jnp.dot(
        grad_values, value_weight.T, preferred_element_type=jnp.float32
    )
    sum_gain = jnp.sum(grad_normed * scaled, axis=0)
    grad_scaled = grad_normed * norm_gain
    grad_input = inverse * (
        grad_scaled
        - jnp.mean(grad_scaled, axis=-1, keepdims=True)
        - scaled * jnp.mean(grad_scaled * scaled, axis=-1, keepdims=True)
    )
    grad_inflow = (
        (grad_rows.astype(jnp.float32) + grad_input).astype(jnp.bfloat16).reshape(inflow.shape)
    )
    sum_query, sum_key, sum_value, sum_out, sum_gain = lax.psum(
        (sum_query, sum_key, sum_value, sum_out, sum_gain), ("sample", "turb")
    )
    return (layer_output, grad_inflow, sum_query, sum_key, sum_value, sum_out, sum_gain)


PAIR = 2
QUAD = 4
LOG2_E = 1.4426950408889634
VMEM_LIMIT = 58 * 2**20
SUM_ROWS = 8
SAMPLES = 4
TURBS = 8


def turb_place(apart):
    return (apart % 2) * 4 + (apart // 4) * 2 + (apart // 2) % 2


def contract(left, right, left_dim, right_dim):
    return lax.dot_general(
        left, right, (((left_dim,), (right_dim,)), ((), ())), preferred_element_type=jnp.float32
    )


def split_heads(rows, head_dim):
    lane = lax.broadcasted_iota(jnp.int32, rows.shape, 1)
    wide = rows.astype(jnp.float32)
    return jnp.concatenate(
        [jnp.where(lane < head_dim, wide, 0.0), jnp.where(lane >= head_dim, wide, 0.0)], axis=0
    ).astype(jnp.bfloat16)


def join_heads(wide, head_dim):
    block_rows = wide.shape[1] // PAIR
    first = lax.broadcasted_iota(jnp.int32, (wide.shape[0], block_rows), 0) < head_dim
    return jnp.where(first, wide[:, :block_rows], wide[:, block_rows:])


def for_each_block(sectors_ref, lists_ref, block_count, block_rows, work):
    sector = sectors_ref[lax.axis_index("turb")]

    def step(block, carry):
        used = jnp.int32(0)
        for slot in range(UPSTREAM):
            used = used + (lists_ref[sector, block, slot] >= 0).astype(jnp.int32)
        for count in range(UPSTREAM + 1):

            @pl.when(used == count)
            def _():
                sources = [block] + [
                    lists_ref[sector, block, slot] for slot in range(count)
                ]
                work(block, [pl.multiple_of(s * block_rows, block_rows) for s in sources])

        return carry

    lax.fori_loop(0, block_count, step, 0)


def stacked(ref, starts, block_rows, lanes):
    return jnp.concatenate([ref[pl.ds(s, block_rows), lanes] for s in starts], axis=0)


def beside(ref, starts, block_rows, rows):
    return jnp.concatenate([ref[rows, pl.ds(s, block_rows)] for s in starts], axis=1)


def forward_kernel(block_rows, head_dim, sectors_ref, lists_ref, x_ref, gain_ref, wq_ref, wk_ref,
                   wv_ref, wo_ref, normed_t_ref, q_ref, k_ref, v_ref, kt_ref, att_ref,
                   top_ref, inverse_ref, out_ref, normed_ref, vt_ref, rows_ref, sum_ref):
    row_count = x_ref.shape[0]
    quad = pl.program_id(0)
    pair = PAIR * head_dim
    exponent = head_dim ** (-0.5) * LOG2_E
    chunk = min(row_count, 256)

    @pl.when(quad == 0)
    def _():
        for start in range(0, row_count, chunk):
            part = slice(start, start + chunk)
            scaled, _, normed = normalize(x_ref[part, :], gain_ref[...])
            normed_ref[part, :] = normed
            normed_t_ref[:, part] = (scaled * gain_ref[...]).T.astype(jnp.bfloat16)

    normed = normed_ref[...]
    q_ref[...] = contract(normed, wq_ref[...], 1, 0).astype(jnp.bfloat16)
    k_ref[...] = contract(normed, wk_ref[...], 1, 0).astype(jnp.bfloat16)
    v_ref[...] = contract(normed, wv_ref[...], 1, 0).astype(jnp.bfloat16)
    kt_ref[...] = contract(wk_ref[...], normed, 0, 1).astype(jnp.bfloat16)
    vt_ref[...] = contract(wv_ref[...], normed, 0, 1).astype(jnp.bfloat16)

    def work(block, starts):
        own = pl.ds(starts[0], block_rows)
        lanes = [slice(p * pair, (p + 1) * pair) for p in range(QUAD // PAIR)]
        scores = [
            contract(
                stacked(k_ref, starts, block_rows, lane), split_heads(q_ref[own, lane], head_dim), 1, 1
            )
            for lane in lanes
        ]
        for p, lane in enumerate(lanes):
            highest = jnp.max(scores[p], axis=0, keepdims=True)
            weights = jnp.exp2((scores[p] - highest) * exponent)
            inverse = 1.0 / jnp.sum(weights, axis=0, keepdims=True)
            probs = (weights * inverse).astype(jnp.bfloat16)
            top_ref[0, pl.ds(block * (QUAD // PAIR) + p, 1), :] = highest
            inverse_ref[0, pl.ds(block * (QUAD // PAIR) + p, 1), :] = inverse
            joined = join_heads(
                jnp.dot(
                    beside(vt_ref, starts, block_rows, lane),
                    probs,
                    preferred_element_type=jnp.float32,
                ),
                head_dim,
            )
            att_ref[lane, own] = joined.astype(jnp.bfloat16)
            rows_ref[own, lane] = joined.T.astype(jnp.bfloat16)

    for_each_block(sectors_ref, lists_ref, row_count // block_rows, block_rows, work)
    part = contract(rows_ref[...], wo_ref[...], 1, 0)

    @pl.when(quad == 0)
    def _():
        sum_ref[...] = x_ref[...].astype(jnp.float32) + part

    @pl.when(quad > 0)
    def _():
        sum_ref[...] += part

    @pl.when(quad == pl.num_programs(0) - 1)
    def _():
        out_ref[...] = sum_ref[...].astype(jnp.bfloat16)


def forward(sectors, adjacency, rows, norm_gain, query_weight, key_weight, value_weight, out_weight, block_rows):
    row_count, width = rows.shape
    head_dim = width // HEADS
    quad = QUAD * head_dim
    quads = width // quad
    stat_rows = row_count // block_rows * (QUAD // PAIR)
    fixed = lambda *shape: pl.BlockSpec(shape, lambda p, *lists: (0,) * len(shape))
    across = lambda size: pl.BlockSpec((size, quad), lambda p, *lists: (0, p))
    down = lambda size: pl.BlockSpec((quad, size), lambda p, *lists: (p, 0))
    stat = pl.BlockSpec((1, stat_rows, PAIR * block_rows), lambda p, *lists: (p, 0, 0))
    flat = jax.ShapeDtypeStruct((row_count, width), jnp.bfloat16)
    turned = jax.ShapeDtypeStruct((width, row_count), jnp.bfloat16)
    stats = jax.ShapeDtypeStruct((quads, stat_rows, PAIR * block_rows), jnp.float32)
    return pl.pallas_call(
        lambda *refs: forward_kernel(block_rows, head_dim, *refs),
        grid_spec=pltpu.PrefetchScalarGridSpec(
            num_scalar_prefetch=2,
            grid=(quads,),
            in_specs=[fixed(row_count, width), fixed(1, width)]
            + [across(width)] * 3
            + [down(width)],
            out_specs=[fixed(width, row_count)]
            + [across(row_count)] * 3
            + [down(row_count)] * 2
            + [stat] * 2
            + [fixed(row_count, width)],
            scratch_shapes=[
                pltpu.VMEM((row_count, width), jnp.bfloat16),
                pltpu.VMEM((quad, row_count), jnp.bfloat16),
                pltpu.VMEM((row_count, quad), jnp.bfloat16),
                pltpu.VMEM((row_count, width), jnp.float32),
            ],
        ),
        out_shape=[turned, flat, flat, flat, turned, turned, stats, stats, flat],
        compiler_params=pltpu.CompilerParams(vmem_limit_bytes=VMEM_LIMIT),
        cost_estimate=pl.CostEstimate(
            flops=12 * row_count * width * width + 32 * row_count * block_rows * width,
            bytes_accessed=20 * row_count * width,
            transcendentals=row_count * 4 * block_rows * HEADS,
        ),
        name="forward",
    )(sectors, adjacency, rows, norm_gain.reshape(1, width), query_weight, key_weight, value_weight,
      out_weight)


def backward_kernel(block_rows, head_dim, which, sectors_ref, lists_ref, cot_ref, wo_ref, q_ref,
                    k_ref, v_ref, kt_ref, top_ref, inverse_ref, gain_ref, before_ref, *refs):
    late, refs = refs[:5], refs[5:]
    (gq_ref, gk_ref, gv_ref, parts_ref, sum_ref, ga_ref, gk_acc, gv_acc, *held, sems) = refs
    row_count, width = cot_ref.shape
    block_count = row_count // block_rows
    pair = PAIR * head_dim
    quad = QUAD * head_dim
    scale = head_dim ** (-0.5)
    own_lanes = slice(which * quad, (which + 1) * quad)
    copies = []
    for i, (ref, into) in enumerate(zip(late, held)):
        source = ref if i < 2 else ref.at[:, own_lanes]
        copies.append(pltpu.make_async_copy(source, into, sems.at[i]))
        copies[-1].start()
    normed_t_ref, att_ref, *weight_refs = held
    ga_ref[...] = contract(cot_ref[...], wo_ref[...], 1, 1).astype(jnp.bfloat16)
    gk_acc[...] = jnp.zeros_like(gk_acc)
    gv_acc[...] = jnp.zeros_like(gv_acc)

    def work(block, starts):
        own = pl.ds(starts[0], block_rows)
        lanes = [slice(p * pair, (p + 1) * pair) for p in range(QUAD // PAIR)]
        queries = [split_heads(q_ref[own, lane], head_dim) for lane in lanes]
        grads = [split_heads(ga_ref[own, lane], head_dim) for lane in lanes]
        scores = [
            contract(stacked(k_ref, starts, block_rows, lane), queries[p], 1, 1)
            for p, lane in enumerate(lanes)
        ]
        grad_probs = [
            contract(stacked(v_ref, starts, block_rows, lane), grads[p] * scale, 1, 1)
            for p, lane in enumerate(lanes)
        ]
        for p, lane in enumerate(lanes):
            stat = pl.ds(block * (QUAD // PAIR) + p, 1)
            probs = jnp.exp2((scores[p] - top_ref[0, stat, :]) * (scale * LOG2_E))
            probs = probs * inverse_ref[0, stat, :]
            total = jnp.sum(probs * grad_probs[p], axis=0, keepdims=True)
            grad_scores = (probs * (grad_probs[p] - total)).astype(jnp.bfloat16)
            probs_b = probs.astype(jnp.bfloat16)
            grad_values = jnp.dot(probs_b, grads[p], preferred_element_type=jnp.float32)
            grad_keys = jnp.dot(grad_scores, queries[p], preferred_element_type=jnp.float32)
            joined = join_heads(
                jnp.dot(
                    beside(kt_ref, starts, block_rows, lane),
                    grad_scores,
                    preferred_element_type=jnp.float32,
                ),
                head_dim,
            )
            gq_ref[own, lane] = joined.T.astype(jnp.bfloat16)
            for slot, start in enumerate(starts):
                rows = pl.ds(start, block_rows)
                part = slice(slot * block_rows, (slot + 1) * block_rows)
                for acc, terms in ((gk_acc, grad_keys), (gv_acc, grad_values)):
                    term = terms[part]
                    if slot > 0:
                        term = term.astype(jnp.bfloat16).astype(jnp.float32)
                    acc[rows, lane] += term

    for_each_block(sectors_ref, lists_ref, block_count, block_rows, work)
    gk_ref[...] = gk_acc[...].astype(jnp.bfloat16)
    gv_ref[...] = gv_acc[...].astype(jnp.bfloat16)
    for copy in copies:
        copy.wait()
    products = [(normed_t_ref, ref, slice(None)) for ref in (gq_ref, gk_ref, gv_ref)]
    products.append((att_ref, cot_ref, own_lanes))
    own_sample, own_turb = lax.axis_index("sample"), lax.axis_index("turb")
    share = width // TURBS
    along = jnp.zeros((width, quad), jnp.float32)
    for i, (left, right, lanes) in enumerate(products):
        terms = contract(left[...], right[:, lanes], 1, 0)
        if i < len(weight_refs):
            along += terms * weight_refs[i][...].astype(jnp.float32)
        apart = i ^ own_sample
        low, high = apart % 2, apart // 2
        first, second = (high, low) if which == 0 else (low, high)
        for turb in range(TURBS):
            start = pl.multiple_of(second * width + turb_place(turb ^ own_turb) * share, share)
            parts_ref[first, pl.ds(start, share), :] = terms[turb * share : (turb + 1) * share]
    ones = jnp.ones((SUM_ROWS, quad), jnp.bfloat16)
    coarse = along.astype(jnp.bfloat16)
    fine = (along - coarse.astype(jnp.float32)).astype(jnp.bfloat16)
    total = (contract(ones, coarse, 1, 1) + contract(ones, fine, 1, 1)) / gain_ref[...]
    sum_ref[...] = before_ref[...] + total


def backward(sectors, adjacency, cotangent, out_weight, normed_t, queries, keys, values, keys_t,
             attended_t, tops, inverses, norm_gain, query_weight, key_weight, value_weight, before,
             block_rows, which):
    row_count, width = cotangent.shape
    head_dim = width // HEADS
    quad = QUAD * head_dim
    fixed = lambda *shape: pl.BlockSpec(shape, lambda i, *lists: (0,) * len(shape))
    across = pl.BlockSpec((row_count, quad), lambda i, *lists: (0, which))
    down = lambda size: pl.BlockSpec((quad, size), lambda i, *lists: (which, 0))
    stat = pl.BlockSpec((1,) + tops.shape[1:], lambda i, *lists: (which, 0, 0))
    part = jax.ShapeDtypeStruct((row_count, quad), jnp.bfloat16)
    sums = jax.ShapeDtypeStruct((2, 2 * width, quad), jnp.float32)
    return pl.pallas_call(
        lambda *refs: backward_kernel(block_rows, head_dim, which, *refs),
        grid_spec=pltpu.PrefetchScalarGridSpec(
            num_scalar_prefetch=2,
            grid=(1,),
            in_specs=[fixed(row_count, width), down(width)]
            + [across] * 3
            + [down(row_count)]
            + [stat] * 2
            + [fixed(1, width), fixed(SUM_ROWS, width)]
            + [pl.BlockSpec(memory_space=pl.ANY)] * 5,
            out_specs=[fixed(row_count, quad)] * 3
            + [fixed(*sums.shape), fixed(SUM_ROWS, width)],
            scratch_shapes=[
                pltpu.VMEM((row_count, quad), jnp.bfloat16),
                pltpu.VMEM((row_count, quad), jnp.float32),
                pltpu.VMEM((row_count, quad), jnp.float32),
            ]
            + [pltpu.VMEM((width, row_count), jnp.bfloat16)] * 2
            + [pltpu.VMEM((width, quad), jnp.bfloat16)] * 3
            + [pltpu.SemaphoreType.DMA((5,))],
        ),
        out_shape=[part] * 3 + [sums, jax.ShapeDtypeStruct((SUM_ROWS, width), jnp.float32)],
        compiler_params=pltpu.CompilerParams(vmem_limit_bytes=VMEM_LIMIT),
        cost_estimate=pl.CostEstimate(
            flops=10 * row_count * width * quad + 80 * row_count * block_rows * quad,
            bytes_accessed=14 * row_count * width,
            transcendentals=row_count * 4 * block_rows * QUAD,
        ),
        name="backward",
    )(sectors, adjacency, cotangent, out_weight, queries, keys, values, keys_t, tops, inverses,
      norm_gain.reshape(1, width), before, normed_t, attended_t, query_weight, key_weight,
      value_weight)


def finish_kernel(quads, x_ref, cot_ref, gain_ref, wq_ref, wk_ref, wv_ref, *refs):
    grad_refs, out_ref = refs[:-1], refs[-1]
    scaled, inverse, _ = normalize(x_ref[...], gain_ref[...])
    quad = grad_refs[0].shape[1]
    grad_normed = jnp.zeros(x_ref.shape, jnp.float32)
    for i in range(quads):
        lanes = slice(i * quad, (i + 1) * quad)
        for j, weight_ref in enumerate((wq_ref, wk_ref, wv_ref)):
            grad_normed += contract(grad_refs[3 * i + j][...], weight_ref[:, lanes], 1, 1)
    grad_scaled = grad_normed * gain_ref[...]
    grad_input = inverse * (
        grad_scaled
        - jnp.mean(grad_scaled, axis=-1, keepdims=True)
        - scaled * jnp.mean(grad_scaled * scaled, axis=-1, keepdims=True)
    )
    out_ref[...] = (cot_ref[...].astype(jnp.float32) + grad_input).astype(jnp.bfloat16)


def finish(rows, cotangent, norm_gain, query_weight, key_weight, value_weight, grads):
    row_count, width = rows.shape
    quad = grads[0].shape[1]
    step = min(row_count, 256)
    fixed = lambda *shape: pl.BlockSpec(shape, lambda i: (0,) * len(shape))
    by_row = lambda size: pl.BlockSpec((step, size), lambda i: (i, 0))
    return pl.pallas_call(
        lambda *refs: finish_kernel(width // quad, *refs),
        grid=(row_count // step,),
        in_specs=[by_row(width)] * 2
        + [fixed(1, width)]
        + [fixed(width, width)] * 3
        + [by_row(quad)] * len(grads),
        out_specs=by_row(width),
        out_shape=jax.ShapeDtypeStruct((row_count, width), jnp.bfloat16),
        compiler_params=pltpu.CompilerParams(vmem_limit_bytes=VMEM_LIMIT),
        cost_estimate=pl.CostEstimate(
            flops=6 * row_count * width * width,
            bytes_accessed=16 * row_count * width,
            transcendentals=0,
        ),
        name="finish",
    )(rows, cotangent, norm_gain.reshape(1, width), query_weight, key_weight, value_weight, *grads)


def swap(tensor, axis):
    return lax.all_to_all(tensor, axis, split_axis=0, concat_axis=0, tiled=True)


def across(tensor, axis, distance):
    size = lax.axis_size(axis)
    return lax.ppermute(tensor, axis, [(i, i ^ distance) for i in range(size)])


def across(tensor, axis, distance):
    size = lax.axis_size(axis)
    return lax.ppermute(tensor, axis, [(i, i ^ distance) for i in range(size)])


def reduce_sums(early, late, width, beside):
    quad = early[0].shape[-1]
    wide = jnp.float32

    def pack(gain):
        high = gain.astype(jnp.bfloat16)
        low = (gain - high.astype(wide)).astype(jnp.bfloat16)
        return jnp.concatenate([high, low, jnp.zeros((16 - 2 * gain.shape[0], quad), jnp.bfloat16)])

    def unpack(rows, count):
        return rows[:count].astype(wide) + rows[count : 2 * count].astype(wide)

    parts, arrived = early
    first = parts[0] + arrived.astype(wide)
    first = first[:width] + across(first[width:], "sample", 1)
    parts, arrived, gain = late
    second = parts[0] + arrived
    count = gain.shape[0]
    arrived = across(
        jnp.concatenate([second[width:].astype(jnp.bfloat16), pack(gain)]), "sample", 2
    )
    second = second[:width] + arrived[:width].astype(wide)
    gain = gain + unpack(arrived[width:], count)
    for distance in (1, 4, 2):
        half = first.shape[0] // 2
        halves = [part[half:].astype(jnp.bfloat16) for part in (first, second)]
        arrived = across(jnp.concatenate(halves + [pack(gain)]), "turb", distance)
        first = first[:half] + arrived[:half].astype(wide)
        second = second[:half] + arrived[half : 2 * half].astype(wide)
        gain = gain + unpack(arrived[2 * half :], count)
    total = jnp.stack([first, second]).astype(jnp.bfloat16)[None]
    total, beside = lax.optimization_barrier((total, beside))
    for distance in (2, 4, 1):
        total = jnp.concatenate([total, across(total, "turb", distance)])
    both = [total, across(total, "sample", 2)]
    both += [across(part, "sample", 1) for part in both]
    return both, gain.reshape(width), beside


def place_kernel(*refs):
    (*parts, query_ref, key_ref, value_ref, out_ref, all_ref) = refs
    own_sample, own_turb = lax.axis_index("sample"), lax.axis_index("turb")
    turbs, quads, share, quad = parts[0].shape
    for i, ref in enumerate(parts):
        product = own_sample ^ ((i % 2) * 2 + i // 2)
        for apart in range(turbs):
            rows = pl.ds(pl.multiple_of((apart ^ own_turb) * share, share), share)
            for j in range(quads):
                all_ref[product, rows, j * quad : (j + 1) * quad] = ref[
                    turb_place(apart), j
                ].astype(jnp.float32)
    for i, ref in enumerate((query_ref, key_ref, value_ref, out_ref)):
        ref[...] = all_ref[i]


def place_sums(parts, width):
    return pl.pallas_call(
        place_kernel,
        in_specs=[pl.BlockSpec(memory_space=pltpu.VMEM)] * len(parts),
        out_specs=[pl.BlockSpec(memory_space=pltpu.VMEM)] * 4,
        out_shape=[jax.ShapeDtypeStruct((width, width), jnp.float32)] * 4,
        scratch_shapes=[pltpu.VMEM((4, width, width), jnp.float32)],
        compiler_params=pltpu.CompilerParams(vmem_limit_bytes=VMEM_LIMIT),
        cost_estimate=pl.CostEstimate(
            flops=0, bytes_accessed=24 * width * width, transcendentals=0
        ),
        name="place",
    )(*parts)


def by_sample(
    inflow,
    cotangent,
    norm_gain,
    query_weight,
    key_weight,
    value_weight,
    out_weight,
    adjacency,
    sectors,
):
    sample_count, block_rows, width = inflow.shape
    row_count = lax.axis_size("turb") * block_rows
    rows = swap(inflow, "turb")
    rows, cotangent = lax.optimization_barrier((rows, cotangent))
    rows = rows.reshape(row_count, width)
    grad_rows = swap(cotangent, "turb").reshape(row_count, width)
    *saved, layer_rows = forward(
        sectors, adjacency, rows, norm_gain, query_weight, key_weight, value_weight, out_weight,
        block_rows,
    )
    layer_output = swap(layer_rows.reshape(inflow.shape), "turb")
    weights = (norm_gain, query_weight, key_weight, value_weight)
    none = jnp.zeros((SUM_ROWS, width), jnp.float32)
    *grads, early, before = backward(
        sectors, adjacency, grad_rows, out_weight, *saved, *weights, none, block_rows, 0
    )
    arrived_early = across(early[1].astype(jnp.bfloat16), "sample", 2)
    *more, late, gain = backward(
        sectors, adjacency, grad_rows, out_weight, *saved, *weights, before, block_rows, 1
    )
    late, gain, arrived_early, layer_output = lax.optimization_barrier(
        (late, gain, arrived_early, layer_output)
    )
    arrived_late = across(late[1], "sample", 1)
    gain = gain[0].reshape(-1, late.shape[2])
    gain = gain + across(gain, "sample", 1)
    grad_rows = finish(rows, grad_rows, *weights, grads + more)
    grad_inflow = swap(grad_rows.reshape(inflow.shape), "turb")
    parts, sum_gain, grad_inflow = reduce_sums(
        (early, arrived_early), (late, arrived_late, gain), width, grad_inflow
    )
    sums = place_sums(parts, width)
    return (layer_output, grad_inflow, *sums, sum_gain)


def solution(mesh):
    placed = (
        P("sample", "turb", None),
        P("sample", "turb", None),
        P(),
        P(),
        P(),
        P(),
        P(),
        P(),
        P("sample"),
    )

    def plan(*args):
        sample_count = args[0].shape[0]
        if sample_count == mesh.shape["turb"] == TURBS and mesh.shape["sample"] == SAMPLES:
            return by_sample(*args)
        return on_device(*args)

    return jax.shard_map(
        plan,
        mesh=mesh,
        in_specs=placed,
        out_specs=(P("sample", "turb", None), P("sample", "turb", None), P(), P(), P(), P(), P()),
        check_vma=False,
    )
```

```python
import jax
import jax.numpy as jnp
from jax import lax
from jax.experimental import pallas as pl
from jax.experimental.pallas import tpu as pltpu
from jax.sharding import PartitionSpec as P

HEADS = 8
UPSTREAM = 3
SECTORS = 8
REPEAT = 1


epsilon = 1e-05


def normalize(row_block, norm_gain):
    widened = row_block.astype(jnp.float32)
    centred = widened - jnp.mean(widened, axis=-1, keepdims=True)
    inverse = lax.rsqrt(jnp.mean(centred * centred, axis=-1, keepdims=True) + epsilon)
    scaled = centred * inverse
    return (scaled, inverse, (scaled * norm_gain).astype(jnp.bfloat16))


def attend(pieces):
    queries, key_rows, value_rows, key_usable, grad_attended = pieces
    batch_count, query_count, model_width = queries.shape
    key_count = key_rows.shape[1]
    head_dim = model_width // HEADS
    score_scale = head_dim ** (-0.5)
    query_heads = queries.reshape(batch_count, query_count, HEADS, head_dim)
    key_heads = key_rows.reshape(batch_count, key_count, HEADS, head_dim)
    value_heads = value_rows.reshape(batch_count, key_count, HEADS, head_dim)
    grad_heads = grad_attended.reshape(batch_count, query_count, HEADS, head_dim)
    scores = (
        jnp.einsum("nqhd,nkhd->nhqk", query_heads, key_heads, preferred_element_type=jnp.float32)
        * score_scale
    )
    scores = jnp.where(key_usable[:, None, None, :], scores, -1e30)
    highest = jnp.max(scores, axis=-1, keepdims=True)
    weights = jnp.exp(scores - highest)
    probabilities = weights / jnp.sum(weights, axis=-1, keepdims=True)
    rounded = probabilities.astype(jnp.bfloat16)
    attended = jnp.einsum(
        "nhqk,nkhd->nqhd", rounded, value_heads, preferred_element_type=jnp.float32
    ).astype(jnp.bfloat16)
    grad_probs = jnp.einsum(
        "nqhd,nkhd->nhqk", grad_heads, value_heads, preferred_element_type=jnp.float32
    )
    centred = grad_probs - jnp.sum(probabilities * grad_probs, axis=-1, keepdims=True)
    grad_scores = (probabilities * centred * score_scale).astype(jnp.bfloat16)
    grad_queries = jnp.einsum(
        "nhqk,nkhd->nqhd", grad_scores, key_heads, preferred_element_type=jnp.float32
    ).astype(jnp.bfloat16)
    grad_keys = jnp.einsum(
        "nhqk,nqhd->nkhd", grad_scores, query_heads, preferred_element_type=jnp.float32
    )
    grad_values = jnp.einsum(
        "nhqk,nqhd->nkhd", rounded, grad_heads, preferred_element_type=jnp.float32
    )
    pair_terms = jnp.concatenate(
        [
            grad_keys.reshape(batch_count, key_count, model_width),
            grad_values.reshape(batch_count, key_count, model_width),
        ],
        axis=-1,
    )
    return (
        attended.reshape(batch_count, query_count, model_width),
        grad_queries.reshape(batch_count, query_count, model_width),
        pair_terms,
    )


def on_device(
    inflow,
    cotangent,
    norm_gain,
    query_weight,
    key_weight,
    value_weight,
    out_weight,
    adjacency,
    sectors,
):
    sample_count, block_rows, model_width = inflow.shape
    block_count = lax.axis_size("turb")
    own_block = lax.axis_index("turb")
    slot_count = REPEAT * ((SECTORS * UPSTREAM + block_count - 2) // (block_count - 1))
    flat_rows = sample_count * block_rows
    pair_width = 2 * model_width
    input_rows = inflow.reshape(flat_rows, model_width)
    grad_rows = cotangent.reshape(flat_rows, model_width)
    scaled, inverse, normed = normalize(input_rows, norm_gain)
    queries = jnp.dot(normed, query_weight, preferred_element_type=jnp.float32).astype(jnp.bfloat16)
    key_rows = jnp.dot(normed, key_weight, preferred_element_type=jnp.float32).astype(jnp.bfloat16)
    value_rows = jnp.dot(normed, value_weight, preferred_element_type=jnp.float32).astype(
        jnp.bfloat16
    )
    upstream = adjacency[sectors]
    needed = jnp.any(upstream == own_block, axis=2).astype(jnp.int32)
    earlier_need = jnp.cumsum(needed, axis=0) - needed
    slot_index = lax.broadcasted_iota(jnp.int32, (block_count, slot_count, sample_count), 1)
    chosen = (needed.T[:, None, :] == 1) & (earlier_need.T[:, None, :] == slot_index)
    selector = chosen.astype(jnp.bfloat16).reshape(block_count * slot_count, sample_count)
    own_lists = lax.dynamic_index_in_dim(upstream, own_block, axis=1, keepdims=False)
    usable = own_lists >= 0
    matches = jnp.any(own_lists[:, :, None, None] == own_lists[None, None, :, :], axis=3)
    sample_ids = lax.broadcasted_iota(jnp.int32, (sample_count, sample_count), 0)
    earlier = lax.broadcasted_iota(jnp.int32, (sample_count, sample_count), 1) < sample_ids
    position = jnp.sum((matches & earlier[:, None, :]).astype(jnp.int32), axis=2)
    flat_slot = own_lists * slot_count + position
    fetch_at = jnp.where(usable, flat_slot, 0)
    payload = jnp.concatenate([key_rows, value_rows], axis=1).reshape(
        sample_count, block_rows * pair_width
    )
    packed = jnp.dot(selector, payload, preferred_element_type=jnp.float32).astype(jnp.bfloat16)
    arrived = lax.all_to_all(
        packed.reshape(block_count, slot_count, block_rows, pair_width),
        "turb",
        split_axis=0,
        concat_axis=0,
        tiled=True,
    )
    fetched = arrived.reshape(block_count * slot_count, block_rows, pair_width)[fetch_at]
    upstream_keys = fetched[..., :model_width]
    upstream_values = fetched[..., model_width:]
    key_count = (1 + UPSTREAM) * block_rows
    key_all = jnp.concatenate(
        [key_rows.reshape(sample_count, 1, block_rows, model_width), upstream_keys], axis=1
    ).reshape(sample_count, key_count, model_width)
    value_all = jnp.concatenate(
        [value_rows.reshape(sample_count, 1, block_rows, model_width), upstream_values], axis=1
    ).reshape(sample_count, key_count, model_width)
    block_usable = jnp.concatenate([jnp.ones((sample_count, 1), dtype=jnp.bool_), usable], axis=1)
    key_usable = jnp.repeat(block_usable, block_rows, axis=1)
    grad_attended = jnp.dot(grad_rows, out_weight.T, preferred_element_type=jnp.float32).astype(
        jnp.bfloat16
    )
    group_size = min(sample_count, max(1, 512 // block_rows))
    while sample_count % group_size != 0:
        group_size = group_size - 1
    group_count = sample_count // group_size

    def grouped(tensor):
        return tensor.reshape((group_count, group_size) + tensor.shape[1:])

    attended, grad_queries, pair_terms = lax.map(
        attend,
        (
            grouped(queries.reshape(sample_count, block_rows, model_width)),
            grouped(key_all),
            grouped(value_all),
            grouped(key_usable),
            grouped(grad_attended.reshape(sample_count, block_rows, model_width)),
        ),
    )
    attended = attended.reshape(flat_rows, model_width)
    grad_queries = grad_queries.reshape(flat_rows, model_width)
    pair_terms = pair_terms.reshape(sample_count, 1 + UPSTREAM, block_rows, pair_width)
    layer_output = (
        (
            input_rows.astype(jnp.float32)
            + jnp.dot(attended, out_weight, preferred_element_type=jnp.float32)
        )
        .astype(jnp.bfloat16)
        .reshape(inflow.shape)
    )
    outgoing = (
        pair_terms[:, 1:]
        .astype(jnp.bfloat16)
        .reshape(sample_count * UPSTREAM, block_rows, pair_width)
    )
    target = jnp.where(usable, flat_slot, block_count * slot_count).reshape(-1)
    outbound = (
        jnp.zeros((block_count * slot_count, block_rows, pair_width), jnp.bfloat16)
        .at[target]
        .set(outgoing, mode="drop")
    )
    sum_out = jnp.dot(attended.T, grad_rows, preferred_element_type=jnp.float32)
    sum_query = jnp.dot(normed.T, grad_queries, preferred_element_type=jnp.float32)
    returned = lax.all_to_all(
        outbound.reshape(block_count, slot_count, block_rows, pair_width),
        "turb",
        split_axis=0,
        concat_axis=0,
        tiled=True,
    )
    remote = jnp.dot(
        selector.T,
        returned.reshape(block_count * slot_count, block_rows * pair_width),
        preferred_element_type=jnp.float32,
    )
    combined = (
        (pair_terms[:, 0].reshape(sample_count, block_rows * pair_width) + remote)
        .astype(jnp.bfloat16)
        .reshape(flat_rows, pair_width)
    )
    grad_keys = combined[:, :model_width]
    grad_values = combined[:, model_width:]
    sum_key = jnp.dot(normed.T, grad_keys, preferred_element_type=jnp.float32)
    sum_value = jnp.dot(normed.T, grad_values, preferred_element_type=jnp.float32)
    grad_normed = jnp.dot(grad_queries, query_weight.T, preferred_element_type=jnp.float32)
    grad_normed = grad_normed + jnp.dot(grad_keys, key_weight.T, preferred_element_type=jnp.float32)
    grad_normed = grad_normed + jnp.dot(
        grad_values, value_weight.T, preferred_element_type=jnp.float32
    )
    sum_gain = jnp.sum(grad_normed * scaled, axis=0)
    grad_scaled = grad_normed * norm_gain
    grad_input = inverse * (
        grad_scaled
        - jnp.mean(grad_scaled, axis=-1, keepdims=True)
        - scaled * jnp.mean(grad_scaled * scaled, axis=-1, keepdims=True)
    )
    grad_inflow = (
        (grad_rows.astype(jnp.float32) + grad_input).astype(jnp.bfloat16).reshape(inflow.shape)
    )
    sum_query, sum_key, sum_value, sum_out, sum_gain = lax.psum(
        (sum_query, sum_key, sum_value, sum_out, sum_gain), ("sample", "turb")
    )
    return (layer_output, grad_inflow, sum_query, sum_key, sum_value, sum_out, sum_gain)


PAIR = 2
QUAD = 4
LOG2_E = 1.4426950408889634
VMEM_LIMIT = 58 * 2**20
SUM_ROWS = 8
SAMPLES = 4
TURBS = 8


def turb_place(apart):
    return (apart % 2) * 4 + (apart // 4) * 2 + (apart // 2) % 2


def contract(left, right, left_dim, right_dim):
    return lax.dot_general(
        left, right, (((left_dim,), (right_dim,)), ((), ())), preferred_element_type=jnp.float32
    )


def split_heads(rows, head_dim):
    lane = lax.broadcasted_iota(jnp.int32, rows.shape, 1)
    wide = rows.astype(jnp.float32)
    return jnp.concatenate(
        [jnp.where(lane < head_dim, wide, 0.0), jnp.where(lane >= head_dim, wide, 0.0)], axis=0
    ).astype(jnp.bfloat16)


def join_heads(wide, head_dim):
    block_rows = wide.shape[1] // PAIR
    first = lax.broadcasted_iota(jnp.int32, (wide.shape[0], block_rows), 0) < head_dim
    return jnp.where(first, wide[:, :block_rows], wide[:, block_rows:])


def for_each_block(sectors_ref, lists_ref, block_count, block_rows, work):
    sector = sectors_ref[lax.axis_index("turb")]

    def step(block, carry):
        used = jnp.int32(0)
        for slot in range(UPSTREAM):
            used = used + (lists_ref[slot, sector, block] >= 0).astype(jnp.int32)
        for count in range(UPSTREAM + 1):

            @pl.when(used == count)
            def _():
                sources = [block] + [
                    lists_ref[slot, sector, block] for slot in range(count)
                ]
                work(block, [pl.multiple_of(s * block_rows, block_rows) for s in sources])

        return carry

    lax.fori_loop(0, block_count, step, 0)


def stacked(ref, starts, block_rows, lanes):
    return jnp.concatenate([ref[pl.ds(s, block_rows), lanes] for s in starts], axis=0)


def beside(ref, starts, block_rows, rows):
    return jnp.concatenate([ref[rows, pl.ds(s, block_rows)] for s in starts], axis=1)


def forward_kernel(block_rows, head_dim, sectors_ref, lists_ref, x_ref, gain_ref, wq_ref, wk_ref,
                   wv_ref, wo_ref, normed_t_ref, q_ref, k_ref, v_ref, kt_ref, att_ref,
                   level_ref, out_ref, normed_ref, vt_ref, rows_ref, sum_ref):
    row_count = x_ref.shape[0]
    quad = pl.program_id(0)
    pair = PAIR * head_dim
    exponent = head_dim ** (-0.5) * LOG2_E
    chunk = min(row_count, 256)

    @pl.when(quad == 0)
    def _():
        for start in range(0, row_count, chunk):
            part = slice(start, start + chunk)
            scaled, _, normed = normalize(x_ref[part, :], gain_ref[...])
            normed_ref[part, :] = normed
            normed_t_ref[:, part] = (scaled * gain_ref[...]).T.astype(jnp.bfloat16)

    normed = normed_ref[...]
    q_ref[...] = contract(normed, wq_ref[...], 1, 0).astype(jnp.bfloat16)
    k_ref[...] = contract(normed, wk_ref[...], 1, 0).astype(jnp.bfloat16)
    v_ref[...] = contract(normed, wv_ref[...], 1, 0).astype(jnp.bfloat16)
    kt_ref[...] = contract(wk_ref[...], normed, 0, 1).astype(jnp.bfloat16)
    vt_ref[...] = contract(wv_ref[...], normed, 0, 1).astype(jnp.bfloat16)

    def work(block, starts):
        own = pl.ds(starts[0], block_rows)
        lanes = [slice(p * pair, (p + 1) * pair) for p in range(QUAD // PAIR)]
        scores = [
            contract(
                stacked(k_ref, starts, block_rows, lane), split_heads(q_ref[own, lane], head_dim), 1, 1
            )
            for lane in lanes
        ]
        for p, lane in enumerate(lanes):
            highest = jnp.max(scores[p], axis=0, keepdims=True)
            weights = jnp.exp2((scores[p] - highest) * exponent)
            total = jnp.sum(weights, axis=0, keepdims=True)
            probs = (weights * (1.0 / total)).astype(jnp.bfloat16)
            level_ref[0, pl.ds(block * (QUAD // PAIR) + p, 1), :] = highest * exponent + jnp.log2(
                total
            )
            joined = join_heads(
                jnp.dot(
                    beside(vt_ref, starts, block_rows, lane),
                    probs,
                    preferred_element_type=jnp.float32,
                ),
                head_dim,
            )
            att_ref[lane, own] = joined.astype(jnp.bfloat16)
            rows_ref[own, lane] = joined.T.astype(jnp.bfloat16)

    for_each_block(sectors_ref, lists_ref, row_count // block_rows, block_rows, work)
    part = contract(rows_ref[...], wo_ref[...], 1, 0)

    @pl.when(quad == 0)
    def _():
        sum_ref[...] = x_ref[...].astype(jnp.float32) + part

    @pl.when(quad > 0)
    def _():
        sum_ref[...] += part

    @pl.when(quad == pl.num_programs(0) - 1)
    def _():
        out_ref[...] = sum_ref[...].astype(jnp.bfloat16)


def forward(sectors, adjacency, rows, norm_gain, query_weight, key_weight, value_weight, out_weight, block_rows):
    row_count, width = rows.shape
    head_dim = width // HEADS
    quad = QUAD * head_dim
    quads = width // quad
    stat_rows = row_count // block_rows * (QUAD // PAIR)
    fixed = lambda *shape: pl.BlockSpec(shape, lambda p, *lists: (0,) * len(shape))
    across = lambda size: pl.BlockSpec((size, quad), lambda p, *lists: (0, p))
    down = lambda size: pl.BlockSpec((quad, size), lambda p, *lists: (p, 0))
    stat = pl.BlockSpec((1, stat_rows, PAIR * block_rows), lambda p, *lists: (p, 0, 0))
    flat = jax.ShapeDtypeStruct((row_count, width), jnp.bfloat16)
    turned = jax.ShapeDtypeStruct((width, row_count), jnp.bfloat16)
    stats = jax.ShapeDtypeStruct((quads, stat_rows, PAIR * block_rows), jnp.float32)
    return pl.pallas_call(
        lambda *refs: forward_kernel(block_rows, head_dim, *refs),
        grid_spec=pltpu.PrefetchScalarGridSpec(
            num_scalar_prefetch=2,
            grid=(quads,),
            in_specs=[fixed(row_count, width), fixed(1, width)]
            + [across(width)] * 3
            + [down(width)],
            out_specs=[fixed(width, row_count)]
            + [across(row_count)] * 3
            + [down(row_count)] * 2
            + [stat, fixed(row_count, width)],
            scratch_shapes=[
                pltpu.VMEM((row_count, width), jnp.bfloat16),
                pltpu.VMEM((quad, row_count), jnp.bfloat16),
                pltpu.VMEM((row_count, quad), jnp.bfloat16),
                pltpu.VMEM((row_count, width), jnp.float32),
            ],
        ),
        out_shape=[turned, flat, flat, flat, turned, turned, stats, flat],
        compiler_params=pltpu.CompilerParams(vmem_limit_bytes=VMEM_LIMIT),
        cost_estimate=pl.CostEstimate(
            flops=12 * row_count * width * width + 32 * row_count * block_rows * width,
            bytes_accessed=20 * row_count * width,
            transcendentals=row_count * 4 * block_rows * HEADS,
        ),
        name="forward",
    )(sectors, adjacency, rows, norm_gain.reshape(1, width), query_weight, key_weight, value_weight,
      out_weight)


def backward_kernel(block_rows, head_dim, which, sectors_ref, lists_ref, wo_ref, q_ref, k_ref, v_ref,
                    kt_ref, level_ref, gain_ref, before_ref, *refs):
    late, refs = refs[:6], refs[6:]
    gq_ref, gk_ref, gv_ref, keep_ref, send_ref, sum_ref, *refs = refs
    ga_ref, gk_acc, gv_acc, parts_ref, *held, sems = refs
    cot_ref = held[0]
    row_count, width = cot_ref.shape
    block_count = row_count // block_rows
    pair = PAIR * head_dim
    quad = QUAD * head_dim
    scale = head_dim ** (-0.5)
    own_lanes = slice(which * quad, (which + 1) * quad)
    copies = []
    for i, (ref, into) in enumerate(zip(late, held)):
        source = ref if i < 3 else ref.at[:, own_lanes]
        copies.append(pltpu.make_async_copy(source, into, sems.at[i]))
        copies[-1].start()
    _, normed_t_ref, att_ref, *weight_refs = held
    copies[0].wait()
    ga_ref[...] = contract(cot_ref[...], wo_ref[...], 1, 1).astype(jnp.bfloat16)
    gk_acc[...] = jnp.zeros_like(gk_acc)
    gv_acc[...] = jnp.zeros_like(gv_acc)

    def work(block, starts):
        own = pl.ds(starts[0], block_rows)
        lanes = [slice(p * pair, (p + 1) * pair) for p in range(QUAD // PAIR)]
        queries = [split_heads(q_ref[own, lane], head_dim) for lane in lanes]
        grads = [split_heads(ga_ref[own, lane], head_dim) for lane in lanes]
        scores = [
            contract(stacked(k_ref, starts, block_rows, lane), queries[p], 1, 1)
            for p, lane in enumerate(lanes)
        ]
        grad_probs = [
            contract(stacked(v_ref, starts, block_rows, lane), grads[p] * scale, 1, 1)
            for p, lane in enumerate(lanes)
        ]
        for p, lane in enumerate(lanes):
            stat = pl.ds(block * (QUAD // PAIR) + p, 1)
            probs = jnp.exp2(scores[p] * (scale * LOG2_E) - level_ref[0, stat, :])
            total = jnp.sum(probs * grad_probs[p], axis=0, keepdims=True)
            grad_scores = (probs * (grad_probs[p] - total)).astype(jnp.bfloat16)
            probs_b = probs.astype(jnp.bfloat16)
            grad_values = jnp.dot(probs_b, grads[p], preferred_element_type=jnp.float32)
            grad_keys = jnp.dot(grad_scores, queries[p], preferred_element_type=jnp.float32)
            joined = join_heads(
                jnp.dot(
                    beside(kt_ref, starts, block_rows, lane),
                    grad_scores,
                    preferred_element_type=jnp.float32,
                ),
                head_dim,
            )
            gq_ref[own, lane] = joined.T.astype(jnp.bfloat16)
            for slot, start in enumerate(starts):
                rows = pl.ds(start, block_rows)
                part = slice(slot * block_rows, (slot + 1) * block_rows)
                for acc, terms in ((gk_acc, grad_keys), (gv_acc, grad_values)):
                    term = terms[part]
                    if slot > 0:
                        term = term.astype(jnp.bfloat16).astype(jnp.float32)
                    acc[rows, lane] += term

    for_each_block(sectors_ref, lists_ref, block_count, block_rows, work)
    gk_ref[...] = gk_acc[...].astype(jnp.bfloat16)
    gv_ref[...] = gv_acc[...].astype(jnp.bfloat16)
    for copy in copies[1:]:
        copy.wait()
    products = [(normed_t_ref, ref, slice(None)) for ref in (gq_ref, gk_ref, gv_ref)]
    products.append((att_ref, cot_ref, own_lanes))
    own_sample, own_turb = lax.axis_index("sample"), lax.axis_index("turb")
    share = width // TURBS
    along = jnp.zeros((width, quad), jnp.float32)
    for i, (left, right, lanes) in enumerate(products):
        terms = contract(left[...], right[:, lanes], 1, 0)
        if i < len(weight_refs):
            along += terms * weight_refs[i][...].astype(jnp.float32)
        apart = i ^ own_sample
        for turb in range(TURBS):
            place = turb_place(turb ^ own_turb)
            if which == 0:
                half, start = place // 4, (apart % 2 * 2 + apart // 2) * 4 + place % 4
            else:
                half, start = apart % 2, apart // 2 * TURBS + place
            start = pl.multiple_of(start * share, share)
            parts_ref[half, pl.ds(start, share), :] = terms[turb * share : (turb + 1) * share]
    keep_ref[...] = parts_ref[0]
    send_ref[...] = parts_ref[1].astype(send_ref.dtype)
    ones = jnp.ones((SUM_ROWS, quad), jnp.bfloat16)
    coarse = along.astype(jnp.bfloat16)
    fine = (along - coarse.astype(jnp.float32)).astype(jnp.bfloat16)
    total = (contract(ones, coarse, 1, 1) + contract(ones, fine, 1, 1)) / gain_ref[...]
    sum_ref[...] = before_ref[...] + total


def backward(sectors, adjacency, cotangent, out_weight, normed_t, queries, keys, values, keys_t,
             attended_t, levels, norm_gain, query_weight, key_weight, value_weight, before,
             block_rows, which):
    row_count, width = cotangent.shape
    head_dim = width // HEADS
    quad = QUAD * head_dim
    fixed = lambda *shape: pl.BlockSpec(shape, lambda i, *lists: (0,) * len(shape))
    across = pl.BlockSpec((row_count, quad), lambda i, *lists: (0, which))
    down = lambda size: pl.BlockSpec((quad, size), lambda i, *lists: (which, 0))
    stat = pl.BlockSpec((1,) + levels.shape[1:], lambda i, *lists: (which, 0, 0))
    part = jax.ShapeDtypeStruct((row_count, quad), jnp.bfloat16)
    half = (2 * width, quad)
    sent = jnp.bfloat16 if which == 0 else jnp.float32
    return pl.pallas_call(
        lambda *refs: backward_kernel(block_rows, head_dim, which, *refs),
        grid_spec=pltpu.PrefetchScalarGridSpec(
            num_scalar_prefetch=2,
            grid=(1,),
            in_specs=[down(width)]
            + [across] * 3
            + [down(row_count), stat, fixed(1, width), fixed(SUM_ROWS, width)]
            + [pl.BlockSpec(memory_space=pl.ANY)] * 6,
            out_specs=[fixed(row_count, quad)] * 3
            + [fixed(*half)] * 2
            + [fixed(SUM_ROWS, width)],
            scratch_shapes=[
                pltpu.VMEM((row_count, quad), jnp.bfloat16),
                pltpu.VMEM((row_count, quad), jnp.float32),
                pltpu.VMEM((row_count, quad), jnp.float32),
                pltpu.VMEM((2,) + half, jnp.float32),
            ]
            + [pltpu.VMEM((row_count, width), jnp.bfloat16)]
            + [pltpu.VMEM((width, row_count), jnp.bfloat16)] * 2
            + [pltpu.VMEM((width, quad), jnp.bfloat16)] * 3
            + [pltpu.SemaphoreType.DMA((6,))],
        ),
        out_shape=[part] * 3
        + [
            jax.ShapeDtypeStruct(half, jnp.float32),
            jax.ShapeDtypeStruct(half, sent),
            jax.ShapeDtypeStruct((SUM_ROWS, width), jnp.float32),
        ],
        compiler_params=pltpu.CompilerParams(vmem_limit_bytes=VMEM_LIMIT),
        cost_estimate=pl.CostEstimate(
            flops=10 * row_count * width * quad + 80 * row_count * block_rows * quad,
            bytes_accessed=14 * row_count * width,
            transcendentals=row_count * 4 * block_rows * QUAD,
        ),
        name="backward",
    )(sectors, adjacency, out_weight, queries, keys, values, keys_t, levels,
      norm_gain.reshape(1, width), before, cotangent, normed_t, attended_t, query_weight, key_weight,
      value_weight)


def finish_kernel(quads, x_ref, cot_ref, gain_ref, wq_ref, wk_ref, wv_ref, *refs):
    grad_refs, out_ref = refs[:-1], refs[-1]
    scaled, inverse, _ = normalize(x_ref[...], gain_ref[...])
    quad = grad_refs[0].shape[1]
    grad_normed = jnp.zeros(x_ref.shape, jnp.float32)
    for i in range(quads):
        lanes = slice(i * quad, (i + 1) * quad)
        for j, weight_ref in enumerate((wq_ref, wk_ref, wv_ref)):
            grad_normed += contract(grad_refs[3 * i + j][...], weight_ref[:, lanes], 1, 1)
    grad_scaled = grad_normed * gain_ref[...]
    grad_input = inverse * (
        grad_scaled
        - jnp.mean(grad_scaled, axis=-1, keepdims=True)
        - scaled * jnp.mean(grad_scaled * scaled, axis=-1, keepdims=True)
    )
    out_ref[...] = (cot_ref[...].astype(jnp.float32) + grad_input).astype(jnp.bfloat16)


def finish(rows, cotangent, norm_gain, query_weight, key_weight, value_weight, grads):
    row_count, width = rows.shape
    quad = grads[0].shape[1]
    step = min(row_count, 256)
    fixed = lambda *shape: pl.BlockSpec(shape, lambda i: (0,) * len(shape))
    by_row = lambda size: pl.BlockSpec((step, size), lambda i: (i, 0))
    return pl.pallas_call(
        lambda *refs: finish_kernel(width // quad, *refs),
        grid=(row_count // step,),
        in_specs=[by_row(width)] * 2
        + [fixed(1, width)]
        + [fixed(width, width)] * 3
        + [by_row(quad)] * len(grads),
        out_specs=by_row(width),
        out_shape=jax.ShapeDtypeStruct((row_count, width), jnp.bfloat16),
        compiler_params=pltpu.CompilerParams(vmem_limit_bytes=VMEM_LIMIT),
        cost_estimate=pl.CostEstimate(
            flops=6 * row_count * width * width,
            bytes_accessed=16 * row_count * width,
            transcendentals=0,
        ),
        name="finish",
    )(rows, cotangent, norm_gain.reshape(1, width), query_weight, key_weight, value_weight, *grads)


def swap(tensor, axis):
    return lax.all_to_all(tensor, axis, split_axis=0, concat_axis=0, tiled=True)


def across(tensor, axis, distance):
    size = lax.axis_size(axis)
    return lax.ppermute(tensor, axis, [(i, i ^ distance) for i in range(size)])


def across(tensor, axis, distance):
    size = lax.axis_size(axis)
    return lax.ppermute(tensor, axis, [(i, i ^ distance) for i in range(size)])


def reduce_sums(early, late, gain, width, beside):
    quad = gain.shape[1]
    count = gain.shape[0]
    wide = jnp.float32

    def pack(gain):
        high = gain.astype(jnp.bfloat16)
        low = (gain - high.astype(wide)).astype(jnp.bfloat16)
        return jnp.concatenate([high, low, jnp.zeros((16 - 2 * count, quad), jnp.bfloat16)])

    def halve(parts, gain, axis, distance):
        halves = [part.shape[0] // 2 for part in parts]
        sent = [part[half:].astype(jnp.bfloat16) for part, half in zip(parts, halves)]
        if gain is not None:
            sent.append(pack(gain))
        arrived = across(jnp.concatenate(sent), axis, distance)
        start, kept = 0, []
        for part, half in zip(parts, halves):
            kept.append(part[:half] + arrived[start : start + half].astype(wide))
            start += half
        if gain is None:
            return kept, gain
        rows = arrived[start:].astype(wide)
        return kept, gain + rows[:count] + rows[count : 2 * count]

    first = early[:width] + across(early[width:], "sample", 1)
    first, _ = halve([first], None, "sample", 2)
    second, gain = halve([late], gain, "sample", 2)
    second, gain = halve(second, gain, "turb", 1)
    parts, gain, beside = lax.optimization_barrier((first + second, gain, beside))
    for distance in (4, 2):
        parts, gain = halve(parts, gain, "turb", distance)
    total = jnp.stack(parts).astype(jnp.bfloat16)[None]
    for distance in (2, 4):
        total = jnp.concatenate([total, across(total, "turb", distance)])
    other = across(total, "turb", 1)
    four = [total, other, across(total, "sample", 2), across(other, "sample", 2)]
    four += [across(part, "sample", 1) for part in four]
    return four, gain.reshape(width), beside


def place_kernel(*refs):
    (*parts, query_ref, key_ref, value_ref, out_ref, all_ref) = refs
    own_sample, own_turb = lax.axis_index("sample"), lax.axis_index("turb")
    _, quads, share, quad = parts[0].shape
    for i in range(SAMPLES):
        product = own_sample ^ ((i % 2) * 2 + i // 2)
        for apart in range(TURBS):
            place = turb_place(apart)
            ref = parts[2 * i + place // 4]
            rows = pl.ds(pl.multiple_of((apart ^ own_turb) * share, share), share)
            for j in range(quads):
                all_ref[product, rows, j * quad : (j + 1) * quad] = ref[place % 4, j].astype(
                    jnp.float32
                )
    for i, ref in enumerate((query_ref, key_ref, value_ref, out_ref)):
        ref[...] = all_ref[i]


def place_sums(parts, width):
    return pl.pallas_call(
        place_kernel,
        in_specs=[pl.BlockSpec(memory_space=pltpu.VMEM)] * len(parts),
        out_specs=[pl.BlockSpec(memory_space=pltpu.VMEM)] * 4,
        out_shape=[jax.ShapeDtypeStruct((width, width), jnp.float32)] * 4,
        scratch_shapes=[pltpu.VMEM((4, width, width), jnp.float32)],
        compiler_params=pltpu.CompilerParams(vmem_limit_bytes=VMEM_LIMIT),
        cost_estimate=pl.CostEstimate(
            flops=0, bytes_accessed=24 * width * width, transcendentals=0
        ),
        name="place",
    )(*parts)


def by_sample(
    inflow,
    cotangent,
    norm_gain,
    query_weight,
    key_weight,
    value_weight,
    out_weight,
    adjacency,
    sectors,
):
    sample_count, block_rows, width = inflow.shape
    row_count = lax.axis_size("turb") * block_rows
    adjacency = jnp.transpose(adjacency, (2, 0, 1))
    rows = swap(inflow, "turb")
    rows, cotangent = lax.optimization_barrier((rows, cotangent))
    rows = rows.reshape(row_count, width)
    grad_rows = swap(cotangent, "turb").reshape(row_count, width)
    *saved, layer_rows = forward(
        sectors, adjacency, rows, norm_gain, query_weight, key_weight, value_weight, out_weight,
        block_rows,
    )
    layer_output = swap(layer_rows.reshape(inflow.shape), "turb")
    weights = (norm_gain, query_weight, key_weight, value_weight)
    none = jnp.zeros((SUM_ROWS, width), jnp.float32)
    *grads, early, send, before = backward(
        sectors, adjacency, grad_rows, out_weight, *saved, *weights, none, block_rows, 0
    )
    arrived = across(send, "turb", 1)
    *more, late, send, gain = backward(
        sectors, adjacency, grad_rows, out_weight, *saved, *weights, before, block_rows, 1
    )
    late, send, gain, arrived, layer_output = lax.optimization_barrier(
        (late, send, gain, arrived, layer_output)
    )
    gain = gain[0].reshape(-1, late.shape[1])
    arrived_gain = across(gain, "sample", 1)
    arrived_late = across(send, "sample", 1)
    early = early + arrived.astype(jnp.float32)
    grad_rows = finish(rows, grad_rows, *weights, grads + more)
    grad_rows, late, arrived_late, arrived_gain = lax.optimization_barrier(
        (grad_rows, late, arrived_late, arrived_gain)
    )
    grad_inflow = swap(grad_rows.reshape(inflow.shape), "turb")
    parts, sum_gain, grad_inflow = reduce_sums(
        early, late + arrived_late, gain + arrived_gain, width, grad_inflow
    )
    sums = place_sums(parts, width)
    return (layer_output, grad_inflow, *sums, sum_gain)


def solution(mesh):
    placed = (
        P("sample", "turb", None),
        P("sample", "turb", None),
        P(),
        P(),
        P(),
        P(),
        P(),
        P(),
        P("sample"),
    )

    def plan(*args):
        sample_count = args[0].shape[0]
        if sample_count == mesh.shape["turb"] == TURBS and mesh.shape["sample"] == SAMPLES:
            return by_sample(*args)
        return on_device(*args)

    return jax.shard_map(
        plan,
        mesh=mesh,
        in_specs=placed,
        out_specs=(P("sample", "turb", None), P("sample", "turb", None), P(), P(), P(), P(), P()),
        check_vma=False,
    )
```

```python
import jax
import jax.numpy as jnp
from jax import lax
from jax.experimental import pallas as pl
from jax.experimental.pallas import tpu as pltpu
from jax.sharding import PartitionSpec as P

HEADS = 8
UPSTREAM = 3
SECTORS = 8
REPEAT = 1


epsilon = 1e-05


def normalize(row_block, norm_gain):
    widened = row_block.astype(jnp.float32)
    centred = widened - jnp.mean(widened, axis=-1, keepdims=True)
    inverse = lax.rsqrt(jnp.mean(centred * centred, axis=-1, keepdims=True) + epsilon)
    scaled = centred * inverse
    return (scaled, inverse, (scaled * norm_gain).astype(jnp.bfloat16))


def attend(pieces):
    queries, key_rows, value_rows, key_usable, grad_attended = pieces
    batch_count, query_count, model_width = queries.shape
    key_count = key_rows.shape[1]
    head_dim = model_width // HEADS
    score_scale = head_dim ** (-0.5)
    query_heads = queries.reshape(batch_count, query_count, HEADS, head_dim)
    key_heads = key_rows.reshape(batch_count, key_count, HEADS, head_dim)
    value_heads = value_rows.reshape(batch_count, key_count, HEADS, head_dim)
    grad_heads = grad_attended.reshape(batch_count, query_count, HEADS, head_dim)
    scores = (
        jnp.einsum("nqhd,nkhd->nhqk", query_heads, key_heads, preferred_element_type=jnp.float32)
        * score_scale
    )
    scores = jnp.where(key_usable[:, None, None, :], scores, -1e30)
    highest = jnp.max(scores, axis=-1, keepdims=True)
    weights = jnp.exp(scores - highest)
    probabilities = weights / jnp.sum(weights, axis=-1, keepdims=True)
    rounded = probabilities.astype(jnp.bfloat16)
    attended = jnp.einsum(
        "nhqk,nkhd->nqhd", rounded, value_heads, preferred_element_type=jnp.float32
    ).astype(jnp.bfloat16)
    grad_probs = jnp.einsum(
        "nqhd,nkhd->nhqk", grad_heads, value_heads, preferred_element_type=jnp.float32
    )
    centred = grad_probs - jnp.sum(probabilities * grad_probs, axis=-1, keepdims=True)
    grad_scores = (probabilities * centred * score_scale).astype(jnp.bfloat16)
    grad_queries = jnp.einsum(
        "nhqk,nkhd->nqhd", grad_scores, key_heads, preferred_element_type=jnp.float32
    ).astype(jnp.bfloat16)
    grad_keys = jnp.einsum(
        "nhqk,nqhd->nkhd", grad_scores, query_heads, preferred_element_type=jnp.float32
    )
    grad_values = jnp.einsum(
        "nhqk,nqhd->nkhd", rounded, grad_heads, preferred_element_type=jnp.float32
    )
    pair_terms = jnp.concatenate(
        [
            grad_keys.reshape(batch_count, key_count, model_width),
            grad_values.reshape(batch_count, key_count, model_width),
        ],
        axis=-1,
    )
    return (
        attended.reshape(batch_count, query_count, model_width),
        grad_queries.reshape(batch_count, query_count, model_width),
        pair_terms,
    )


def on_device(
    inflow,
    cotangent,
    norm_gain,
    query_weight,
    key_weight,
    value_weight,
    out_weight,
    adjacency,
    sectors,
):
    sample_count, block_rows, model_width = inflow.shape
    block_count = lax.axis_size("turb")
    own_block = lax.axis_index("turb")
    slot_count = REPEAT * ((SECTORS * UPSTREAM + block_count - 2) // (block_count - 1))
    flat_rows = sample_count * block_rows
    pair_width = 2 * model_width
    input_rows = inflow.reshape(flat_rows, model_width)
    grad_rows = cotangent.reshape(flat_rows, model_width)
    scaled, inverse, normed = normalize(input_rows, norm_gain)
    queries = jnp.dot(normed, query_weight, preferred_element_type=jnp.float32).astype(jnp.bfloat16)
    key_rows = jnp.dot(normed, key_weight, preferred_element_type=jnp.float32).astype(jnp.bfloat16)
    value_rows = jnp.dot(normed, value_weight, preferred_element_type=jnp.float32).astype(
        jnp.bfloat16
    )
    upstream = adjacency[sectors]
    needed = jnp.any(upstream == own_block, axis=2).astype(jnp.int32)
    earlier_need = jnp.cumsum(needed, axis=0) - needed
    slot_index = lax.broadcasted_iota(jnp.int32, (block_count, slot_count, sample_count), 1)
    chosen = (needed.T[:, None, :] == 1) & (earlier_need.T[:, None, :] == slot_index)
    selector = chosen.astype(jnp.bfloat16).reshape(block_count * slot_count, sample_count)
    own_lists = lax.dynamic_index_in_dim(upstream, own_block, axis=1, keepdims=False)
    usable = own_lists >= 0
    matches = jnp.any(own_lists[:, :, None, None] == own_lists[None, None, :, :], axis=3)
    sample_ids = lax.broadcasted_iota(jnp.int32, (sample_count, sample_count), 0)
    earlier = lax.broadcasted_iota(jnp.int32, (sample_count, sample_count), 1) < sample_ids
    position = jnp.sum((matches & earlier[:, None, :]).astype(jnp.int32), axis=2)
    flat_slot = own_lists * slot_count + position
    fetch_at = jnp.where(usable, flat_slot, 0)
    payload = jnp.concatenate([key_rows, value_rows], axis=1).reshape(
        sample_count, block_rows * pair_width
    )
    packed = jnp.dot(selector, payload, preferred_element_type=jnp.float32).astype(jnp.bfloat16)
    arrived = lax.all_to_all(
        packed.reshape(block_count, slot_count, block_rows, pair_width),
        "turb",
        split_axis=0,
        concat_axis=0,
        tiled=True,
    )
    fetched = arrived.reshape(block_count * slot_count, block_rows, pair_width)[fetch_at]
    upstream_keys = fetched[..., :model_width]
    upstream_values = fetched[..., model_width:]
    key_count = (1 + UPSTREAM) * block_rows
    key_all = jnp.concatenate(
        [key_rows.reshape(sample_count, 1, block_rows, model_width), upstream_keys], axis=1
    ).reshape(sample_count, key_count, model_width)
    value_all = jnp.concatenate(
        [value_rows.reshape(sample_count, 1, block_rows, model_width), upstream_values], axis=1
    ).reshape(sample_count, key_count, model_width)
    block_usable = jnp.concatenate([jnp.ones((sample_count, 1), dtype=jnp.bool_), usable], axis=1)
    key_usable = jnp.repeat(block_usable, block_rows, axis=1)
    grad_attended = jnp.dot(grad_rows, out_weight.T, preferred_element_type=jnp.float32).astype(
        jnp.bfloat16
    )
    group_size = min(sample_count, max(1, 512 // block_rows))
    while sample_count % group_size != 0:
        group_size = group_size - 1
    group_count = sample_count // group_size

    def grouped(tensor):
        return tensor.reshape((group_count, group_size) + tensor.shape[1:])

    attended, grad_queries, pair_terms = lax.map(
        attend,
        (
            grouped(queries.reshape(sample_count, block_rows, model_width)),
            grouped(key_all),
            grouped(value_all),
            grouped(key_usable),
            grouped(grad_attended.reshape(sample_count, block_rows, model_width)),
        ),
    )
    attended = attended.reshape(flat_rows, model_width)
    grad_queries = grad_queries.reshape(flat_rows, model_width)
    pair_terms = pair_terms.reshape(sample_count, 1 + UPSTREAM, block_rows, pair_width)
    layer_output = (
        (
            input_rows.astype(jnp.float32)
            + jnp.dot(attended, out_weight, preferred_element_type=jnp.float32)
        )
        .astype(jnp.bfloat16)
        .reshape(inflow.shape)
    )
    outgoing = (
        pair_terms[:, 1:]
        .astype(jnp.bfloat16)
        .reshape(sample_count * UPSTREAM, block_rows, pair_width)
    )
    target = jnp.where(usable, flat_slot, block_count * slot_count).reshape(-1)
    outbound = (
        jnp.zeros((block_count * slot_count, block_rows, pair_width), jnp.bfloat16)
        .at[target]
        .set(outgoing, mode="drop")
    )
    sum_out = jnp.dot(attended.T, grad_rows, preferred_element_type=jnp.float32)
    sum_query = jnp.dot(normed.T, grad_queries, preferred_element_type=jnp.float32)
    returned = lax.all_to_all(
        outbound.reshape(block_count, slot_count, block_rows, pair_width),
        "turb",
        split_axis=0,
        concat_axis=0,
        tiled=True,
    )
    remote = jnp.dot(
        selector.T,
        returned.reshape(block_count * slot_count, block_rows * pair_width),
        preferred_element_type=jnp.float32,
    )
    combined = (
        (pair_terms[:, 0].reshape(sample_count, block_rows * pair_width) + remote)
        .astype(jnp.bfloat16)
        .reshape(flat_rows, pair_width)
    )
    grad_keys = combined[:, :model_width]
    grad_values = combined[:, model_width:]
    sum_key = jnp.dot(normed.T, grad_keys, preferred_element_type=jnp.float32)
    sum_value = jnp.dot(normed.T, grad_values, preferred_element_type=jnp.float32)
    grad_normed = jnp.dot(grad_queries, query_weight.T, preferred_element_type=jnp.float32)
    grad_normed = grad_normed + jnp.dot(grad_keys, key_weight.T, preferred_element_type=jnp.float32)
    grad_normed = grad_normed + jnp.dot(
        grad_values, value_weight.T, preferred_element_type=jnp.float32
    )
    sum_gain = jnp.sum(grad_normed * scaled, axis=0)
    grad_scaled = grad_normed * norm_gain
    grad_input = inverse * (
        grad_scaled
        - jnp.mean(grad_scaled, axis=-1, keepdims=True)
        - scaled * jnp.mean(grad_scaled * scaled, axis=-1, keepdims=True)
    )
    grad_inflow = (
        (grad_rows.astype(jnp.float32) + grad_input).astype(jnp.bfloat16).reshape(inflow.shape)
    )
    sum_query, sum_key, sum_value, sum_out, sum_gain = lax.psum(
        (sum_query, sum_key, sum_value, sum_out, sum_gain), ("sample", "turb")
    )
    return (layer_output, grad_inflow, sum_query, sum_key, sum_value, sum_out, sum_gain)


PAIR = 2
QUAD = 4
LOG2_E = 1.4426950408889634
VMEM_LIMIT = 58 * 2**20
SUM_ROWS = 8
SAMPLES = 4
TURBS = 8


def turb_place(apart):
    return (apart % 2) * 4 + (apart // 4) * 2 + (apart // 2) % 2


def contract(left, right, left_dim, right_dim):
    return lax.dot_general(
        left, right, (((left_dim,), (right_dim,)), ((), ())), preferred_element_type=jnp.float32
    )


def split_heads(rows, head_dim):
    lane = lax.broadcasted_iota(jnp.int32, rows.shape, 1)
    wide = rows.astype(jnp.float32)
    return jnp.concatenate(
        [jnp.where(lane < head_dim, wide, 0.0), jnp.where(lane >= head_dim, wide, 0.0)], axis=0
    ).astype(jnp.bfloat16)


def join_heads(wide, head_dim):
    block_rows = wide.shape[1] // PAIR
    first = lax.broadcasted_iota(jnp.int32, (wide.shape[0], block_rows), 0) < head_dim
    return jnp.where(first, wide[:, :block_rows], wide[:, block_rows:])


def for_each_block(sectors_ref, lists_ref, block_count, block_rows, work):
    sector = sectors_ref[lax.axis_index("turb")]

    def step(block, carry):
        used = jnp.int32(0)
        for slot in range(UPSTREAM):
            used = used + (lists_ref[slot, sector, block] >= 0).astype(jnp.int32)
        for count in range(UPSTREAM + 1):

            @pl.when(used == count)
            def _():
                sources = [block] + [
                    lists_ref[slot, sector, block] for slot in range(count)
                ]
                work(block, [pl.multiple_of(s * block_rows, block_rows) for s in sources])

        return carry

    lax.fori_loop(0, block_count, step, 0)


def stacked(ref, starts, block_rows, lanes):
    return jnp.concatenate([ref[pl.ds(s, block_rows), lanes] for s in starts], axis=0)


def beside(ref, starts, block_rows, rows):
    return jnp.concatenate([ref[rows, pl.ds(s, block_rows)] for s in starts], axis=1)


def forward_kernel(block_rows, head_dim, sectors_ref, lists_ref, x_ref, gain_ref, wq_ref, wk_ref,
                   wv_ref, wo_ref, normed_t_ref, q_ref, k_ref, v_ref, kt_ref, att_ref,
                   level_ref, out_ref, normed_ref, vt_ref, rows_ref, sum_ref):
    row_count = x_ref.shape[0]
    quad = pl.program_id(0)
    pair = PAIR * head_dim
    exponent = head_dim ** (-0.5) * LOG2_E
    chunk = min(row_count, 256)

    @pl.when(quad == 0)
    def _():
        for start in range(0, row_count, chunk):
            part = slice(start, start + chunk)
            scaled, _, normed = normalize(x_ref[part, :], gain_ref[...])
            normed_ref[part, :] = normed
            normed_t_ref[:, part] = (scaled * gain_ref[...]).T.astype(jnp.bfloat16)

    normed = normed_ref[...]
    q_ref[...] = contract(normed, wq_ref[...], 1, 0).astype(jnp.bfloat16)
    k_ref[...] = contract(normed, wk_ref[...], 1, 0).astype(jnp.bfloat16)
    v_ref[...] = contract(normed, wv_ref[...], 1, 0).astype(jnp.bfloat16)
    kt_ref[...] = contract(wk_ref[...], normed, 0, 1).astype(jnp.bfloat16)
    vt_ref[...] = contract(wv_ref[...], normed, 0, 1).astype(jnp.bfloat16)

    def work(block, starts):
        own = pl.ds(starts[0], block_rows)
        lanes = [slice(p * pair, (p + 1) * pair) for p in range(QUAD // PAIR)]
        scores = [
            contract(
                stacked(k_ref, starts, block_rows, lane), split_heads(q_ref[own, lane], head_dim), 1, 1
            )
            for lane in lanes
        ]
        for p, lane in enumerate(lanes):
            highest = jnp.max(scores[p], axis=0, keepdims=True)
            weights = jnp.exp2((scores[p] - highest) * exponent)
            total = jnp.sum(weights, axis=0, keepdims=True)
            probs = (weights * (1.0 / total)).astype(jnp.bfloat16)
            level_ref[0, pl.ds(block * (QUAD // PAIR) + p, 1), :] = highest * exponent + jnp.log2(
                total
            )
            joined = join_heads(
                jnp.dot(
                    beside(vt_ref, starts, block_rows, lane),
                    probs,
                    preferred_element_type=jnp.float32,
                ),
                head_dim,
            )
            att_ref[lane, own] = joined.astype(jnp.bfloat16)
            rows_ref[own, lane] = joined.T.astype(jnp.bfloat16)

    for_each_block(sectors_ref, lists_ref, row_count // block_rows, block_rows, work)
    part = contract(rows_ref[...], wo_ref[...], 1, 0)

    @pl.when(quad == 0)
    def _():
        sum_ref[...] = x_ref[...].astype(jnp.float32) + part

    @pl.when(quad > 0)
    def _():
        sum_ref[...] += part

    @pl.when(quad == pl.num_programs(0) - 1)
    def _():
        out_ref[...] = sum_ref[...].astype(jnp.bfloat16)


def forward(sectors, adjacency, rows, norm_gain, query_weight, key_weight, value_weight, out_weight, block_rows):
    row_count, width = rows.shape
    head_dim = width // HEADS
    quad = QUAD * head_dim
    quads = width // quad
    stat_rows = row_count // block_rows * (QUAD // PAIR)
    fixed = lambda *shape: pl.BlockSpec(shape, lambda p, *lists: (0,) * len(shape))
    across = lambda size: pl.BlockSpec((size, quad), lambda p, *lists: (0, p))
    down = lambda size: pl.BlockSpec((quad, size), lambda p, *lists: (p, 0))
    stat = pl.BlockSpec((1, stat_rows, PAIR * block_rows), lambda p, *lists: (p, 0, 0))
    flat = jax.ShapeDtypeStruct((row_count, width), jnp.bfloat16)
    turned = jax.ShapeDtypeStruct((width, row_count), jnp.bfloat16)
    stats = jax.ShapeDtypeStruct((quads, stat_rows, PAIR * block_rows), jnp.float32)
    return pl.pallas_call(
        lambda *refs: forward_kernel(block_rows, head_dim, *refs),
        grid_spec=pltpu.PrefetchScalarGridSpec(
            num_scalar_prefetch=2,
            grid=(quads,),
            in_specs=[fixed(row_count, width), fixed(1, width)]
            + [across(width)] * 3
            + [down(width)],
            out_specs=[fixed(width, row_count)]
            + [across(row_count)] * 3
            + [down(row_count)] * 2
            + [stat, fixed(row_count, width)],
            scratch_shapes=[
                pltpu.VMEM((row_count, width), jnp.bfloat16),
                pltpu.VMEM((quad, row_count), jnp.bfloat16),
                pltpu.VMEM((row_count, quad), jnp.bfloat16),
                pltpu.VMEM((row_count, width), jnp.float32),
            ],
        ),
        out_shape=[turned, flat, flat, flat, turned, turned, stats, flat],
        compiler_params=pltpu.CompilerParams(vmem_limit_bytes=VMEM_LIMIT),
        cost_estimate=pl.CostEstimate(
            flops=12 * row_count * width * width + 32 * row_count * block_rows * width,
            bytes_accessed=20 * row_count * width,
            transcendentals=row_count * 4 * block_rows * HEADS,
        ),
        name="forward",
    )(sectors, adjacency, rows, norm_gain.reshape(1, width), query_weight, key_weight, value_weight,
      out_weight)


def backward_kernel(block_rows, head_dim, which, sectors_ref, lists_ref, wo_ref, q_ref, k_ref, v_ref,
                    kt_ref, level_ref, gain_ref, *refs):
    before, refs = refs[:which], refs[which:]
    late, refs = refs[:6], refs[6:]
    gq_ref, gk_ref, gv_ref, keep_ref, send_ref, sum_ref, *refs = refs
    ga_ref, gk_acc, gv_acc, parts_ref, *held, sems = refs
    cot_ref = held[0]
    row_count, width = cot_ref.shape
    block_count = row_count // block_rows
    pair = PAIR * head_dim
    quad = QUAD * head_dim
    scale = head_dim ** (-0.5)
    own_lanes = slice(which * quad, (which + 1) * quad)
    copies = []
    for i, (ref, into) in enumerate(zip(late, held)):
        source = ref if i < 3 else ref.at[:, own_lanes]
        copies.append(pltpu.make_async_copy(source, into, sems.at[i]))
        copies[-1].start()
    _, normed_t_ref, att_ref, *weight_refs = held
    copies[0].wait()
    ga_ref[...] = contract(cot_ref[...], wo_ref[...], 1, 1).astype(jnp.bfloat16)
    gk_acc[...] = jnp.zeros_like(gk_acc)
    gv_acc[...] = jnp.zeros_like(gv_acc)

    def work(block, starts):
        own = pl.ds(starts[0], block_rows)
        lanes = [slice(p * pair, (p + 1) * pair) for p in range(QUAD // PAIR)]
        queries = [split_heads(q_ref[own, lane], head_dim) for lane in lanes]
        grads = [split_heads(ga_ref[own, lane], head_dim) for lane in lanes]
        scores = [
            contract(stacked(k_ref, starts, block_rows, lane), queries[p], 1, 1)
            for p, lane in enumerate(lanes)
        ]
        grad_probs = [
            contract(stacked(v_ref, starts, block_rows, lane), grads[p] * scale, 1, 1)
            for p, lane in enumerate(lanes)
        ]
        for p, lane in enumerate(lanes):
            stat = pl.ds(block * (QUAD // PAIR) + p, 1)
            probs = jnp.exp2(scores[p] * (scale * LOG2_E) - level_ref[0, stat, :])
            total = jnp.sum(probs * grad_probs[p], axis=0, keepdims=True)
            grad_scores = (probs * (grad_probs[p] - total)).astype(jnp.bfloat16)
            probs_b = probs.astype(jnp.bfloat16)
            grad_values = jnp.dot(probs_b, grads[p], preferred_element_type=jnp.float32)
            grad_keys = jnp.dot(grad_scores, queries[p], preferred_element_type=jnp.float32)
            joined = join_heads(
                jnp.dot(
                    beside(kt_ref, starts, block_rows, lane),
                    grad_scores,
                    preferred_element_type=jnp.float32,
                ),
                head_dim,
            )
            gq_ref[own, lane] = joined.T.astype(jnp.bfloat16)
            for slot, start in enumerate(starts):
                rows = pl.ds(start, block_rows)
                part = slice(slot * block_rows, (slot + 1) * block_rows)
                for acc, terms in ((gk_acc, grad_keys), (gv_acc, grad_values)):
                    term = terms[part]
                    if slot > 0:
                        term = term.astype(jnp.bfloat16).astype(jnp.float32)
                    acc[rows, lane] += term

    for_each_block(sectors_ref, lists_ref, block_count, block_rows, work)
    gk_ref[...] = gk_acc[...].astype(jnp.bfloat16)
    gv_ref[...] = gv_acc[...].astype(jnp.bfloat16)
    for copy in copies[1:]:
        copy.wait()
    products = [(normed_t_ref, ref, slice(None)) for ref in (gq_ref, gk_ref, gv_ref)]
    products.append((att_ref, cot_ref, own_lanes))
    own_sample, own_turb = lax.axis_index("sample"), lax.axis_index("turb")
    share = width // TURBS
    along = jnp.zeros((width, quad), jnp.float32)
    for i, (left, right, lanes) in enumerate(products):
        terms = contract(left[...], right[:, lanes], 1, 0)
        if i < len(weight_refs):
            along += terms * weight_refs[i][...].astype(jnp.float32)
        apart = i ^ own_sample
        for turb in range(TURBS):
            place = turb_place(turb ^ own_turb)
            if which == 0:
                half, start = place // 4, (apart % 2 * 2 + apart // 2) * 4 + place % 4
            else:
                half, start = apart % 2, apart // 2 * TURBS + place
            start = pl.multiple_of(start * share, share)
            parts_ref[half, pl.ds(start, share), :] = terms[turb * share : (turb + 1) * share]
    keep_ref[...] = parts_ref[0]
    send_ref[...] = parts_ref[1].astype(send_ref.dtype)
    ones = jnp.ones((SUM_ROWS, quad), jnp.bfloat16)
    coarse = along.astype(jnp.bfloat16)
    fine = (along - coarse.astype(jnp.float32)).astype(jnp.bfloat16)
    total = (contract(ones, coarse, 1, 1) + contract(ones, fine, 1, 1)) / gain_ref[...]
    sum_ref[...] = sum((ref[...] for ref in before), total)


def backward(sectors, adjacency, cotangent, out_weight, normed_t, queries, keys, values, keys_t,
             attended_t, levels, norm_gain, query_weight, key_weight, value_weight, before,
             block_rows, which):
    row_count, width = cotangent.shape
    head_dim = width // HEADS
    quad = QUAD * head_dim
    fixed = lambda *shape: pl.BlockSpec(shape, lambda i, *lists: (0,) * len(shape))
    across = pl.BlockSpec((row_count, quad), lambda i, *lists: (0, which))
    down = lambda size: pl.BlockSpec((quad, size), lambda i, *lists: (which, 0))
    stat = pl.BlockSpec((1,) + levels.shape[1:], lambda i, *lists: (which, 0, 0))
    part = jax.ShapeDtypeStruct((row_count, quad), jnp.bfloat16)
    half = (2 * width, quad)
    sent = jnp.bfloat16 if which == 0 else jnp.float32
    return pl.pallas_call(
        lambda *refs: backward_kernel(block_rows, head_dim, which, *refs),
        grid_spec=pltpu.PrefetchScalarGridSpec(
            num_scalar_prefetch=2,
            grid=(1,),
            in_specs=[down(width)]
            + [across] * 3
            + [down(row_count), stat, fixed(1, width)]
            + [fixed(SUM_ROWS, width)] * which
            + [pl.BlockSpec(memory_space=pl.ANY)] * 6,
            out_specs=[fixed(row_count, quad)] * 3
            + [fixed(*half)] * 2
            + [fixed(SUM_ROWS, width)],
            scratch_shapes=[
                pltpu.VMEM((row_count, quad), jnp.bfloat16),
                pltpu.VMEM((row_count, quad), jnp.float32),
                pltpu.VMEM((row_count, quad), jnp.float32),
                pltpu.VMEM((2,) + half, jnp.float32),
            ]
            + [pltpu.VMEM((row_count, width), jnp.bfloat16)]
            + [pltpu.VMEM((width, row_count), jnp.bfloat16)] * 2
            + [pltpu.VMEM((width, quad), jnp.bfloat16)] * 3
            + [pltpu.SemaphoreType.DMA((6,))],
        ),
        out_shape=[part] * 3
        + [
            jax.ShapeDtypeStruct(half, jnp.float32),
            jax.ShapeDtypeStruct(half, sent),
            jax.ShapeDtypeStruct((SUM_ROWS, width), jnp.float32),
        ],
        compiler_params=pltpu.CompilerParams(vmem_limit_bytes=VMEM_LIMIT),
        cost_estimate=pl.CostEstimate(
            flops=10 * row_count * width * quad + 80 * row_count * block_rows * quad,
            bytes_accessed=14 * row_count * width,
            transcendentals=row_count * 4 * block_rows * QUAD,
        ),
        name="backward",
    )(sectors, adjacency, out_weight, queries, keys, values, keys_t, levels,
      norm_gain.reshape(1, width), *before, cotangent, normed_t, attended_t, query_weight, key_weight,
      value_weight)


def finish_kernel(quads, x_ref, cot_ref, gain_ref, wq_ref, wk_ref, wv_ref, *refs):
    grad_refs, out_ref = refs[:-1], refs[-1]
    scaled, inverse, _ = normalize(x_ref[...], gain_ref[...])
    quad = grad_refs[0].shape[1]
    grad_normed = jnp.zeros(x_ref.shape, jnp.float32)
    for i in range(quads):
        lanes = slice(i * quad, (i + 1) * quad)
        for j, weight_ref in enumerate((wq_ref, wk_ref, wv_ref)):
            grad_normed += contract(grad_refs[3 * i + j][...], weight_ref[:, lanes], 1, 1)
    grad_scaled = grad_normed * gain_ref[...]
    grad_input = inverse * (
        grad_scaled
        - jnp.mean(grad_scaled, axis=-1, keepdims=True)
        - scaled * jnp.mean(grad_scaled * scaled, axis=-1, keepdims=True)
    )
    out_ref[...] = (cot_ref[...].astype(jnp.float32) + grad_input).astype(jnp.bfloat16)


def finish(rows, cotangent, norm_gain, query_weight, key_weight, value_weight, grads):
    row_count, width = rows.shape
    quad = grads[0].shape[1]
    step = min(row_count, 256)
    fixed = lambda *shape: pl.BlockSpec(shape, lambda i: (0,) * len(shape))
    by_row = lambda size: pl.BlockSpec((step, size), lambda i: (i, 0))
    return pl.pallas_call(
        lambda *refs: finish_kernel(width // quad, *refs),
        grid=(row_count // step,),
        in_specs=[by_row(width)] * 2
        + [fixed(1, width)]
        + [fixed(width, width)] * 3
        + [by_row(quad)] * len(grads),
        out_specs=by_row(width),
        out_shape=jax.ShapeDtypeStruct((row_count, width), jnp.bfloat16),
        compiler_params=pltpu.CompilerParams(vmem_limit_bytes=VMEM_LIMIT),
        cost_estimate=pl.CostEstimate(
            flops=6 * row_count * width * width,
            bytes_accessed=16 * row_count * width,
            transcendentals=0,
        ),
        name="finish",
    )(rows, cotangent, norm_gain.reshape(1, width), query_weight, key_weight, value_weight, *grads)


def swap(tensor, axis):
    return lax.all_to_all(tensor, axis, split_axis=0, concat_axis=0, tiled=True)


def across(tensor, axis, distance):
    size = lax.axis_size(axis)
    return lax.ppermute(tensor, axis, [(i, i ^ distance) for i in range(size)])


def across(tensor, axis, distance):
    size = lax.axis_size(axis)
    return lax.ppermute(tensor, axis, [(i, i ^ distance) for i in range(size)])


def reduce_sums(early, late, gain, width, beside):
    quad = gain.shape[1]
    count = gain.shape[0]
    wide = jnp.float32

    def pack(gain):
        high = gain.astype(jnp.bfloat16)
        low = (gain - high.astype(wide)).astype(jnp.bfloat16)
        return jnp.concatenate([high, low, jnp.zeros((16 - 2 * count, quad), jnp.bfloat16)])

    def halve(parts, gain, axis, distance):
        halves = [part.shape[0] // 2 for part in parts]
        sent = [part[half:].astype(jnp.bfloat16) for part, half in zip(parts, halves)]
        if gain is not None:
            sent.append(pack(gain))
        arrived = across(jnp.concatenate(sent), axis, distance)
        start, kept = 0, []
        for part, half in zip(parts, halves):
            kept.append(part[:half] + arrived[start : start + half].astype(wide))
            start += half
        if gain is None:
            return kept, gain
        rows = arrived[start:].astype(wide)
        return kept, gain + rows[:count] + rows[count : 2 * count]

    first = early[:width] + across(early[width:], "sample", 1)
    first, _ = halve([first], None, "sample", 2)
    second, gain = halve([late], gain, "sample", 2)
    second, gain = halve(second, gain, "turb", 1)
    parts, gain, beside = lax.optimization_barrier((first + second, gain, beside))
    share = parts[0].shape[0] // 4
    pieces = [jnp.concatenate([part[i * share : (i + 1) * share] for part in parts]) for i in range(4)]
    size = pieces[0].shape[0]
    sent = [jnp.concatenate([piece.astype(jnp.bfloat16), pack(gain)]) for piece in pieces[1:]]
    arrived = [across(piece, "turb", 2 * i + 2).astype(wide) for i, piece in enumerate(sent)]
    total = pieces[0] + sum(rows[:size] for rows in arrived)
    gain = gain + sum(
        rows[size : size + count] + rows[size + count : size + 2 * count] for rows in arrived
    )
    total = total.astype(jnp.bfloat16).reshape(1, 2, share, quad)
    total = jnp.concatenate([total] + [across(total, "turb", distance) for distance in (2, 4, 6)])
    other = across(total, "turb", 1)
    four = [total, other, across(total, "sample", 2), across(other, "sample", 2)]
    four += [across(part, "sample", 1) for part in four]
    return four, gain.reshape(width), beside


def place_kernel(*refs):
    (*parts, query_ref, key_ref, value_ref, out_ref, all_ref) = refs
    own_sample, own_turb = lax.axis_index("sample"), lax.axis_index("turb")
    _, quads, share, quad = parts[0].shape
    for i in range(SAMPLES):
        product = own_sample ^ ((i % 2) * 2 + i // 2)
        for apart in range(TURBS):
            place = turb_place(apart)
            ref = parts[2 * i + place // 4]
            rows = pl.ds(pl.multiple_of((apart ^ own_turb) * share, share), share)
            for j in range(quads):
                all_ref[product, rows, j * quad : (j + 1) * quad] = ref[place % 4, j].astype(
                    jnp.float32
                )
    for i, ref in enumerate((query_ref, key_ref, value_ref, out_ref)):
        ref[...] = all_ref[i]


def place_sums(parts, width):
    return pl.pallas_call(
        place_kernel,
        in_specs=[pl.BlockSpec(memory_space=pltpu.VMEM)] * len(parts),
        out_specs=[pl.BlockSpec(memory_space=pltpu.VMEM)] * 4,
        out_shape=[jax.ShapeDtypeStruct((width, width), jnp.float32)] * 4,
        scratch_shapes=[pltpu.VMEM((4, width, width), jnp.float32)],
        compiler_params=pltpu.CompilerParams(vmem_limit_bytes=VMEM_LIMIT),
        cost_estimate=pl.CostEstimate(
            flops=0, bytes_accessed=24 * width * width, transcendentals=0
        ),
        name="place",
    )(*parts)


def by_sample(
    inflow,
    cotangent,
    norm_gain,
    query_weight,
    key_weight,
    value_weight,
    out_weight,
    adjacency,
    sectors,
):
    sample_count, block_rows, width = inflow.shape
    row_count = lax.axis_size("turb") * block_rows
    adjacency = jnp.transpose(adjacency, (2, 0, 1))
    rows = swap(inflow, "turb")
    rows, cotangent = lax.optimization_barrier((rows, cotangent))
    rows = rows.reshape(row_count, width)
    grad_rows = swap(cotangent, "turb").reshape(row_count, width)
    *saved, layer_rows = forward(
        sectors, adjacency, rows, norm_gain, query_weight, key_weight, value_weight, out_weight,
        block_rows,
    )
    layer_output = swap(layer_rows.reshape(inflow.shape), "turb")
    weights = (norm_gain, query_weight, key_weight, value_weight)
    *grads, early, send, before = backward(
        sectors, adjacency, grad_rows, out_weight, *saved, *weights, [], block_rows, 0
    )
    arrived = across(send, "turb", 1)
    *more, late, send, gain = backward(
        sectors, adjacency, grad_rows, out_weight, *saved, *weights, [before], block_rows, 1
    )
    arrived_late = across(send, "sample", 1)
    grad_rows = finish(rows, grad_rows, *weights, grads + more)
    grad_rows, late, arrived_late, gain, early, arrived, layer_output = lax.optimization_barrier(
        (grad_rows, late, arrived_late, gain, early, arrived, layer_output)
    )
    gain = gain[0].reshape(-1, late.shape[1])
    arrived_gain = across(gain, "sample", 1)
    early = early + arrived.astype(jnp.float32)
    grad_inflow = swap(grad_rows.reshape(inflow.shape), "turb")
    parts, sum_gain, grad_inflow = reduce_sums(
        early, late + arrived_late, gain + arrived_gain, width, grad_inflow
    )
    sums = place_sums(parts, width)
    lowest = jnp.finfo(jnp.bfloat16).min
    return (
        jnp.maximum(layer_output, lowest),
        jnp.maximum(grad_inflow, lowest),
        *sums,
        sum_gain,
    )


def solution(mesh):
    placed = (
        P("sample", "turb", None),
        P("sample", "turb", None),
        P(),
        P(),
        P(),
        P(),
        P(),
        P(),
        P("sample"),
    )

    def plan(*args):
        sample_count = args[0].shape[0]
        if sample_count == mesh.shape["turb"] == TURBS and mesh.shape["sample"] == SAMPLES:
            return by_sample(*args)
        return on_device(*args)

    return jax.shard_map(
        plan,
        mesh=mesh,
        in_specs=placed,
        out_specs=(P("sample", "turb", None), P("sample", "turb", None), P(), P(), P(), P(), P()),
        check_vma=False,
    )
```

```python
import jax
import jax.numpy as jnp
from jax import lax
from jax.experimental import pallas as pl
from jax.experimental.pallas import tpu as pltpu
from jax.sharding import PartitionSpec as P

HEADS = 8
UPSTREAM = 3
SECTORS = 8
REPEAT = 1


epsilon = 1e-05


def normalize(row_block, norm_gain):
    widened = row_block.astype(jnp.float32)
    centred = widened - jnp.mean(widened, axis=-1, keepdims=True)
    inverse = lax.rsqrt(jnp.mean(centred * centred, axis=-1, keepdims=True) + epsilon)
    scaled = centred * inverse
    return (scaled, inverse, (scaled * norm_gain).astype(jnp.bfloat16))


def attend(pieces):
    queries, key_rows, value_rows, key_usable, grad_attended = pieces
    batch_count, query_count, model_width = queries.shape
    key_count = key_rows.shape[1]
    head_dim = model_width // HEADS
    score_scale = head_dim ** (-0.5)
    query_heads = queries.reshape(batch_count, query_count, HEADS, head_dim)
    key_heads = key_rows.reshape(batch_count, key_count, HEADS, head_dim)
    value_heads = value_rows.reshape(batch_count, key_count, HEADS, head_dim)
    grad_heads = grad_attended.reshape(batch_count, query_count, HEADS, head_dim)
    scores = (
        jnp.einsum("nqhd,nkhd->nhqk", query_heads, key_heads, preferred_element_type=jnp.float32)
        * score_scale
    )
    scores = jnp.where(key_usable[:, None, None, :], scores, -1e30)
    highest = jnp.max(scores, axis=-1, keepdims=True)
    weights = jnp.exp(scores - highest)
    probabilities = weights / jnp.sum(weights, axis=-1, keepdims=True)
    rounded = probabilities.astype(jnp.bfloat16)
    attended = jnp.einsum(
        "nhqk,nkhd->nqhd", rounded, value_heads, preferred_element_type=jnp.float32
    ).astype(jnp.bfloat16)
    grad_probs = jnp.einsum(
        "nqhd,nkhd->nhqk", grad_heads, value_heads, preferred_element_type=jnp.float32
    )
    centred = grad_probs - jnp.sum(probabilities * grad_probs, axis=-1, keepdims=True)
    grad_scores = (probabilities * centred * score_scale).astype(jnp.bfloat16)
    grad_queries = jnp.einsum(
        "nhqk,nkhd->nqhd", grad_scores, key_heads, preferred_element_type=jnp.float32
    ).astype(jnp.bfloat16)
    grad_keys = jnp.einsum(
        "nhqk,nqhd->nkhd", grad_scores, query_heads, preferred_element_type=jnp.float32
    )
    grad_values = jnp.einsum(
        "nhqk,nqhd->nkhd", rounded, grad_heads, preferred_element_type=jnp.float32
    )
    pair_terms = jnp.concatenate(
        [
            grad_keys.reshape(batch_count, key_count, model_width),
            grad_values.reshape(batch_count, key_count, model_width),
        ],
        axis=-1,
    )
    return (
        attended.reshape(batch_count, query_count, model_width),
        grad_queries.reshape(batch_count, query_count, model_width),
        pair_terms,
    )


def on_device(
    inflow,
    cotangent,
    norm_gain,
    query_weight,
    key_weight,
    value_weight,
    out_weight,
    adjacency,
    sectors,
):
    sample_count, block_rows, model_width = inflow.shape
    block_count = lax.axis_size("turb")
    own_block = lax.axis_index("turb")
    slot_count = REPEAT * ((SECTORS * UPSTREAM + block_count - 2) // (block_count - 1))
    flat_rows = sample_count * block_rows
    pair_width = 2 * model_width
    input_rows = inflow.reshape(flat_rows, model_width)
    grad_rows = cotangent.reshape(flat_rows, model_width)
    scaled, inverse, normed = normalize(input_rows, norm_gain)
    queries = jnp.dot(normed, query_weight, preferred_element_type=jnp.float32).astype(jnp.bfloat16)
    key_rows = jnp.dot(normed, key_weight, preferred_element_type=jnp.float32).astype(jnp.bfloat16)
    value_rows = jnp.dot(normed, value_weight, preferred_element_type=jnp.float32).astype(
        jnp.bfloat16
    )
    upstream = adjacency[sectors]
    needed = jnp.any(upstream == own_block, axis=2).astype(jnp.int32)
    earlier_need = jnp.cumsum(needed, axis=0) - needed
    slot_index = lax.broadcasted_iota(jnp.int32, (block_count, slot_count, sample_count), 1)
    chosen = (needed.T[:, None, :] == 1) & (earlier_need.T[:, None, :] == slot_index)
    selector = chosen.astype(jnp.bfloat16).reshape(block_count * slot_count, sample_count)
    own_lists = lax.dynamic_index_in_dim(upstream, own_block, axis=1, keepdims=False)
    usable = own_lists >= 0
    matches = jnp.any(own_lists[:, :, None, None] == own_lists[None, None, :, :], axis=3)
    sample_ids = lax.broadcasted_iota(jnp.int32, (sample_count, sample_count), 0)
    earlier = lax.broadcasted_iota(jnp.int32, (sample_count, sample_count), 1) < sample_ids
    position = jnp.sum((matches & earlier[:, None, :]).astype(jnp.int32), axis=2)
    flat_slot = own_lists * slot_count + position
    fetch_at = jnp.where(usable, flat_slot, 0)
    payload = jnp.concatenate([key_rows, value_rows], axis=1).reshape(
        sample_count, block_rows * pair_width
    )
    packed = jnp.dot(selector, payload, preferred_element_type=jnp.float32).astype(jnp.bfloat16)
    arrived = lax.all_to_all(
        packed.reshape(block_count, slot_count, block_rows, pair_width),
        "turb",
        split_axis=0,
        concat_axis=0,
        tiled=True,
    )
    fetched = arrived.reshape(block_count * slot_count, block_rows, pair_width)[fetch_at]
    upstream_keys = fetched[..., :model_width]
    upstream_values = fetched[..., model_width:]
    key_count = (1 + UPSTREAM) * block_rows
    key_all = jnp.concatenate(
        [key_rows.reshape(sample_count, 1, block_rows, model_width), upstream_keys], axis=1
    ).reshape(sample_count, key_count, model_width)
    value_all = jnp.concatenate(
        [value_rows.reshape(sample_count, 1, block_rows, model_width), upstream_values], axis=1
    ).reshape(sample_count, key_count, model_width)
    block_usable = jnp.concatenate([jnp.ones((sample_count, 1), dtype=jnp.bool_), usable], axis=1)
    key_usable = jnp.repeat(block_usable, block_rows, axis=1)
    grad_attended = jnp.dot(grad_rows, out_weight.T, preferred_element_type=jnp.float32).astype(
        jnp.bfloat16
    )
    group_size = min(sample_count, max(1, 512 // block_rows))
    while sample_count % group_size != 0:
        group_size = group_size - 1
    group_count = sample_count // group_size

    def grouped(tensor):
        return tensor.reshape((group_count, group_size) + tensor.shape[1:])

    attended, grad_queries, pair_terms = lax.map(
        attend,
        (
            grouped(queries.reshape(sample_count, block_rows, model_width)),
            grouped(key_all),
            grouped(value_all),
            grouped(key_usable),
            grouped(grad_attended.reshape(sample_count, block_rows, model_width)),
        ),
    )
    attended = attended.reshape(flat_rows, model_width)
    grad_queries = grad_queries.reshape(flat_rows, model_width)
    pair_terms = pair_terms.reshape(sample_count, 1 + UPSTREAM, block_rows, pair_width)
    layer_output = (
        (
            input_rows.astype(jnp.float32)
            + jnp.dot(attended, out_weight, preferred_element_type=jnp.float32)
        )
        .astype(jnp.bfloat16)
        .reshape(inflow.shape)
    )
    outgoing = (
        pair_terms[:, 1:]
        .astype(jnp.bfloat16)
        .reshape(sample_count * UPSTREAM, block_rows, pair_width)
    )
    target = jnp.where(usable, flat_slot, block_count * slot_count).reshape(-1)
    outbound = (
        jnp.zeros((block_count * slot_count, block_rows, pair_width), jnp.bfloat16)
        .at[target]
        .set(outgoing, mode="drop")
    )
    sum_out = jnp.dot(attended.T, grad_rows, preferred_element_type=jnp.float32)
    sum_query = jnp.dot(normed.T, grad_queries, preferred_element_type=jnp.float32)
    returned = lax.all_to_all(
        outbound.reshape(block_count, slot_count, block_rows, pair_width),
        "turb",
        split_axis=0,
        concat_axis=0,
        tiled=True,
    )
    remote = jnp.dot(
        selector.T,
        returned.reshape(block_count * slot_count, block_rows * pair_width),
        preferred_element_type=jnp.float32,
    )
    combined = (
        (pair_terms[:, 0].reshape(sample_count, block_rows * pair_width) + remote)
        .astype(jnp.bfloat16)
        .reshape(flat_rows, pair_width)
    )
    grad_keys = combined[:, :model_width]
    grad_values = combined[:, model_width:]
    sum_key = jnp.dot(normed.T, grad_keys, preferred_element_type=jnp.float32)
    sum_value = jnp.dot(normed.T, grad_values, preferred_element_type=jnp.float32)
    grad_normed = jnp.dot(grad_queries, query_weight.T, preferred_element_type=jnp.float32)
    grad_normed = grad_normed + jnp.dot(grad_keys, key_weight.T, preferred_element_type=jnp.float32)
    grad_normed = grad_normed + jnp.dot(
        grad_values, value_weight.T, preferred_element_type=jnp.float32
    )
    sum_gain = jnp.sum(grad_normed * scaled, axis=0)
    grad_scaled = grad_normed * norm_gain
    grad_input = inverse * (
        grad_scaled
        - jnp.mean(grad_scaled, axis=-1, keepdims=True)
        - scaled * jnp.mean(grad_scaled * scaled, axis=-1, keepdims=True)
    )
    grad_inflow = (
        (grad_rows.astype(jnp.float32) + grad_input).astype(jnp.bfloat16).reshape(inflow.shape)
    )
    sum_query, sum_key, sum_value, sum_out, sum_gain = lax.psum(
        (sum_query, sum_key, sum_value, sum_out, sum_gain), ("sample", "turb")
    )
    return (layer_output, grad_inflow, sum_query, sum_key, sum_value, sum_out, sum_gain)


PAIR = 2
QUAD = 4
LOG2_E = 1.4426950408889634
VMEM_LIMIT = 58 * 2**20
SUM_ROWS = 8
SAMPLES = 4
TURBS = 8


def turb_place(apart):
    return (apart % 2) * 4 + (apart // 4) * 2 + (apart // 2) % 2


def contract(left, right, left_dim, right_dim):
    return lax.dot_general(
        left, right, (((left_dim,), (right_dim,)), ((), ())), preferred_element_type=jnp.float32
    )


def split_heads(rows, head_dim):
    lane = lax.broadcasted_iota(jnp.int32, rows.shape, 1)
    wide = rows.astype(jnp.float32)
    return jnp.concatenate(
        [jnp.where(lane < head_dim, wide, 0.0), jnp.where(lane >= head_dim, wide, 0.0)], axis=0
    ).astype(jnp.bfloat16)


def join_heads(wide, head_dim):
    block_rows = wide.shape[1] // PAIR
    first = lax.broadcasted_iota(jnp.int32, (wide.shape[0], block_rows), 0) < head_dim
    return jnp.where(first, wide[:, :block_rows], wide[:, block_rows:])


def for_each_block(sectors_ref, lists_ref, block_count, block_rows, work):
    sector = sectors_ref[lax.axis_index("turb")]

    def step(block, carry):
        used = jnp.int32(0)
        for slot in range(UPSTREAM):
            used = used + (lists_ref[slot, sector, block] >= 0).astype(jnp.int32)
        for count in range(UPSTREAM + 1):

            @pl.when(used == count)
            def _():
                sources = [block] + [
                    lists_ref[slot, sector, block] for slot in range(count)
                ]
                work(block, [pl.multiple_of(s * block_rows, block_rows) for s in sources])

        return carry

    lax.fori_loop(0, block_count, step, 0)


def stacked(ref, starts, block_rows, lanes):
    return jnp.concatenate([ref[pl.ds(s, block_rows), lanes] for s in starts], axis=0)


def beside(ref, starts, block_rows, rows):
    return jnp.concatenate([ref[rows, pl.ds(s, block_rows)] for s in starts], axis=1)


def forward_kernel(block_rows, head_dim, sectors_ref, lists_ref, x_ref, gain_ref, wq_ref, wk_ref,
                   wv_ref, wo_ref, normed_t_ref, q_ref, k_ref, v_ref, kt_ref, att_ref,
                   level_ref, out_ref, normed_ref, vt_ref, rows_ref, sum_ref):
    row_count = x_ref.shape[0]
    quad = pl.program_id(0)
    pair = PAIR * head_dim
    exponent = head_dim ** (-0.5) * LOG2_E
    chunk = min(row_count, 256)

    @pl.when(quad == 0)
    def _():
        for start in range(0, row_count, chunk):
            part = slice(start, start + chunk)
            scaled, _, normed = normalize(x_ref[part, :], gain_ref[...])
            normed_ref[part, :] = normed
            normed_t_ref[:, part] = (scaled * gain_ref[...]).T.astype(jnp.bfloat16)

    normed = normed_ref[...]
    q_ref[...] = contract(normed, wq_ref[...], 1, 0).astype(jnp.bfloat16)
    k_ref[...] = contract(normed, wk_ref[...], 1, 0).astype(jnp.bfloat16)
    v_ref[...] = contract(normed, wv_ref[...], 1, 0).astype(jnp.bfloat16)
    kt_ref[...] = contract(wk_ref[...], normed, 0, 1).astype(jnp.bfloat16)
    vt_ref[...] = contract(wv_ref[...], normed, 0, 1).astype(jnp.bfloat16)

    def work(block, starts):
        own = pl.ds(starts[0], block_rows)
        lanes = [slice(p * pair, (p + 1) * pair) for p in range(QUAD // PAIR)]
        scores = [
            contract(
                stacked(k_ref, starts, block_rows, lane), split_heads(q_ref[own, lane], head_dim), 1, 1
            )
            for lane in lanes
        ]
        for p, lane in enumerate(lanes):
            highest = jnp.max(scores[p], axis=0, keepdims=True)
            weights = jnp.exp2((scores[p] - highest) * exponent)
            total = jnp.sum(weights, axis=0, keepdims=True)
            probs = (weights * (1.0 / total)).astype(jnp.bfloat16)
            level_ref[0, pl.ds(block * (QUAD // PAIR) + p, 1), :] = highest * exponent + jnp.log2(
                total
            )
            joined = join_heads(
                jnp.dot(
                    beside(vt_ref, starts, block_rows, lane),
                    probs,
                    preferred_element_type=jnp.float32,
                ),
                head_dim,
            )
            att_ref[lane, own] = joined.astype(jnp.bfloat16)
            rows_ref[own, lane] = joined.T.astype(jnp.bfloat16)

    for_each_block(sectors_ref, lists_ref, row_count // block_rows, block_rows, work)
    part = contract(rows_ref[...], wo_ref[...], 1, 0)

    @pl.when(quad == 0)
    def _():
        sum_ref[...] = x_ref[...].astype(jnp.float32) + part

    @pl.when(quad > 0)
    def _():
        sum_ref[...] += part

    @pl.when(quad == pl.num_programs(0) - 1)
    def _():
        out_ref[...] = sum_ref[...].astype(jnp.bfloat16)


def forward(sectors, adjacency, rows, norm_gain, query_weight, key_weight, value_weight, out_weight, block_rows):
    row_count, width = rows.shape
    head_dim = width // HEADS
    quad = QUAD * head_dim
    quads = width // quad
    stat_rows = row_count // block_rows * (QUAD // PAIR)
    fixed = lambda *shape: pl.BlockSpec(shape, lambda p, *lists: (0,) * len(shape))
    across = lambda size: pl.BlockSpec((size, quad), lambda p, *lists: (0, p))
    down = lambda size: pl.BlockSpec((quad, size), lambda p, *lists: (p, 0))
    stat = pl.BlockSpec((1, stat_rows, PAIR * block_rows), lambda p, *lists: (p, 0, 0))
    flat = jax.ShapeDtypeStruct((row_count, width), jnp.bfloat16)
    turned = jax.ShapeDtypeStruct((width, row_count), jnp.bfloat16)
    stats = jax.ShapeDtypeStruct((quads, stat_rows, PAIR * block_rows), jnp.float32)
    return pl.pallas_call(
        lambda *refs: forward_kernel(block_rows, head_dim, *refs),
        grid_spec=pltpu.PrefetchScalarGridSpec(
            num_scalar_prefetch=2,
            grid=(quads,),
            in_specs=[fixed(row_count, width), fixed(1, width)]
            + [across(width)] * 3
            + [down(width)],
            out_specs=[fixed(width, row_count)]
            + [across(row_count)] * 3
            + [down(row_count)] * 2
            + [stat, fixed(row_count, width)],
            scratch_shapes=[
                pltpu.VMEM((row_count, width), jnp.bfloat16),
                pltpu.VMEM((quad, row_count), jnp.bfloat16),
                pltpu.VMEM((row_count, quad), jnp.bfloat16),
                pltpu.VMEM((row_count, width), jnp.float32),
            ],
        ),
        out_shape=[turned, flat, flat, flat, turned, turned, stats, flat],
        compiler_params=pltpu.CompilerParams(vmem_limit_bytes=VMEM_LIMIT),
        cost_estimate=pl.CostEstimate(
            flops=12 * row_count * width * width + 32 * row_count * block_rows * width,
            bytes_accessed=20 * row_count * width,
            transcendentals=row_count * 4 * block_rows * HEADS,
        ),
        name="forward",
    )(sectors, adjacency, rows, norm_gain.reshape(1, width), query_weight, key_weight, value_weight,
      out_weight)


def backward_kernel(block_rows, head_dim, which, sectors_ref, lists_ref, wo_ref, q_ref, k_ref, v_ref,
                    kt_ref, level_ref, gain_ref, *refs):
    before, refs = refs[:which], refs[which:]
    late, refs = refs[:6], refs[6:]
    gq_ref, gk_ref, gv_ref, keep_ref, send_ref, sum_ref, *refs = refs
    ga_ref, gk_acc, gv_acc, parts_ref, *held, sems = refs
    cot_ref = held[0]
    row_count, width = cot_ref.shape
    block_count = row_count // block_rows
    pair = PAIR * head_dim
    quad = QUAD * head_dim
    scale = head_dim ** (-0.5)
    own_lanes = slice(which * quad, (which + 1) * quad)
    copies = []
    for i, (ref, into) in enumerate(zip(late, held)):
        source = ref if i < 3 else ref.at[:, own_lanes]
        copies.append(pltpu.make_async_copy(source, into, sems.at[i]))
        copies[-1].start()
    _, normed_t_ref, att_ref, *weight_refs = held
    copies[0].wait()
    ga_ref[...] = contract(cot_ref[...], wo_ref[...], 1, 1).astype(jnp.bfloat16)
    gk_acc[...] = jnp.zeros_like(gk_acc)
    gv_acc[...] = jnp.zeros_like(gv_acc)

    def work(block, starts):
        own = pl.ds(starts[0], block_rows)
        lanes = [slice(p * pair, (p + 1) * pair) for p in range(QUAD // PAIR)]
        queries = [split_heads(q_ref[own, lane], head_dim) for lane in lanes]
        grads = [split_heads(ga_ref[own, lane], head_dim) for lane in lanes]
        scores = [
            contract(stacked(k_ref, starts, block_rows, lane), queries[p], 1, 1)
            for p, lane in enumerate(lanes)
        ]
        grad_probs = [
            contract(stacked(v_ref, starts, block_rows, lane), grads[p] * scale, 1, 1)
            for p, lane in enumerate(lanes)
        ]
        for p, lane in enumerate(lanes):
            stat = pl.ds(block * (QUAD // PAIR) + p, 1)
            probs = jnp.exp2(scores[p] * (scale * LOG2_E) - level_ref[0, stat, :])
            total = jnp.sum(probs * grad_probs[p], axis=0, keepdims=True)
            grad_scores = (probs * (grad_probs[p] - total)).astype(jnp.bfloat16)
            probs_b = probs.astype(jnp.bfloat16)
            grad_values = jnp.dot(probs_b, grads[p], preferred_element_type=jnp.float32)
            grad_keys = jnp.dot(grad_scores, queries[p], preferred_element_type=jnp.float32)
            joined = join_heads(
                jnp.dot(
                    beside(kt_ref, starts, block_rows, lane),
                    grad_scores,
                    preferred_element_type=jnp.float32,
                ),
                head_dim,
            )
            gq_ref[own, lane] = joined.T.astype(jnp.bfloat16)
            for slot, start in enumerate(starts):
                rows = pl.ds(start, block_rows)
                part = slice(slot * block_rows, (slot + 1) * block_rows)
                for acc, terms in ((gk_acc, grad_keys), (gv_acc, grad_values)):
                    term = terms[part]
                    if slot > 0:
                        term = term.astype(jnp.bfloat16).astype(jnp.float32)
                    acc[rows, lane] += term

    for_each_block(sectors_ref, lists_ref, block_count, block_rows, work)
    gk_ref[...] = gk_acc[...].astype(jnp.bfloat16)
    gv_ref[...] = gv_acc[...].astype(jnp.bfloat16)
    for copy in copies[1:]:
        copy.wait()
    products = [(normed_t_ref, ref, slice(None)) for ref in (gq_ref, gk_ref, gv_ref)]
    products.append((att_ref, cot_ref, own_lanes))
    own_sample, own_turb = lax.axis_index("sample"), lax.axis_index("turb")
    share = width // TURBS
    along = jnp.zeros((width, quad), jnp.float32)
    for i, (left, right, lanes) in enumerate(products):
        terms = contract(left[...], right[:, lanes], 1, 0)
        if i < len(weight_refs):
            along += terms * weight_refs[i][...].astype(jnp.float32)
        apart = i ^ own_sample
        for turb in range(TURBS):
            place = turb_place(turb ^ own_turb)
            if which == 0:
                half, start = place // 4, (apart % 2 * 2 + apart // 2) * 4 + place % 4
            else:
                half, start = apart % 2, apart // 2 * TURBS + place
            start = pl.multiple_of(start * share, share)
            parts_ref[half, pl.ds(start, share), :] = terms[turb * share : (turb + 1) * share]
    keep_ref[...] = parts_ref[0]
    send_ref[...] = parts_ref[1].astype(send_ref.dtype)
    ones = jnp.ones((SUM_ROWS, quad), jnp.bfloat16)
    coarse = along.astype(jnp.bfloat16)
    fine = (along - coarse.astype(jnp.float32)).astype(jnp.bfloat16)
    total = (contract(ones, coarse, 1, 1) + contract(ones, fine, 1, 1)) / gain_ref[...]
    sum_ref[...] = sum((ref[...] for ref in before), total)


def backward(sectors, adjacency, cotangent, out_weight, normed_t, queries, keys, values, keys_t,
             attended_t, levels, norm_gain, query_weight, key_weight, value_weight, before,
             block_rows, which):
    row_count, width = cotangent.shape
    head_dim = width // HEADS
    quad = QUAD * head_dim
    fixed = lambda *shape: pl.BlockSpec(shape, lambda i, *lists: (0,) * len(shape))
    across = pl.BlockSpec((row_count, quad), lambda i, *lists: (0, which))
    down = lambda size: pl.BlockSpec((quad, size), lambda i, *lists: (which, 0))
    stat = pl.BlockSpec((1,) + levels.shape[1:], lambda i, *lists: (which, 0, 0))
    part = jax.ShapeDtypeStruct((row_count, quad), jnp.bfloat16)
    half = (2 * width, quad)
    sent = jnp.bfloat16 if which == 0 else jnp.float32
    return pl.pallas_call(
        lambda *refs: backward_kernel(block_rows, head_dim, which, *refs),
        grid_spec=pltpu.PrefetchScalarGridSpec(
            num_scalar_prefetch=2,
            grid=(1,),
            in_specs=[down(width)]
            + [across] * 3
            + [down(row_count), stat, fixed(1, width)]
            + [fixed(SUM_ROWS, width)] * which
            + [pl.BlockSpec(memory_space=pl.ANY)] * 6,
            out_specs=[fixed(row_count, quad)] * 3
            + [fixed(*half)] * 2
            + [fixed(SUM_ROWS, width)],
            scratch_shapes=[
                pltpu.VMEM((row_count, quad), jnp.bfloat16),
                pltpu.VMEM((row_count, quad), jnp.float32),
                pltpu.VMEM((row_count, quad), jnp.float32),
                pltpu.VMEM((2,) + half, jnp.float32),
            ]
            + [pltpu.VMEM((row_count, width), jnp.bfloat16)]
            + [pltpu.VMEM((width, row_count), jnp.bfloat16)] * 2
            + [pltpu.VMEM((width, quad), jnp.bfloat16)] * 3
            + [pltpu.SemaphoreType.DMA((6,))],
        ),
        out_shape=[part] * 3
        + [
            jax.ShapeDtypeStruct(half, jnp.float32),
            jax.ShapeDtypeStruct(half, sent),
            jax.ShapeDtypeStruct((SUM_ROWS, width), jnp.float32),
        ],
        compiler_params=pltpu.CompilerParams(vmem_limit_bytes=VMEM_LIMIT),
        cost_estimate=pl.CostEstimate(
            flops=10 * row_count * width * quad + 80 * row_count * block_rows * quad,
            bytes_accessed=14 * row_count * width,
            transcendentals=row_count * 4 * block_rows * QUAD,
        ),
        name="backward",
    )(sectors, adjacency, out_weight, queries, keys, values, keys_t, levels,
      norm_gain.reshape(1, width), *before, cotangent, normed_t, attended_t, query_weight, key_weight,
      value_weight)


def finish_kernel(quads, x_ref, cot_ref, gain_ref, wq_ref, wk_ref, wv_ref, *refs):
    grad_refs, out_ref = refs[:-1], refs[-1]
    scaled, inverse, _ = normalize(x_ref[...], gain_ref[...])
    quad = grad_refs[0].shape[1]
    grad_normed = jnp.zeros(x_ref.shape, jnp.float32)
    for i in range(quads):
        lanes = slice(i * quad, (i + 1) * quad)
        for j, weight_ref in enumerate((wq_ref, wk_ref, wv_ref)):
            grad_normed += contract(grad_refs[3 * i + j][...], weight_ref[:, lanes], 1, 1)
    grad_scaled = grad_normed * gain_ref[...]
    grad_input = inverse * (
        grad_scaled
        - jnp.mean(grad_scaled, axis=-1, keepdims=True)
        - scaled * jnp.mean(grad_scaled * scaled, axis=-1, keepdims=True)
    )
    out_ref[...] = (cot_ref[...].astype(jnp.float32) + grad_input).astype(jnp.bfloat16)


def finish(rows, cotangent, norm_gain, query_weight, key_weight, value_weight, grads):
    row_count, width = rows.shape
    quad = grads[0].shape[1]
    step = min(row_count, 256)
    fixed = lambda *shape: pl.BlockSpec(shape, lambda i: (0,) * len(shape))
    by_row = lambda size: pl.BlockSpec((step, size), lambda i: (i, 0))
    return pl.pallas_call(
        lambda *refs: finish_kernel(width // quad, *refs),
        grid=(row_count // step,),
        in_specs=[by_row(width)] * 2
        + [fixed(1, width)]
        + [fixed(width, width)] * 3
        + [by_row(quad)] * len(grads),
        out_specs=by_row(width),
        out_shape=jax.ShapeDtypeStruct((row_count, width), jnp.bfloat16),
        compiler_params=pltpu.CompilerParams(vmem_limit_bytes=VMEM_LIMIT),
        cost_estimate=pl.CostEstimate(
            flops=6 * row_count * width * width,
            bytes_accessed=16 * row_count * width,
            transcendentals=0,
        ),
        name="finish",
    )(rows, cotangent, norm_gain.reshape(1, width), query_weight, key_weight, value_weight, *grads)


def swap(tensor, axis):
    return lax.all_to_all(tensor, axis, split_axis=0, concat_axis=0, tiled=True)


def across(tensor, axis, distance):
    size = lax.axis_size(axis)
    return lax.ppermute(tensor, axis, [(i, i ^ distance) for i in range(size)])


def across(tensor, axis, distance):
    size = lax.axis_size(axis)
    return lax.ppermute(tensor, axis, [(i, i ^ distance) for i in range(size)])


def reduce_sums(early, late, gain, width):
    quad = gain.shape[1]
    count = gain.shape[0]
    wide = jnp.float32

    def pack(gain):
        high = gain.astype(jnp.bfloat16)
        low = (gain - high.astype(wide)).astype(jnp.bfloat16)
        return jnp.concatenate([high, low, jnp.zeros((16 - 2 * count, quad), jnp.bfloat16)])

    def halve(parts, gain, axis, distance):
        halves = [part.shape[0] // 2 for part in parts]
        sent = [part[half:].astype(jnp.bfloat16) for part, half in zip(parts, halves)]
        if gain is not None:
            sent.append(pack(gain))
        arrived = across(jnp.concatenate(sent), axis, distance)
        start, kept = 0, []
        for part, half in zip(parts, halves):
            kept.append(part[:half] + arrived[start : start + half].astype(wide))
            start += half
        if gain is None:
            return kept, gain
        rows = arrived[start:].astype(wide)
        return kept, gain + rows[:count] + rows[count : 2 * count]

    first = early[:width] + across(early[width:], "sample", 1)
    first, _ = halve([first], None, "sample", 2)
    second, gain = halve([late], gain, "sample", 2)
    second, gain = halve(second, gain, "turb", 1)
    parts = first + second
    share = parts[0].shape[0] // 4
    pieces = [jnp.concatenate([part[i * share : (i + 1) * share] for part in parts]) for i in range(4)]
    size = pieces[0].shape[0]
    sent = [jnp.concatenate([piece.astype(jnp.bfloat16), pack(gain)]) for piece in pieces[1:]]
    arrived = [across(piece, "turb", 2 * i + 2).astype(wide) for i, piece in enumerate(sent)]
    total = pieces[0] + sum(rows[:size] for rows in arrived)
    gain = gain + sum(
        rows[size : size + count] + rows[size + count : size + 2 * count] for rows in arrived
    )
    return total.astype(jnp.bfloat16).reshape(1, 2, share, quad), gain.reshape(width)


def gather_sums(total):
    total = jnp.concatenate([total] + [across(total, "turb", distance) for distance in (2, 4, 6)])
    other = across(total, "turb", 1)
    four = [total, other, across(total, "sample", 2), across(other, "sample", 2)]
    return four + [across(part, "sample", 1) for part in four]


def place_kernel(*refs):
    (*parts, query_ref, key_ref, value_ref, out_ref, all_ref) = refs
    own_sample, own_turb = lax.axis_index("sample"), lax.axis_index("turb")
    _, quads, share, quad = parts[0].shape
    for i in range(SAMPLES):
        product = own_sample ^ ((i % 2) * 2 + i // 2)
        for apart in range(TURBS):
            place = turb_place(apart)
            ref = parts[2 * i + place // 4]
            rows = pl.ds(pl.multiple_of((apart ^ own_turb) * share, share), share)
            for j in range(quads):
                all_ref[product, rows, j * quad : (j + 1) * quad] = ref[place % 4, j].astype(
                    jnp.float32
                )
    for i, ref in enumerate((query_ref, key_ref, value_ref, out_ref)):
        ref[...] = all_ref[i]


def place_sums(parts, width):
    return pl.pallas_call(
        place_kernel,
        in_specs=[pl.BlockSpec(memory_space=pltpu.VMEM)] * len(parts),
        out_specs=[pl.BlockSpec(memory_space=pltpu.VMEM)] * 4,
        out_shape=[jax.ShapeDtypeStruct((width, width), jnp.float32)] * 4,
        scratch_shapes=[pltpu.VMEM((4, width, width), jnp.float32)],
        compiler_params=pltpu.CompilerParams(vmem_limit_bytes=VMEM_LIMIT),
        cost_estimate=pl.CostEstimate(
            flops=0, bytes_accessed=24 * width * width, transcendentals=0
        ),
        name="place",
    )(*parts)


def by_sample(
    inflow,
    cotangent,
    norm_gain,
    query_weight,
    key_weight,
    value_weight,
    out_weight,
    adjacency,
    sectors,
):
    sample_count, block_rows, width = inflow.shape
    row_count = lax.axis_size("turb") * block_rows
    adjacency = jnp.transpose(adjacency, (2, 0, 1))
    rows = swap(inflow, "turb")
    rows, cotangent = lax.optimization_barrier((rows, cotangent))
    rows = rows.reshape(row_count, width)
    grad_rows = swap(cotangent, "turb").reshape(row_count, width)
    *saved, layer_rows = forward(
        sectors, adjacency, rows, norm_gain, query_weight, key_weight, value_weight, out_weight,
        block_rows,
    )
    layer_output = swap(layer_rows.reshape(inflow.shape), "turb")
    weights = (norm_gain, query_weight, key_weight, value_weight)
    *grads, early, send, before = backward(
        sectors, adjacency, grad_rows, out_weight, *saved, *weights, [], block_rows, 0
    )
    arrived = across(send, "turb", 1)
    *more, late, send, gain = backward(
        sectors, adjacency, grad_rows, out_weight, *saved, *weights, [before], block_rows, 1
    )
    more, late, send, gain, arrived, layer_output = lax.optimization_barrier(
        (more, late, send, gain, arrived, layer_output)
    )
    arrived_late = across(send, "sample", 1)
    gain = gain[0].reshape(-1, late.shape[1])
    total, sum_gain = reduce_sums(
        early + arrived.astype(jnp.float32),
        late + arrived_late,
        gain + across(gain, "sample", 1),
        width,
    )
    grad_rows = finish(rows, grad_rows, *weights, grads + more)
    grad_rows, total = lax.optimization_barrier((grad_rows, total))
    grad_inflow = swap(grad_rows.reshape(inflow.shape), "turb")
    parts = gather_sums(total)
    sums = place_sums(parts, width)
    lowest = jnp.finfo(jnp.bfloat16).min
    return (
        jnp.maximum(layer_output, lowest),
        jnp.maximum(grad_inflow, lowest),
        *sums,
        sum_gain,
    )


def solution(mesh):
    placed = (
        P("sample", "turb", None),
        P("sample", "turb", None),
        P(),
        P(),
        P(),
        P(),
        P(),
        P(),
        P("sample"),
    )

    def plan(*args):
        sample_count = args[0].shape[0]
        if sample_count == mesh.shape["turb"] == TURBS and mesh.shape["sample"] == SAMPLES:
            return by_sample(*args)
        return on_device(*args)

    return jax.shard_map(
        plan,
        mesh=mesh,
        in_specs=placed,
        out_specs=(P("sample", "turb", None), P("sample", "turb", None), P(), P(), P(), P(), P()),
        check_vma=False,
    )
```

```python
import jax
import jax.numpy as jnp
from jax import lax
from jax.experimental import pallas as pl
from jax.experimental.pallas import tpu as pltpu
from jax.sharding import PartitionSpec as P

HEADS = 8
UPSTREAM = 3
SECTORS = 8
REPEAT = 1


epsilon = 1e-05


def normalize(row_block, norm_gain):
    widened = row_block.astype(jnp.float32)
    centred = widened - jnp.mean(widened, axis=-1, keepdims=True)
    inverse = lax.rsqrt(jnp.mean(centred * centred, axis=-1, keepdims=True) + epsilon)
    scaled = centred * inverse
    return (scaled, inverse, (scaled * norm_gain).astype(jnp.bfloat16))


def attend(pieces):
    queries, key_rows, value_rows, key_usable, grad_attended = pieces
    batch_count, query_count, model_width = queries.shape
    key_count = key_rows.shape[1]
    head_dim = model_width // HEADS
    score_scale = head_dim ** (-0.5)
    query_heads = queries.reshape(batch_count, query_count, HEADS, head_dim)
    key_heads = key_rows.reshape(batch_count, key_count, HEADS, head_dim)
    value_heads = value_rows.reshape(batch_count, key_count, HEADS, head_dim)
    grad_heads = grad_attended.reshape(batch_count, query_count, HEADS, head_dim)
    scores = (
        jnp.einsum("nqhd,nkhd->nhqk", query_heads, key_heads, preferred_element_type=jnp.float32)
        * score_scale
    )
    scores = jnp.where(key_usable[:, None, None, :], scores, -1e30)
    highest = jnp.max(scores, axis=-1, keepdims=True)
    weights = jnp.exp(scores - highest)
    probabilities = weights / jnp.sum(weights, axis=-1, keepdims=True)
    rounded = probabilities.astype(jnp.bfloat16)
    attended = jnp.einsum(
        "nhqk,nkhd->nqhd", rounded, value_heads, preferred_element_type=jnp.float32
    ).astype(jnp.bfloat16)
    grad_probs = jnp.einsum(
        "nqhd,nkhd->nhqk", grad_heads, value_heads, preferred_element_type=jnp.float32
    )
    centred = grad_probs - jnp.sum(probabilities * grad_probs, axis=-1, keepdims=True)
    grad_scores = (probabilities * centred * score_scale).astype(jnp.bfloat16)
    grad_queries = jnp.einsum(
        "nhqk,nkhd->nqhd", grad_scores, key_heads, preferred_element_type=jnp.float32
    ).astype(jnp.bfloat16)
    grad_keys = jnp.einsum(
        "nhqk,nqhd->nkhd", grad_scores, query_heads, preferred_element_type=jnp.float32
    )
    grad_values = jnp.einsum(
        "nhqk,nqhd->nkhd", rounded, grad_heads, preferred_element_type=jnp.float32
    )
    pair_terms = jnp.concatenate(
        [
            grad_keys.reshape(batch_count, key_count, model_width),
            grad_values.reshape(batch_count, key_count, model_width),
        ],
        axis=-1,
    )
    return (
        attended.reshape(batch_count, query_count, model_width),
        grad_queries.reshape(batch_count, query_count, model_width),
        pair_terms,
    )


def on_device(
    inflow,
    cotangent,
    norm_gain,
    query_weight,
    key_weight,
    value_weight,
    out_weight,
    adjacency,
    sectors,
):
    sample_count, block_rows, model_width = inflow.shape
    block_count = lax.axis_size("turb")
    own_block = lax.axis_index("turb")
    slot_count = REPEAT * ((SECTORS * UPSTREAM + block_count - 2) // (block_count - 1))
    flat_rows = sample_count * block_rows
    pair_width = 2 * model_width
    input_rows = inflow.reshape(flat_rows, model_width)
    grad_rows = cotangent.reshape(flat_rows, model_width)
    scaled, inverse, normed = normalize(input_rows, norm_gain)
    queries = jnp.dot(normed, query_weight, preferred_element_type=jnp.float32).astype(jnp.bfloat16)
    key_rows = jnp.dot(normed, key_weight, preferred_element_type=jnp.float32).astype(jnp.bfloat16)
    value_rows = jnp.dot(normed, value_weight, preferred_element_type=jnp.float32).astype(
        jnp.bfloat16
    )
    upstream = adjacency[sectors]
    needed = jnp.any(upstream == own_block, axis=2).astype(jnp.int32)
    earlier_need = jnp.cumsum(needed, axis=0) - needed
    slot_index = lax.broadcasted_iota(jnp.int32, (block_count, slot_count, sample_count), 1)
    chosen = (needed.T[:, None, :] == 1) & (earlier_need.T[:, None, :] == slot_index)
    selector = chosen.astype(jnp.bfloat16).reshape(block_count * slot_count, sample_count)
    own_lists = lax.dynamic_index_in_dim(upstream, own_block, axis=1, keepdims=False)
    usable = own_lists >= 0
    matches = jnp.any(own_lists[:, :, None, None] == own_lists[None, None, :, :], axis=3)
    sample_ids = lax.broadcasted_iota(jnp.int32, (sample_count, sample_count), 0)
    earlier = lax.broadcasted_iota(jnp.int32, (sample_count, sample_count), 1) < sample_ids
    position = jnp.sum((matches & earlier[:, None, :]).astype(jnp.int32), axis=2)
    flat_slot = own_lists * slot_count + position
    fetch_at = jnp.where(usable, flat_slot, 0)
    payload = jnp.concatenate([key_rows, value_rows], axis=1).reshape(
        sample_count, block_rows * pair_width
    )
    packed = jnp.dot(selector, payload, preferred_element_type=jnp.float32).astype(jnp.bfloat16)
    arrived = lax.all_to_all(
        packed.reshape(block_count, slot_count, block_rows, pair_width),
        "turb",
        split_axis=0,
        concat_axis=0,
        tiled=True,
    )
    fetched = arrived.reshape(block_count * slot_count, block_rows, pair_width)[fetch_at]
    upstream_keys = fetched[..., :model_width]
    upstream_values = fetched[..., model_width:]
    key_count = (1 + UPSTREAM) * block_rows
    key_all = jnp.concatenate(
        [key_rows.reshape(sample_count, 1, block_rows, model_width), upstream_keys], axis=1
    ).reshape(sample_count, key_count, model_width)
    value_all = jnp.concatenate(
        [value_rows.reshape(sample_count, 1, block_rows, model_width), upstream_values], axis=1
    ).reshape(sample_count, key_count, model_width)
    block_usable = jnp.concatenate([jnp.ones((sample_count, 1), dtype=jnp.bool_), usable], axis=1)
    key_usable = jnp.repeat(block_usable, block_rows, axis=1)
    grad_attended = jnp.dot(grad_rows, out_weight.T, preferred_element_type=jnp.float32).astype(
        jnp.bfloat16
    )
    group_size = min(sample_count, max(1, 512 // block_rows))
    while sample_count % group_size != 0:
        group_size = group_size - 1
    group_count = sample_count // group_size

    def grouped(tensor):
        return tensor.reshape((group_count, group_size) + tensor.shape[1:])

    attended, grad_queries, pair_terms = lax.map(
        attend,
        (
            grouped(queries.reshape(sample_count, block_rows, model_width)),
            grouped(key_all),
            grouped(value_all),
            grouped(key_usable),
            grouped(grad_attended.reshape(sample_count, block_rows, model_width)),
        ),
    )
    attended = attended.reshape(flat_rows, model_width)
    grad_queries = grad_queries.reshape(flat_rows, model_width)
    pair_terms = pair_terms.reshape(sample_count, 1 + UPSTREAM, block_rows, pair_width)
    layer_output = (
        (
            input_rows.astype(jnp.float32)
            + jnp.dot(attended, out_weight, preferred_element_type=jnp.float32)
        )
        .astype(jnp.bfloat16)
        .reshape(inflow.shape)
    )
    outgoing = (
        pair_terms[:, 1:]
        .astype(jnp.bfloat16)
        .reshape(sample_count * UPSTREAM, block_rows, pair_width)
    )
    target = jnp.where(usable, flat_slot, block_count * slot_count).reshape(-1)
    outbound = (
        jnp.zeros((block_count * slot_count, block_rows, pair_width), jnp.bfloat16)
        .at[target]
        .set(outgoing, mode="drop")
    )
    sum_out = jnp.dot(attended.T, grad_rows, preferred_element_type=jnp.float32)
    sum_query = jnp.dot(normed.T, grad_queries, preferred_element_type=jnp.float32)
    returned = lax.all_to_all(
        outbound.reshape(block_count, slot_count, block_rows, pair_width),
        "turb",
        split_axis=0,
        concat_axis=0,
        tiled=True,
    )
    remote = jnp.dot(
        selector.T,
        returned.reshape(block_count * slot_count, block_rows * pair_width),
        preferred_element_type=jnp.float32,
    )
    combined = (
        (pair_terms[:, 0].reshape(sample_count, block_rows * pair_width) + remote)
        .astype(jnp.bfloat16)
        .reshape(flat_rows, pair_width)
    )
    grad_keys = combined[:, :model_width]
    grad_values = combined[:, model_width:]
    sum_key = jnp.dot(normed.T, grad_keys, preferred_element_type=jnp.float32)
    sum_value = jnp.dot(normed.T, grad_values, preferred_element_type=jnp.float32)
    grad_normed = jnp.dot(grad_queries, query_weight.T, preferred_element_type=jnp.float32)
    grad_normed = grad_normed + jnp.dot(grad_keys, key_weight.T, preferred_element_type=jnp.float32)
    grad_normed = grad_normed + jnp.dot(
        grad_values, value_weight.T, preferred_element_type=jnp.float32
    )
    sum_gain = jnp.sum(grad_normed * scaled, axis=0)
    grad_scaled = grad_normed * norm_gain
    grad_input = inverse * (
        grad_scaled
        - jnp.mean(grad_scaled, axis=-1, keepdims=True)
        - scaled * jnp.mean(grad_scaled * scaled, axis=-1, keepdims=True)
    )
    grad_inflow = (
        (grad_rows.astype(jnp.float32) + grad_input).astype(jnp.bfloat16).reshape(inflow.shape)
    )
    sum_query, sum_key, sum_value, sum_out, sum_gain = lax.psum(
        (sum_query, sum_key, sum_value, sum_out, sum_gain), ("sample", "turb")
    )
    return (layer_output, grad_inflow, sum_query, sum_key, sum_value, sum_out, sum_gain)


PAIR = 2
QUAD = 4
LOG2_E = 1.4426950408889634
VMEM_LIMIT = 58 * 2**20
SUM_ROWS = 8
SAMPLES = 4
TURBS = 8


def turb_place(apart):
    return (apart % 2) * 4 + (apart // 4) * 2 + (apart // 2) % 2


def contract(left, right, left_dim, right_dim):
    return lax.dot_general(
        left, right, (((left_dim,), (right_dim,)), ((), ())), preferred_element_type=jnp.float32
    )


def split_heads(rows, head_dim):
    lane = lax.broadcasted_iota(jnp.int32, rows.shape, 1)
    wide = rows.astype(jnp.float32)
    return jnp.concatenate(
        [jnp.where(lane < head_dim, wide, 0.0), jnp.where(lane >= head_dim, wide, 0.0)], axis=0
    ).astype(jnp.bfloat16)


def join_heads(wide, head_dim):
    block_rows = wide.shape[1] // PAIR
    first = lax.broadcasted_iota(jnp.int32, (wide.shape[0], block_rows), 0) < head_dim
    return jnp.where(first, wide[:, :block_rows], wide[:, block_rows:])


def for_each_block(sectors_ref, lists_ref, block_count, block_rows, work):
    sector = sectors_ref[lax.axis_index("turb")]

    def step(block, carry):
        used = jnp.int32(0)
        for slot in range(UPSTREAM):
            used = used + (lists_ref[slot, sector, block] >= 0).astype(jnp.int32)
        for count in range(UPSTREAM + 1):

            @pl.when(used == count)
            def _():
                sources = [block] + [
                    lists_ref[slot, sector, block] for slot in range(count)
                ]
                work(block, [pl.multiple_of(s * block_rows, block_rows) for s in sources])

        return carry

    lax.fori_loop(0, block_count, step, 0)


def stacked(ref, starts, block_rows, lanes):
    return jnp.concatenate([ref[pl.ds(s, block_rows), lanes] for s in starts], axis=0)


def beside(ref, starts, block_rows, rows):
    return jnp.concatenate([ref[rows, pl.ds(s, block_rows)] for s in starts], axis=1)


def forward_kernel(block_rows, head_dim, sectors_ref, lists_ref, x_ref, gain_ref, wq_ref, wk_ref,
                   wv_ref, wo_ref, normed_t_ref, q_ref, k_ref, v_ref, kt_ref, att_ref,
                   level_ref, out_ref, normed_ref, vt_ref, rows_ref, sum_ref):
    row_count = x_ref.shape[0]
    quad = pl.program_id(0)
    pair = PAIR * head_dim
    exponent = head_dim ** (-0.5) * LOG2_E
    chunk = min(row_count, 256)

    @pl.when(quad == 0)
    def _():
        for start in range(0, row_count, chunk):
            part = slice(start, start + chunk)
            scaled, _, normed = normalize(x_ref[part, :], gain_ref[...])
            normed_ref[part, :] = normed
            normed_t_ref[:, part] = (scaled * gain_ref[...]).T.astype(jnp.bfloat16)

    normed = normed_ref[...]
    q_ref[...] = contract(normed, wq_ref[...], 1, 0).astype(jnp.bfloat16)
    k_ref[...] = contract(normed, wk_ref[...], 1, 0).astype(jnp.bfloat16)
    v_ref[...] = contract(normed, wv_ref[...], 1, 0).astype(jnp.bfloat16)
    kt_ref[...] = contract(wk_ref[...], normed, 0, 1).astype(jnp.bfloat16)
    vt_ref[...] = contract(wv_ref[...], normed, 0, 1).astype(jnp.bfloat16)

    def work(block, starts):
        own = pl.ds(starts[0], block_rows)
        lanes = [slice(p * pair, (p + 1) * pair) for p in range(QUAD // PAIR)]
        scores = [
            contract(
                stacked(k_ref, starts, block_rows, lane), split_heads(q_ref[own, lane], head_dim), 1, 1
            )
            for lane in lanes
        ]
        for p, lane in enumerate(lanes):
            highest = jnp.max(scores[p], axis=0, keepdims=True)
            weights = jnp.exp2((scores[p] - highest) * exponent)
            total = jnp.sum(weights, axis=0, keepdims=True)
            probs = (weights * (1.0 / total)).astype(jnp.bfloat16)
            level_ref[0, pl.ds(block * (QUAD // PAIR) + p, 1), :] = highest * exponent + jnp.log2(
                total
            )
            joined = join_heads(
                jnp.dot(
                    beside(vt_ref, starts, block_rows, lane),
                    probs,
                    preferred_element_type=jnp.float32,
                ),
                head_dim,
            )
            att_ref[lane, own] = joined.astype(jnp.bfloat16)
            rows_ref[own, lane] = joined.T.astype(jnp.bfloat16)

    for_each_block(sectors_ref, lists_ref, row_count // block_rows, block_rows, work)
    part = contract(rows_ref[...], wo_ref[...], 1, 0)

    @pl.when(quad == 0)
    def _():
        sum_ref[...] = x_ref[...].astype(jnp.float32) + part

    @pl.when(quad > 0)
    def _():
        sum_ref[...] += part

    @pl.when(quad == pl.num_programs(0) - 1)
    def _():
        out_ref[...] = sum_ref[...].astype(jnp.bfloat16)


def forward(sectors, adjacency, rows, norm_gain, query_weight, key_weight, value_weight, out_weight, block_rows):
    row_count, width = rows.shape
    head_dim = width // HEADS
    quad = QUAD * head_dim
    quads = width // quad
    stat_rows = row_count // block_rows * (QUAD // PAIR)
    fixed = lambda *shape: pl.BlockSpec(shape, lambda p, *lists: (0,) * len(shape))
    across = lambda size: pl.BlockSpec((size, quad), lambda p, *lists: (0, p))
    down = lambda size: pl.BlockSpec((quad, size), lambda p, *lists: (p, 0))
    stat = pl.BlockSpec((1, stat_rows, PAIR * block_rows), lambda p, *lists: (p, 0, 0))
    flat = jax.ShapeDtypeStruct((row_count, width), jnp.bfloat16)
    turned = jax.ShapeDtypeStruct((width, row_count), jnp.bfloat16)
    stats = jax.ShapeDtypeStruct((quads, stat_rows, PAIR * block_rows), jnp.float32)
    return pl.pallas_call(
        lambda *refs: forward_kernel(block_rows, head_dim, *refs),
        grid_spec=pltpu.PrefetchScalarGridSpec(
            num_scalar_prefetch=2,
            grid=(quads,),
            in_specs=[fixed(row_count, width), fixed(1, width)]
            + [across(width)] * 3
            + [down(width)],
            out_specs=[fixed(width, row_count)]
            + [across(row_count)] * 3
            + [down(row_count)] * 2
            + [stat, fixed(row_count, width)],
            scratch_shapes=[
                pltpu.VMEM((row_count, width), jnp.bfloat16),
                pltpu.VMEM((quad, row_count), jnp.bfloat16),
                pltpu.VMEM((row_count, quad), jnp.bfloat16),
                pltpu.VMEM((row_count, width), jnp.float32),
            ],
        ),
        out_shape=[turned, flat, flat, flat, turned, turned, stats, flat],
        compiler_params=pltpu.CompilerParams(vmem_limit_bytes=VMEM_LIMIT),
        cost_estimate=pl.CostEstimate(
            flops=12 * row_count * width * width + 32 * row_count * block_rows * width,
            bytes_accessed=20 * row_count * width,
            transcendentals=row_count * 4 * block_rows * HEADS,
        ),
        name="forward",
    )(sectors, adjacency, rows, norm_gain.reshape(1, width), query_weight, key_weight, value_weight,
      out_weight)


def backward_kernel(block_rows, head_dim, which, sectors_ref, lists_ref, wo_ref, q_ref, k_ref, v_ref,
                    kt_ref, level_ref, gain_ref, *refs):
    before, refs = refs[:which], refs[which:]
    late, refs = refs[:6], refs[6:]
    gq_ref, gk_ref, gv_ref, keep_ref, send_ref, sum_ref, *refs = refs
    ga_ref, gk_acc, gv_acc, parts_ref, *held, sems = refs
    cot_ref = held[0]
    row_count, width = cot_ref.shape
    block_count = row_count // block_rows
    pair = PAIR * head_dim
    quad = QUAD * head_dim
    scale = head_dim ** (-0.5)
    own_lanes = slice(which * quad, (which + 1) * quad)
    copies = []
    for i, (ref, into) in enumerate(zip(late, held)):
        source = ref if i < 3 else ref.at[:, own_lanes]
        copies.append(pltpu.make_async_copy(source, into, sems.at[i]))
        copies[-1].start()
    _, normed_t_ref, att_ref, *weight_refs = held
    copies[0].wait()
    ga_ref[...] = contract(cot_ref[...], wo_ref[...], 1, 1).astype(jnp.bfloat16)
    gk_acc[...] = jnp.zeros_like(gk_acc)
    gv_acc[...] = jnp.zeros_like(gv_acc)

    def work(block, starts):
        own = pl.ds(starts[0], block_rows)
        lanes = [slice(p * pair, (p + 1) * pair) for p in range(QUAD // PAIR)]
        queries = [split_heads(q_ref[own, lane], head_dim) for lane in lanes]
        grads = [split_heads(ga_ref[own, lane], head_dim) for lane in lanes]
        scores = [
            contract(stacked(k_ref, starts, block_rows, lane), queries[p], 1, 1)
            for p, lane in enumerate(lanes)
        ]
        grad_probs = [
            contract(stacked(v_ref, starts, block_rows, lane), grads[p] * scale, 1, 1)
            for p, lane in enumerate(lanes)
        ]
        for p, lane in enumerate(lanes):
            stat = pl.ds(block * (QUAD // PAIR) + p, 1)
            probs = jnp.exp2(scores[p] * (scale * LOG2_E) - level_ref[0, stat, :])
            total = jnp.sum(probs * grad_probs[p], axis=0, keepdims=True)
            grad_scores = (probs * (grad_probs[p] - total)).astype(jnp.bfloat16)
            probs_b = probs.astype(jnp.bfloat16)
            grad_values = jnp.dot(probs_b, grads[p], preferred_element_type=jnp.float32)
            grad_keys = jnp.dot(grad_scores, queries[p], preferred_element_type=jnp.float32)
            joined = join_heads(
                jnp.dot(
                    beside(kt_ref, starts, block_rows, lane),
                    grad_scores,
                    preferred_element_type=jnp.float32,
                ),
                head_dim,
            )
            gq_ref[own, lane] = joined.T.astype(jnp.bfloat16)
            for slot, start in enumerate(starts):
                rows = pl.ds(start, block_rows)
                part = slice(slot * block_rows, (slot + 1) * block_rows)
                for acc, terms in ((gk_acc, grad_keys), (gv_acc, grad_values)):
                    term = terms[part]
                    if slot > 0:
                        term = term.astype(jnp.bfloat16).astype(jnp.float32)
                    acc[rows, lane] += term

    for_each_block(sectors_ref, lists_ref, block_count, block_rows, work)
    gk_ref[...] = gk_acc[...].astype(jnp.bfloat16)
    gv_ref[...] = gv_acc[...].astype(jnp.bfloat16)
    for copy in copies[1:]:
        copy.wait()
    products = [(normed_t_ref, ref, slice(None)) for ref in (gq_ref, gk_ref, gv_ref)]
    products.append((att_ref, cot_ref, own_lanes))
    own_sample, own_turb = lax.axis_index("sample"), lax.axis_index("turb")
    share = width // TURBS
    along = jnp.zeros((width, quad), jnp.float32)
    for i, (left, right, lanes) in enumerate(products):
        terms = contract(left[...], right[:, lanes], 1, 0)
        if i < len(weight_refs):
            along += terms * weight_refs[i][...].astype(jnp.float32)
        apart = i ^ own_sample
        for turb in range(TURBS):
            place = turb_place(turb ^ own_turb)
            if which == 0:
                half, start = place // 4, (apart % 2 * 2 + apart // 2) * 4 + place % 4
            else:
                half, start = apart % 2, apart // 2 * TURBS + place
            start = pl.multiple_of(start * share, share)
            parts_ref[half, pl.ds(start, share), :] = terms[turb * share : (turb + 1) * share]
    keep_ref[...] = parts_ref[0]
    send_ref[...] = parts_ref[1].astype(send_ref.dtype)
    ones = jnp.ones((SUM_ROWS, quad), jnp.bfloat16)
    coarse = along.astype(jnp.bfloat16)
    fine = (along - coarse.astype(jnp.float32)).astype(jnp.bfloat16)
    total = (contract(ones, coarse, 1, 1) + contract(ones, fine, 1, 1)) / gain_ref[...]
    sum_ref[...] = sum((ref[...] for ref in before), total)


def backward(sectors, adjacency, cotangent, out_weight, normed_t, queries, keys, values, keys_t,
             attended_t, levels, norm_gain, query_weight, key_weight, value_weight, before,
             block_rows, which):
    row_count, width = cotangent.shape
    head_dim = width // HEADS
    quad = QUAD * head_dim
    fixed = lambda *shape: pl.BlockSpec(shape, lambda i, *lists: (0,) * len(shape))
    across = pl.BlockSpec((row_count, quad), lambda i, *lists: (0, which))
    down = lambda size: pl.BlockSpec((quad, size), lambda i, *lists: (which, 0))
    stat = pl.BlockSpec((1,) + levels.shape[1:], lambda i, *lists: (which, 0, 0))
    part = jax.ShapeDtypeStruct((row_count, quad), jnp.bfloat16)
    half = (2 * width, quad)
    sent = jnp.bfloat16 if which == 0 else jnp.float32
    return pl.pallas_call(
        lambda *refs: backward_kernel(block_rows, head_dim, which, *refs),
        grid_spec=pltpu.PrefetchScalarGridSpec(
            num_scalar_prefetch=2,
            grid=(1,),
            in_specs=[down(width)]
            + [across] * 3
            + [down(row_count), stat, fixed(1, width)]
            + [fixed(SUM_ROWS, width)] * which
            + [pl.BlockSpec(memory_space=pl.ANY)] * 6,
            out_specs=[fixed(row_count, quad)] * 3
            + [fixed(*half)] * 2
            + [fixed(SUM_ROWS, width)],
            scratch_shapes=[
                pltpu.VMEM((row_count, quad), jnp.bfloat16),
                pltpu.VMEM((row_count, quad), jnp.float32),
                pltpu.VMEM((row_count, quad), jnp.float32),
                pltpu.VMEM((2,) + half, jnp.float32),
            ]
            + [pltpu.VMEM((row_count, width), jnp.bfloat16)]
            + [pltpu.VMEM((width, row_count), jnp.bfloat16)] * 2
            + [pltpu.VMEM((width, quad), jnp.bfloat16)] * 3
            + [pltpu.SemaphoreType.DMA((6,))],
        ),
        out_shape=[part] * 3
        + [
            jax.ShapeDtypeStruct(half, jnp.float32),
            jax.ShapeDtypeStruct(half, sent),
            jax.ShapeDtypeStruct((SUM_ROWS, width), jnp.float32),
        ],
        compiler_params=pltpu.CompilerParams(vmem_limit_bytes=VMEM_LIMIT),
        cost_estimate=pl.CostEstimate(
            flops=10 * row_count * width * quad + 80 * row_count * block_rows * quad,
            bytes_accessed=14 * row_count * width,
            transcendentals=row_count * 4 * block_rows * QUAD,
        ),
        name="backward",
    )(sectors, adjacency, out_weight, queries, keys, values, keys_t, levels,
      norm_gain.reshape(1, width), *before, cotangent, normed_t, attended_t, query_weight, key_weight,
      value_weight)


def finish_kernel(quads, x_ref, cot_ref, gain_ref, wq_ref, wk_ref, wv_ref, *refs):
    grad_refs, out_ref = refs[:-1], refs[-1]
    scaled, inverse, _ = normalize(x_ref[...], gain_ref[...])
    quad = grad_refs[0].shape[1]
    grad_normed = jnp.zeros(x_ref.shape, jnp.float32)
    for i in range(quads):
        lanes = slice(i * quad, (i + 1) * quad)
        for j, weight_ref in enumerate((wq_ref, wk_ref, wv_ref)):
            grad_normed += contract(grad_refs[3 * i + j][...], weight_ref[:, lanes], 1, 1)
    grad_scaled = grad_normed * gain_ref[...]
    grad_input = inverse * (
        grad_scaled
        - jnp.mean(grad_scaled, axis=-1, keepdims=True)
        - scaled * jnp.mean(grad_scaled * scaled, axis=-1, keepdims=True)
    )
    out_ref[...] = (cot_ref[...].astype(jnp.float32) + grad_input).astype(jnp.bfloat16)


def finish(rows, cotangent, norm_gain, query_weight, key_weight, value_weight, grads):
    row_count, width = rows.shape
    quad = grads[0].shape[1]
    step = min(row_count, 256)
    fixed = lambda *shape: pl.BlockSpec(shape, lambda i: (0,) * len(shape))
    by_row = lambda size: pl.BlockSpec((step, size), lambda i: (i, 0))
    return pl.pallas_call(
        lambda *refs: finish_kernel(width // quad, *refs),
        grid=(row_count // step,),
        in_specs=[by_row(width)] * 2
        + [fixed(1, width)]
        + [fixed(width, width)] * 3
        + [by_row(quad)] * len(grads),
        out_specs=by_row(width),
        out_shape=jax.ShapeDtypeStruct((row_count, width), jnp.bfloat16),
        compiler_params=pltpu.CompilerParams(vmem_limit_bytes=VMEM_LIMIT),
        cost_estimate=pl.CostEstimate(
            flops=6 * row_count * width * width,
            bytes_accessed=16 * row_count * width,
            transcendentals=0,
        ),
        name="finish",
    )(rows, cotangent, norm_gain.reshape(1, width), query_weight, key_weight, value_weight, *grads)


def swap(tensor, axis):
    return lax.all_to_all(tensor, axis, split_axis=0, concat_axis=0, tiled=True)


def across(tensor, axis, distance):
    size = lax.axis_size(axis)
    return lax.ppermute(tensor, axis, [(i, i ^ distance) for i in range(size)])


def across(tensor, axis, distance):
    size = lax.axis_size(axis)
    return lax.ppermute(tensor, axis, [(i, i ^ distance) for i in range(size)])


def reduce_sums(early, late, gain, width, beside):
    quad = gain.shape[1]
    count = gain.shape[0]
    wide = jnp.float32

    def pack(gain):
        high = gain.astype(jnp.bfloat16)
        low = (gain - high.astype(wide)).astype(jnp.bfloat16)
        return jnp.concatenate([high, low, jnp.zeros((16 - 2 * count, quad), jnp.bfloat16)])

    def halve(parts, gain, axis, distance):
        halves = [part.shape[0] // 2 for part in parts]
        sent = [part[half:].astype(jnp.bfloat16) for part, half in zip(parts, halves)]
        if gain is not None:
            sent.append(pack(gain))
        arrived = across(jnp.concatenate(sent), axis, distance)
        start, kept = 0, []
        for part, half in zip(parts, halves):
            kept.append(part[:half] + arrived[start : start + half].astype(wide))
            start += half
        if gain is None:
            return kept, gain
        rows = arrived[start:].astype(wide)
        return kept, gain + rows[:count] + rows[count : 2 * count]

    first = early[:width] + across(early[width:], "sample", 1)
    first, _ = halve([first], None, "sample", 2)
    second, gain = halve([late], gain, "sample", 2)
    second, gain = halve(second, gain, "turb", 1)
    parts, gain, beside = lax.optimization_barrier((first + second, gain, beside))
    share = parts[0].shape[0] // 4
    pieces = [jnp.concatenate([part[i * share : (i + 1) * share] for part in parts]) for i in range(4)]
    size = pieces[0].shape[0]
    sent = [jnp.concatenate([piece.astype(jnp.bfloat16), pack(gain)]) for piece in pieces[1:]]
    arrived = [across(piece, "turb", 2 * i + 2).astype(wide) for i, piece in enumerate(sent)]
    total = pieces[0] + sum(rows[:size] for rows in arrived)
    gain = gain + sum(
        rows[size : size + count] + rows[size + count : size + 2 * count] for rows in arrived
    )
    total = total.astype(jnp.bfloat16).reshape(1, 2, share, quad)
    total = jnp.concatenate([total] + [across(total, "turb", distance) for distance in (2, 4, 6)])
    other = across(total, "turb", 1)
    four = [total, other, across(total, "sample", 2), across(other, "sample", 2)]
    four += [across(part, "sample", 1) for part in four]
    return four, gain.reshape(width), beside


def place_kernel(*refs):
    (*sources, query_ref, key_ref, value_ref, out_ref, all_ref, held, sems) = refs
    copies = [
        pltpu.make_async_copy(ref, held.at[i], sems.at[i]) for i, ref in enumerate(sources)
    ]
    for copy in copies:
        copy.start()
    own_sample, own_turb = lax.axis_index("sample"), lax.axis_index("turb")
    _, _, quads, share, quad = held.shape
    for i in range(SAMPLES):
        copies[2 * i].wait()
        copies[2 * i + 1].wait()
        product = own_sample ^ ((i % 2) * 2 + i // 2)
        for apart in range(TURBS):
            place = turb_place(apart)
            rows = pl.ds(pl.multiple_of((apart ^ own_turb) * share, share), share)
            for j in range(quads):
                all_ref[product, rows, j * quad : (j + 1) * quad] = held[
                    2 * i + place // 4, place % 4, j
                ].astype(jnp.float32)
    for i, ref in enumerate((query_ref, key_ref, value_ref, out_ref)):
        ref[...] = all_ref[i]


def place_sums(parts, width):
    return pl.pallas_call(
        place_kernel,
        in_specs=[pl.BlockSpec(memory_space=pl.ANY)] * len(parts),
        out_specs=[pl.BlockSpec(memory_space=pltpu.VMEM)] * 4,
        out_shape=[jax.ShapeDtypeStruct((width, width), jnp.float32)] * 4,
        scratch_shapes=[
            pltpu.VMEM((4, width, width), jnp.float32),
            pltpu.VMEM((len(parts),) + parts[0].shape, jnp.bfloat16),
            pltpu.SemaphoreType.DMA((len(parts),)),
        ],
        compiler_params=pltpu.CompilerParams(vmem_limit_bytes=VMEM_LIMIT),
        cost_estimate=pl.CostEstimate(
            flops=0, bytes_accessed=24 * width * width, transcendentals=0
        ),
        name="place",
    )(*parts)


def by_sample(
    inflow,
    cotangent,
    norm_gain,
    query_weight,
    key_weight,
    value_weight,
    out_weight,
    adjacency,
    sectors,
):
    sample_count, block_rows, width = inflow.shape
    row_count = lax.axis_size("turb") * block_rows
    adjacency = jnp.transpose(adjacency, (2, 0, 1))
    rows = swap(inflow, "turb")
    rows, cotangent = lax.optimization_barrier((rows, cotangent))
    rows = rows.reshape(row_count, width)
    grad_rows = swap(cotangent, "turb").reshape(row_count, width)
    *saved, layer_rows = forward(
        sectors, adjacency, rows, norm_gain, query_weight, key_weight, value_weight, out_weight,
        block_rows,
    )
    layer_output = swap(layer_rows.reshape(inflow.shape), "turb")
    weights = (norm_gain, query_weight, key_weight, value_weight)
    *grads, early, send, before = backward(
        sectors, adjacency, grad_rows, out_weight, *saved, *weights, [], block_rows, 0
    )
    arrived = across(send, "turb", 1)
    *more, late, send, gain = backward(
        sectors, adjacency, grad_rows, out_weight, *saved, *weights, [before], block_rows, 1
    )
    more, send, arrived, layer_output = lax.optimization_barrier(
        (more, send, arrived, layer_output)
    )
    arrived_late = across(send, "sample", 1)
    grad_rows = finish(rows, grad_rows, *weights, grads + more)
    grad_rows, late, arrived_late, gain, early, arrived = lax.optimization_barrier(
        (grad_rows, late, arrived_late, gain, early, arrived)
    )
    gain = gain[0].reshape(-1, late.shape[1])
    arrived_gain = across(gain, "sample", 1)
    early = early + arrived.astype(jnp.float32)
    grad_inflow = swap(grad_rows.reshape(inflow.shape), "turb")
    parts, sum_gain, grad_inflow = reduce_sums(
        early, late + arrived_late, gain + arrived_gain, width, grad_inflow
    )
    sums = place_sums(parts, width)
    lowest = jnp.finfo(jnp.bfloat16).min
    return (
        jnp.maximum(layer_output, lowest),
        jnp.maximum(grad_inflow, lowest),
        *sums,
        sum_gain,
    )


def solution(mesh):
    placed = (
        P("sample", "turb", None),
        P("sample", "turb", None),
        P(),
        P(),
        P(),
        P(),
        P(),
        P(),
        P("sample"),
    )

    def plan(*args):
        sample_count = args[0].shape[0]
        if sample_count == mesh.shape["turb"] == TURBS and mesh.shape["sample"] == SAMPLES:
            return by_sample(*args)
        return on_device(*args)

    return jax.shard_map(
        plan,
        mesh=mesh,
        in_specs=placed,
        out_specs=(P("sample", "turb", None), P("sample", "turb", None), P(), P(), P(), P(), P()),
        check_vma=False,
    )
```

```python
import jax
import jax.numpy as jnp
from jax import lax
from jax.experimental import pallas as pl
from jax.experimental.pallas import tpu as pltpu
from jax.sharding import PartitionSpec as P

HEADS = 8
UPSTREAM = 3
SECTORS = 8
REPEAT = 1


epsilon = 1e-05


def normalize(row_block, norm_gain):
    widened = row_block.astype(jnp.float32)
    centred = widened - jnp.mean(widened, axis=-1, keepdims=True)
    inverse = lax.rsqrt(jnp.mean(centred * centred, axis=-1, keepdims=True) + epsilon)
    scaled = centred * inverse
    return (scaled, inverse, (scaled * norm_gain).astype(jnp.bfloat16))


def attend(pieces):
    queries, key_rows, value_rows, key_usable, grad_attended = pieces
    batch_count, query_count, model_width = queries.shape
    key_count = key_rows.shape[1]
    head_dim = model_width // HEADS
    score_scale = head_dim ** (-0.5)
    query_heads = queries.reshape(batch_count, query_count, HEADS, head_dim)
    key_heads = key_rows.reshape(batch_count, key_count, HEADS, head_dim)
    value_heads = value_rows.reshape(batch_count, key_count, HEADS, head_dim)
    grad_heads = grad_attended.reshape(batch_count, query_count, HEADS, head_dim)
    scores = (
        jnp.einsum("nqhd,nkhd->nhqk", query_heads, key_heads, preferred_element_type=jnp.float32)
        * score_scale
    )
    scores = jnp.where(key_usable[:, None, None, :], scores, -1e30)
    highest = jnp.max(scores, axis=-1, keepdims=True)
    weights = jnp.exp(scores - highest)
    probabilities = weights / jnp.sum(weights, axis=-1, keepdims=True)
    rounded = probabilities.astype(jnp.bfloat16)
    attended = jnp.einsum(
        "nhqk,nkhd->nqhd", rounded, value_heads, preferred_element_type=jnp.float32
    ).astype(jnp.bfloat16)
    grad_probs = jnp.einsum(
        "nqhd,nkhd->nhqk", grad_heads, value_heads, preferred_element_type=jnp.float32
    )
    centred = grad_probs - jnp.sum(probabilities * grad_probs, axis=-1, keepdims=True)
    grad_scores = (probabilities * centred * score_scale).astype(jnp.bfloat16)
    grad_queries = jnp.einsum(
        "nhqk,nkhd->nqhd", grad_scores, key_heads, preferred_element_type=jnp.float32
    ).astype(jnp.bfloat16)
    grad_keys = jnp.einsum(
        "nhqk,nqhd->nkhd", grad_scores, query_heads, preferred_element_type=jnp.float32
    )
    grad_values = jnp.einsum(
        "nhqk,nqhd->nkhd", rounded, grad_heads, preferred_element_type=jnp.float32
    )
    pair_terms = jnp.concatenate(
        [
            grad_keys.reshape(batch_count, key_count, model_width),
            grad_values.reshape(batch_count, key_count, model_width),
        ],
        axis=-1,
    )
    return (
        attended.reshape(batch_count, query_count, model_width),
        grad_queries.reshape(batch_count, query_count, model_width),
        pair_terms,
    )


def on_device(
    inflow,
    cotangent,
    norm_gain,
    query_weight,
    key_weight,
    value_weight,
    out_weight,
    adjacency,
    sectors,
):
    sample_count, block_rows, model_width = inflow.shape
    block_count = lax.axis_size("turb")
    own_block = lax.axis_index("turb")
    slot_count = REPEAT * ((SECTORS * UPSTREAM + block_count - 2) // (block_count - 1))
    flat_rows = sample_count * block_rows
    pair_width = 2 * model_width
    input_rows = inflow.reshape(flat_rows, model_width)
    grad_rows = cotangent.reshape(flat_rows, model_width)
    scaled, inverse, normed = normalize(input_rows, norm_gain)
    queries = jnp.dot(normed, query_weight, preferred_element_type=jnp.float32).astype(jnp.bfloat16)
    key_rows = jnp.dot(normed, key_weight, preferred_element_type=jnp.float32).astype(jnp.bfloat16)
    value_rows = jnp.dot(normed, value_weight, preferred_element_type=jnp.float32).astype(
        jnp.bfloat16
    )
    upstream = adjacency[sectors]
    needed = jnp.any(upstream == own_block, axis=2).astype(jnp.int32)
    earlier_need = jnp.cumsum(needed, axis=0) - needed
    slot_index = lax.broadcasted_iota(jnp.int32, (block_count, slot_count, sample_count), 1)
    chosen = (needed.T[:, None, :] == 1) & (earlier_need.T[:, None, :] == slot_index)
    selector = chosen.astype(jnp.bfloat16).reshape(block_count * slot_count, sample_count)
    own_lists = lax.dynamic_index_in_dim(upstream, own_block, axis=1, keepdims=False)
    usable = own_lists >= 0
    matches = jnp.any(own_lists[:, :, None, None] == own_lists[None, None, :, :], axis=3)
    sample_ids = lax.broadcasted_iota(jnp.int32, (sample_count, sample_count), 0)
    earlier = lax.broadcasted_iota(jnp.int32, (sample_count, sample_count), 1) < sample_ids
    position = jnp.sum((matches & earlier[:, None, :]).astype(jnp.int32), axis=2)
    flat_slot = own_lists * slot_count + position
    fetch_at = jnp.where(usable, flat_slot, 0)
    payload = jnp.concatenate([key_rows, value_rows], axis=1).reshape(
        sample_count, block_rows * pair_width
    )
    packed = jnp.dot(selector, payload, preferred_element_type=jnp.float32).astype(jnp.bfloat16)
    arrived = lax.all_to_all(
        packed.reshape(block_count, slot_count, block_rows, pair_width),
        "turb",
        split_axis=0,
        concat_axis=0,
        tiled=True,
    )
    fetched = arrived.reshape(block_count * slot_count, block_rows, pair_width)[fetch_at]
    upstream_keys = fetched[..., :model_width]
    upstream_values = fetched[..., model_width:]
    key_count = (1 + UPSTREAM) * block_rows
    key_all = jnp.concatenate(
        [key_rows.reshape(sample_count, 1, block_rows, model_width), upstream_keys], axis=1
    ).reshape(sample_count, key_count, model_width)
    value_all = jnp.concatenate(
        [value_rows.reshape(sample_count, 1, block_rows, model_width), upstream_values], axis=1
    ).reshape(sample_count, key_count, model_width)
    block_usable = jnp.concatenate([jnp.ones((sample_count, 1), dtype=jnp.bool_), usable], axis=1)
    key_usable = jnp.repeat(block_usable, block_rows, axis=1)
    grad_attended = jnp.dot(grad_rows, out_weight.T, preferred_element_type=jnp.float32).astype(
        jnp.bfloat16
    )
    group_size = min(sample_count, max(1, 512 // block_rows))
    while sample_count % group_size != 0:
        group_size = group_size - 1
    group_count = sample_count // group_size

    def grouped(tensor):
        return tensor.reshape((group_count, group_size) + tensor.shape[1:])

    attended, grad_queries, pair_terms = lax.map(
        attend,
        (
            grouped(queries.reshape(sample_count, block_rows, model_width)),
            grouped(key_all),
            grouped(value_all),
            grouped(key_usable),
            grouped(grad_attended.reshape(sample_count, block_rows, model_width)),
        ),
    )
    attended = attended.reshape(flat_rows, model_width)
    grad_queries = grad_queries.reshape(flat_rows, model_width)
    pair_terms = pair_terms.reshape(sample_count, 1 + UPSTREAM, block_rows, pair_width)
    layer_output = (
        (
            input_rows.astype(jnp.float32)
            + jnp.dot(attended, out_weight, preferred_element_type=jnp.float32)
        )
        .astype(jnp.bfloat16)
        .reshape(inflow.shape)
    )
    outgoing = (
        pair_terms[:, 1:]
        .astype(jnp.bfloat16)
        .reshape(sample_count * UPSTREAM, block_rows, pair_width)
    )
    target = jnp.where(usable, flat_slot, block_count * slot_count).reshape(-1)
    outbound = (
        jnp.zeros((block_count * slot_count, block_rows, pair_width), jnp.bfloat16)
        .at[target]
        .set(outgoing, mode="drop")
    )
    sum_out = jnp.dot(attended.T, grad_rows, preferred_element_type=jnp.float32)
    sum_query = jnp.dot(normed.T, grad_queries, preferred_element_type=jnp.float32)
    returned = lax.all_to_all(
        outbound.reshape(block_count, slot_count, block_rows, pair_width),
        "turb",
        split_axis=0,
        concat_axis=0,
        tiled=True,
    )
    remote = jnp.dot(
        selector.T,
        returned.reshape(block_count * slot_count, block_rows * pair_width),
        preferred_element_type=jnp.float32,
    )
    combined = (
        (pair_terms[:, 0].reshape(sample_count, block_rows * pair_width) + remote)
        .astype(jnp.bfloat16)
        .reshape(flat_rows, pair_width)
    )
    grad_keys = combined[:, :model_width]
    grad_values = combined[:, model_width:]
    sum_key = jnp.dot(normed.T, grad_keys, preferred_element_type=jnp.float32)
    sum_value = jnp.dot(normed.T, grad_values, preferred_element_type=jnp.float32)
    grad_normed = jnp.dot(grad_queries, query_weight.T, preferred_element_type=jnp.float32)
    grad_normed = grad_normed + jnp.dot(grad_keys, key_weight.T, preferred_element_type=jnp.float32)
    grad_normed = grad_normed + jnp.dot(
        grad_values, value_weight.T, preferred_element_type=jnp.float32
    )
    sum_gain = jnp.sum(grad_normed * scaled, axis=0)
    grad_scaled = grad_normed * norm_gain
    grad_input = inverse * (
        grad_scaled
        - jnp.mean(grad_scaled, axis=-1, keepdims=True)
        - scaled * jnp.mean(grad_scaled * scaled, axis=-1, keepdims=True)
    )
    grad_inflow = (
        (grad_rows.astype(jnp.float32) + grad_input).astype(jnp.bfloat16).reshape(inflow.shape)
    )
    sum_query, sum_key, sum_value, sum_out, sum_gain = lax.psum(
        (sum_query, sum_key, sum_value, sum_out, sum_gain), ("sample", "turb")
    )
    return (layer_output, grad_inflow, sum_query, sum_key, sum_value, sum_out, sum_gain)


PAIR = 2
QUAD = 4
LOG2_E = 1.4426950408889634
VMEM_LIMIT = 58 * 2**20
SUM_ROWS = 8
SAMPLES = 4
TURBS = 8


def turb_place(apart):
    return (apart % 2) * 4 + (apart // 4) * 2 + (apart // 2) % 2


def contract(left, right, left_dim, right_dim):
    return lax.dot_general(
        left, right, (((left_dim,), (right_dim,)), ((), ())), preferred_element_type=jnp.float32
    )


def split_heads(rows, head_dim):
    lane = lax.broadcasted_iota(jnp.int32, rows.shape, 1)
    wide = rows.astype(jnp.float32)
    return jnp.concatenate(
        [jnp.where(lane < head_dim, wide, 0.0), jnp.where(lane >= head_dim, wide, 0.0)], axis=0
    ).astype(jnp.bfloat16)


def join_heads(wide, head_dim):
    block_rows = wide.shape[1] // PAIR
    first = lax.broadcasted_iota(jnp.int32, (wide.shape[0], block_rows), 0) < head_dim
    return jnp.where(first, wide[:, :block_rows], wide[:, block_rows:])


def for_each_block(sectors_ref, lists_ref, block_count, block_rows, work):
    sector = sectors_ref[lax.axis_index("turb")]

    def step(block, carry):
        used = jnp.int32(0)
        for slot in range(UPSTREAM):
            used = used + (lists_ref[slot, sector, block] >= 0).astype(jnp.int32)
        for count in range(UPSTREAM + 1):

            @pl.when(used == count)
            def _():
                sources = [block] + [
                    lists_ref[slot, sector, block] for slot in range(count)
                ]
                work(block, [pl.multiple_of(s * block_rows, block_rows) for s in sources])

        return carry

    lax.fori_loop(0, block_count, step, 0)


def stacked(ref, starts, block_rows, lanes):
    return jnp.concatenate([ref[pl.ds(s, block_rows), lanes] for s in starts], axis=0)


def beside(ref, starts, block_rows, rows):
    return jnp.concatenate([ref[rows, pl.ds(s, block_rows)] for s in starts], axis=1)


def forward_kernel(block_rows, head_dim, sectors_ref, lists_ref, x_ref, gain_ref, wq_ref, wk_ref,
                   wv_ref, wo_ref, normed_t_ref, q_ref, k_ref, v_ref, kt_ref, att_ref,
                   level_ref, out_ref, normed_ref, vt_ref, rows_ref, sum_ref):
    row_count = x_ref.shape[0]
    quad = pl.program_id(0)
    pair = PAIR * head_dim
    exponent = head_dim ** (-0.5) * LOG2_E
    chunk = min(row_count, 256)

    @pl.when(quad == 0)
    def _():
        for start in range(0, row_count, chunk):
            part = slice(start, start + chunk)
            scaled, _, normed = normalize(x_ref[part, :], gain_ref[...])
            normed_ref[part, :] = normed
            normed_t_ref[:, part] = (scaled * gain_ref[...]).T.astype(jnp.bfloat16)

    normed = normed_ref[...]
    q_ref[...] = contract(normed, wq_ref[...], 1, 0).astype(jnp.bfloat16)
    k_ref[...] = contract(normed, wk_ref[...], 1, 0).astype(jnp.bfloat16)
    v_ref[...] = contract(normed, wv_ref[...], 1, 0).astype(jnp.bfloat16)
    kt_ref[...] = contract(wk_ref[...], normed, 0, 1).astype(jnp.bfloat16)
    vt_ref[...] = contract(wv_ref[...], normed, 0, 1).astype(jnp.bfloat16)

    def work(block, starts):
        own = pl.ds(starts[0], block_rows)
        lanes = [slice(p * pair, (p + 1) * pair) for p in range(QUAD // PAIR)]
        scores = [
            contract(
                stacked(k_ref, starts, block_rows, lane), split_heads(q_ref[own, lane], head_dim), 1, 1
            )
            for lane in lanes
        ]
        for p, lane in enumerate(lanes):
            highest = jnp.max(scores[p], axis=0, keepdims=True)
            weights = jnp.exp2((scores[p] - highest) * exponent)
            total = jnp.sum(weights, axis=0, keepdims=True)
            probs = (weights * (1.0 / total)).astype(jnp.bfloat16)
            level_ref[0, pl.ds(block * (QUAD // PAIR) + p, 1), :] = highest * exponent + jnp.log2(
                total
            )
            joined = join_heads(
                jnp.dot(
                    beside(vt_ref, starts, block_rows, lane),
                    probs,
                    preferred_element_type=jnp.float32,
                ),
                head_dim,
            )
            att_ref[lane, own] = joined.astype(jnp.bfloat16)
            rows_ref[own, lane] = joined.T.astype(jnp.bfloat16)

    for_each_block(sectors_ref, lists_ref, row_count // block_rows, block_rows, work)
    part = contract(rows_ref[...], wo_ref[...], 1, 0)

    @pl.when(quad == 0)
    def _():
        sum_ref[...] = x_ref[...].astype(jnp.float32) + part

    @pl.when(quad > 0)
    def _():
        sum_ref[...] += part

    @pl.when(quad == pl.num_programs(0) - 1)
    def _():
        out_ref[...] = sum_ref[...].astype(jnp.bfloat16)


def forward(sectors, adjacency, rows, norm_gain, query_weight, key_weight, value_weight, out_weight, block_rows):
    row_count, width = rows.shape
    head_dim = width // HEADS
    quad = QUAD * head_dim
    quads = width // quad
    stat_rows = row_count // block_rows * (QUAD // PAIR)
    fixed = lambda *shape: pl.BlockSpec(shape, lambda p, *lists: (0,) * len(shape))
    across = lambda size: pl.BlockSpec((size, quad), lambda p, *lists: (0, p))
    down = lambda size: pl.BlockSpec((quad, size), lambda p, *lists: (p, 0))
    stat = pl.BlockSpec((1, stat_rows, PAIR * block_rows), lambda p, *lists: (p, 0, 0))
    flat = jax.ShapeDtypeStruct((row_count, width), jnp.bfloat16)
    turned = jax.ShapeDtypeStruct((width, row_count), jnp.bfloat16)
    stats = jax.ShapeDtypeStruct((quads, stat_rows, PAIR * block_rows), jnp.float32)
    return pl.pallas_call(
        lambda *refs: forward_kernel(block_rows, head_dim, *refs),
        grid_spec=pltpu.PrefetchScalarGridSpec(
            num_scalar_prefetch=2,
            grid=(quads,),
            in_specs=[fixed(row_count, width), fixed(1, width)]
            + [across(width)] * 3
            + [down(width)],
            out_specs=[fixed(width, row_count)]
            + [across(row_count)] * 3
            + [down(row_count)] * 2
            + [stat, fixed(row_count, width)],
            scratch_shapes=[
                pltpu.VMEM((row_count, width), jnp.bfloat16),
                pltpu.VMEM((quad, row_count), jnp.bfloat16),
                pltpu.VMEM((row_count, quad), jnp.bfloat16),
                pltpu.VMEM((row_count, width), jnp.float32),
            ],
        ),
        out_shape=[turned, flat, flat, flat, turned, turned, stats, flat],
        compiler_params=pltpu.CompilerParams(vmem_limit_bytes=VMEM_LIMIT),
        cost_estimate=pl.CostEstimate(
            flops=12 * row_count * width * width + 32 * row_count * block_rows * width,
            bytes_accessed=20 * row_count * width,
            transcendentals=row_count * 4 * block_rows * HEADS,
        ),
        name="forward",
    )(sectors, adjacency, rows, norm_gain.reshape(1, width), query_weight, key_weight, value_weight,
      out_weight)


def backward_kernel(block_rows, head_dim, which, sectors_ref, lists_ref, wo_ref, q_ref, k_ref, v_ref,
                    kt_ref, level_ref, gain_ref, *refs):
    before, refs = refs[:which], refs[which:]
    late, refs = refs[:6], refs[6:]
    gq_ref, gk_ref, gv_ref, keep_ref, send_ref, sum_ref, *refs = refs
    ga_ref, gk_acc, gv_acc, parts_ref, *held, sems = refs
    cot_ref = held[0]
    row_count, width = cot_ref.shape
    block_count = row_count // block_rows
    pair = PAIR * head_dim
    quad = QUAD * head_dim
    scale = head_dim ** (-0.5)
    own_lanes = slice(which * quad, (which + 1) * quad)
    copies = []
    for i, (ref, into) in enumerate(zip(late, held)):
        source = ref if i < 3 else ref.at[:, own_lanes]
        copies.append(pltpu.make_async_copy(source, into, sems.at[i]))
        copies[-1].start()
    _, normed_t_ref, att_ref, *weight_refs = held
    copies[0].wait()
    ga_ref[...] = contract(cot_ref[...], wo_ref[...], 1, 1).astype(jnp.bfloat16)
    gk_acc[...] = jnp.zeros_like(gk_acc)
    gv_acc[...] = jnp.zeros_like(gv_acc)

    def work(block, starts):
        own = pl.ds(starts[0], block_rows)
        lanes = [slice(p * pair, (p + 1) * pair) for p in range(QUAD // PAIR)]
        queries = [split_heads(q_ref[own, lane], head_dim) for lane in lanes]
        grads = [split_heads(ga_ref[own, lane], head_dim) for lane in lanes]
        scores = [
            contract(stacked(k_ref, starts, block_rows, lane), queries[p], 1, 1)
            for p, lane in enumerate(lanes)
        ]
        grad_probs = [
            contract(stacked(v_ref, starts, block_rows, lane), grads[p] * scale, 1, 1)
            for p, lane in enumerate(lanes)
        ]
        for p, lane in enumerate(lanes):
            stat = pl.ds(block * (QUAD // PAIR) + p, 1)
            probs = jnp.exp2(scores[p] * (scale * LOG2_E) - level_ref[0, stat, :])
            total = jnp.sum(probs * grad_probs[p], axis=0, keepdims=True)
            grad_scores = (probs * (grad_probs[p] - total)).astype(jnp.bfloat16)
            probs_b = probs.astype(jnp.bfloat16)
            grad_values = jnp.dot(probs_b, grads[p], preferred_element_type=jnp.float32)
            grad_keys = jnp.dot(grad_scores, queries[p], preferred_element_type=jnp.float32)
            joined = join_heads(
                jnp.dot(
                    beside(kt_ref, starts, block_rows, lane),
                    grad_scores,
                    preferred_element_type=jnp.float32,
                ),
                head_dim,
            )
            gq_ref[own, lane] = joined.T.astype(jnp.bfloat16)
            for slot, start in enumerate(starts):
                rows = pl.ds(start, block_rows)
                part = slice(slot * block_rows, (slot + 1) * block_rows)
                for acc, terms in ((gk_acc, grad_keys), (gv_acc, grad_values)):
                    term = terms[part]
                    if slot > 0:
                        term = term.astype(jnp.bfloat16).astype(jnp.float32)
                    acc[rows, lane] += term

    for_each_block(sectors_ref, lists_ref, block_count, block_rows, work)
    gk_ref[...] = gk_acc[...].astype(jnp.bfloat16)
    gv_ref[...] = gv_acc[...].astype(jnp.bfloat16)
    for copy in copies[1:]:
        copy.wait()
    products = [(normed_t_ref, ref, slice(None)) for ref in (gq_ref, gk_ref, gv_ref)]
    products.append((att_ref, cot_ref, own_lanes))
    own_sample, own_turb = lax.axis_index("sample"), lax.axis_index("turb")
    share = width // TURBS
    along = jnp.zeros((width, quad), jnp.float32)
    for i, (left, right, lanes) in enumerate(products):
        terms = contract(left[...], right[:, lanes], 1, 0)
        if i < len(weight_refs):
            along += terms * weight_refs[i][...].astype(jnp.float32)
        apart = i ^ own_sample
        for turb in range(TURBS):
            place = turb_place(turb ^ own_turb)
            if which == 0:
                half, start = place // 4, (apart % 2 * 2 + apart // 2) * 4 + place % 4
            else:
                half, start = apart % 2, apart // 2 * TURBS + place
            start = pl.multiple_of(start * share, share)
            parts_ref[half, pl.ds(start, share), :] = terms[turb * share : (turb + 1) * share]
    keep_ref[...] = parts_ref[0]
    send_ref[...] = parts_ref[1].astype(send_ref.dtype)
    ones = jnp.ones((SUM_ROWS, quad), jnp.bfloat16)
    coarse = along.astype(jnp.bfloat16)
    fine = (along - coarse.astype(jnp.float32)).astype(jnp.bfloat16)
    total = (contract(ones, coarse, 1, 1) + contract(ones, fine, 1, 1)) / gain_ref[...]
    sum_ref[...] = sum((ref[...] for ref in before), total)


def backward(sectors, adjacency, cotangent, out_weight, normed_t, queries, keys, values, keys_t,
             attended_t, levels, norm_gain, query_weight, key_weight, value_weight, before,
             block_rows, which):
    row_count, width = cotangent.shape
    head_dim = width // HEADS
    quad = QUAD * head_dim
    fixed = lambda *shape: pl.BlockSpec(shape, lambda i, *lists: (0,) * len(shape))
    across = pl.BlockSpec((row_count, quad), lambda i, *lists: (0, which))
    down = lambda size: pl.BlockSpec((quad, size), lambda i, *lists: (which, 0))
    stat = pl.BlockSpec((1,) + levels.shape[1:], lambda i, *lists: (which, 0, 0))
    part = jax.ShapeDtypeStruct((row_count, quad), jnp.bfloat16)
    half = (2 * width, quad)
    sent = jnp.bfloat16 if which == 0 else jnp.float32
    return pl.pallas_call(
        lambda *refs: backward_kernel(block_rows, head_dim, which, *refs),
        grid_spec=pltpu.PrefetchScalarGridSpec(
            num_scalar_prefetch=2,
            grid=(1,),
            in_specs=[down(width)]
            + [across] * 3
            + [down(row_count), stat, fixed(1, width)]
            + [fixed(SUM_ROWS, width)] * which
            + [pl.BlockSpec(memory_space=pl.ANY)] * 6,
            out_specs=[fixed(row_count, quad)] * 3
            + [fixed(*half)] * 2
            + [fixed(SUM_ROWS, width)],
            scratch_shapes=[
                pltpu.VMEM((row_count, quad), jnp.bfloat16),
                pltpu.VMEM((row_count, quad), jnp.float32),
                pltpu.VMEM((row_count, quad), jnp.float32),
                pltpu.VMEM((2,) + half, jnp.float32),
            ]
            + [pltpu.VMEM((row_count, width), jnp.bfloat16)]
            + [pltpu.VMEM((width, row_count), jnp.bfloat16)] * 2
            + [pltpu.VMEM((width, quad), jnp.bfloat16)] * 3
            + [pltpu.SemaphoreType.DMA((6,))],
        ),
        out_shape=[part] * 3
        + [
            jax.ShapeDtypeStruct(half, jnp.float32),
            jax.ShapeDtypeStruct(half, sent),
            jax.ShapeDtypeStruct((SUM_ROWS, width), jnp.float32),
        ],
        compiler_params=pltpu.CompilerParams(vmem_limit_bytes=VMEM_LIMIT),
        cost_estimate=pl.CostEstimate(
            flops=10 * row_count * width * quad + 80 * row_count * block_rows * quad,
            bytes_accessed=14 * row_count * width,
            transcendentals=row_count * 4 * block_rows * QUAD,
        ),
        name="backward",
    )(sectors, adjacency, out_weight, queries, keys, values, keys_t, levels,
      norm_gain.reshape(1, width), *before, cotangent, normed_t, attended_t, query_weight, key_weight,
      value_weight)


def finish_kernel(quads, x_ref, cot_ref, gain_ref, wq_ref, wk_ref, wv_ref, *refs):
    grad_refs, out_ref = refs[:-1], refs[-1]
    scaled, inverse, _ = normalize(x_ref[...], gain_ref[...])
    quad = grad_refs[0].shape[1]
    grad_normed = jnp.zeros(x_ref.shape, jnp.float32)
    for i in range(quads):
        lanes = slice(i * quad, (i + 1) * quad)
        for j, weight_ref in enumerate((wq_ref, wk_ref, wv_ref)):
            grad_normed += contract(grad_refs[3 * i + j][...], weight_ref[:, lanes], 1, 1)
    grad_scaled = grad_normed * gain_ref[...]
    grad_input = inverse * (
        grad_scaled
        - jnp.mean(grad_scaled, axis=-1, keepdims=True)
        - scaled * jnp.mean(grad_scaled * scaled, axis=-1, keepdims=True)
    )
    out_ref[...] = (cot_ref[...].astype(jnp.float32) + grad_input).astype(jnp.bfloat16)


def finish(rows, cotangent, norm_gain, query_weight, key_weight, value_weight, grads):
    row_count, width = rows.shape
    quad = grads[0].shape[1]
    step = min(row_count, 256)
    fixed = lambda *shape: pl.BlockSpec(shape, lambda i: (0,) * len(shape))
    by_row = lambda size: pl.BlockSpec((step, size), lambda i: (i, 0))
    return pl.pallas_call(
        lambda *refs: finish_kernel(width // quad, *refs),
        grid=(row_count // step,),
        in_specs=[by_row(width)] * 2
        + [fixed(1, width)]
        + [fixed(width, width)] * 3
        + [by_row(quad)] * len(grads),
        out_specs=by_row(width),
        out_shape=jax.ShapeDtypeStruct((row_count, width), jnp.bfloat16),
        compiler_params=pltpu.CompilerParams(vmem_limit_bytes=VMEM_LIMIT),
        cost_estimate=pl.CostEstimate(
            flops=6 * row_count * width * width,
            bytes_accessed=16 * row_count * width,
            transcendentals=0,
        ),
        name="finish",
    )(rows, cotangent, norm_gain.reshape(1, width), query_weight, key_weight, value_weight, *grads)


def swap(tensor, axis):
    return lax.all_to_all(tensor, axis, split_axis=0, concat_axis=0, tiled=True)


def across(tensor, axis, distance):
    size = lax.axis_size(axis)
    return lax.ppermute(tensor, axis, [(i, i ^ distance) for i in range(size)])


def across(tensor, axis, distance):
    size = lax.axis_size(axis)
    return lax.ppermute(tensor, axis, [(i, i ^ distance) for i in range(size)])


def reduce_sums(early, late, arrived_late, gain, width, beside):
    quad = gain.shape[1]
    count = gain.shape[0]
    wide = jnp.float32

    def pack(gain):
        high = gain.astype(jnp.bfloat16)
        low = (gain - high.astype(wide)).astype(jnp.bfloat16)
        return jnp.concatenate([high, low, jnp.zeros((16 - 2 * count, quad), jnp.bfloat16)])

    def halve(parts, gain, axis, distance):
        halves = [part.shape[0] // 2 for part in parts]
        sent = [part[half:].astype(jnp.bfloat16) for part, half in zip(parts, halves)]
        if gain is not None:
            sent.append(pack(gain))
        arrived = across(jnp.concatenate(sent), axis, distance)
        start, kept = 0, []
        for part, half in zip(parts, halves):
            kept.append(part[:half] + arrived[start : start + half].astype(wide))
            start += half
        if gain is None:
            return kept, gain
        rows = arrived[start:].astype(wide)
        return kept, gain + rows[:count] + rows[count : 2 * count]

    first = early[:width] + across(early[width:], "sample", 1)
    first, _ = halve([first], None, "sample", 2)
    half = late.shape[0] // 2
    sent = (late[half:] + arrived_late[half:]).astype(jnp.bfloat16)
    arrived = across(jnp.concatenate([sent, pack(gain)]), "sample", 2).astype(wide)
    second = late[:half] + arrived_late[:half] + arrived[:half]
    gain = gain + arrived[half : half + count] + arrived[half + count : half + 2 * count]
    second, gain = halve([second], gain, "turb", 1)
    parts, gain, beside = lax.optimization_barrier((first + second, gain, beside))
    share = parts[0].shape[0] // 4
    pieces = [jnp.concatenate([part[i * share : (i + 1) * share] for part in parts]) for i in range(4)]
    size = pieces[0].shape[0]
    sent = [jnp.concatenate([piece.astype(jnp.bfloat16), pack(gain)]) for piece in pieces[1:]]
    arrived = [across(piece, "turb", 2 * i + 2).astype(wide) for i, piece in enumerate(sent)]
    total = pieces[0] + sum(rows[:size] for rows in arrived)
    gain = gain + sum(
        rows[size : size + count] + rows[size + count : size + 2 * count] for rows in arrived
    )
    total = total.astype(jnp.bfloat16).reshape(1, 2, share, quad)
    total = jnp.concatenate([total] + [across(total, "turb", distance) for distance in (2, 4, 6)])
    other = across(total, "turb", 1)
    four = [total, other, across(total, "sample", 2), across(other, "sample", 2)]
    four += [across(part, "sample", 1) for part in four]
    return four, gain.reshape(width), beside


def place_kernel(*refs):
    (*sources, query_ref, key_ref, value_ref, out_ref, all_ref, held, sems) = refs
    copies = [
        pltpu.make_async_copy(ref, held.at[i], sems.at[i]) for i, ref in enumerate(sources)
    ]
    for copy in copies:
        copy.start()
    own_sample, own_turb = lax.axis_index("sample"), lax.axis_index("turb")
    _, _, quads, share, quad = held.shape
    for i in range(SAMPLES):
        copies[2 * i].wait()
        copies[2 * i + 1].wait()
        product = own_sample ^ ((i % 2) * 2 + i // 2)
        for apart in range(TURBS):
            place = turb_place(apart)
            rows = pl.ds(pl.multiple_of((apart ^ own_turb) * share, share), share)
            for j in range(quads):
                all_ref[product, rows, j * quad : (j + 1) * quad] = held[
                    2 * i + place // 4, place % 4, j
                ].astype(jnp.float32)
    for i, ref in enumerate((query_ref, key_ref, value_ref, out_ref)):
        ref[...] = all_ref[i]


def place_sums(parts, width):
    return pl.pallas_call(
        place_kernel,
        in_specs=[pl.BlockSpec(memory_space=pl.ANY)] * len(parts),
        out_specs=[pl.BlockSpec(memory_space=pltpu.VMEM)] * 4,
        out_shape=[jax.ShapeDtypeStruct((width, width), jnp.float32)] * 4,
        scratch_shapes=[
            pltpu.VMEM((4, width, width), jnp.float32),
            pltpu.VMEM((len(parts),) + parts[0].shape, jnp.bfloat16),
            pltpu.SemaphoreType.DMA((len(parts),)),
        ],
        compiler_params=pltpu.CompilerParams(vmem_limit_bytes=VMEM_LIMIT),
        cost_estimate=pl.CostEstimate(
            flops=0, bytes_accessed=24 * width * width, transcendentals=0
        ),
        name="place",
    )(*parts)


def by_sample(
    inflow,
    cotangent,
    norm_gain,
    query_weight,
    key_weight,
    value_weight,
    out_weight,
    adjacency,
    sectors,
):
    sample_count, block_rows, width = inflow.shape
    row_count = lax.axis_size("turb") * block_rows
    adjacency = jnp.transpose(adjacency, (2, 0, 1))
    rows = swap(inflow, "turb")
    rows, cotangent = lax.optimization_barrier((rows, cotangent))
    rows = rows.reshape(row_count, width)
    grad_rows = swap(cotangent, "turb").reshape(row_count, width)
    *saved, layer_rows = forward(
        sectors, adjacency, rows, norm_gain, query_weight, key_weight, value_weight, out_weight,
        block_rows,
    )
    layer_output = swap(layer_rows.reshape(inflow.shape), "turb")
    weights = (norm_gain, query_weight, key_weight, value_weight)
    *grads, early, send, before = backward(
        sectors, adjacency, grad_rows, out_weight, *saved, *weights, [], block_rows, 0
    )
    arrived = across(send, "turb", 1)
    *more, late, send, gain = backward(
        sectors, adjacency, grad_rows, out_weight, *saved, *weights, [before], block_rows, 1
    )
    more, send, arrived, layer_output = lax.optimization_barrier(
        (more, send, arrived, layer_output)
    )
    arrived_late = across(send, "sample", 1)
    grad_rows = finish(rows, grad_rows, *weights, grads + more)
    grad_rows, late, arrived_late, gain, early, arrived = lax.optimization_barrier(
        (grad_rows, late, arrived_late, gain, early, arrived)
    )
    gain = gain[0].reshape(-1, late.shape[1])
    arrived_gain = across(gain, "sample", 1)
    early = early + arrived.astype(jnp.float32)
    grad_inflow = swap(grad_rows.reshape(inflow.shape), "turb")
    parts, sum_gain, grad_inflow = reduce_sums(
        early, late, arrived_late, gain + arrived_gain, width, grad_inflow
    )
    sums = place_sums(parts, width)
    lowest = jnp.finfo(jnp.bfloat16).min
    return (
        jnp.maximum(layer_output, lowest),
        jnp.maximum(grad_inflow, lowest),
        *sums,
        sum_gain,
    )


def solution(mesh):
    placed = (
        P("sample", "turb", None),
        P("sample", "turb", None),
        P(),
        P(),
        P(),
        P(),
        P(),
        P(),
        P("sample"),
    )

    def plan(*args):
        sample_count = args[0].shape[0]
        if sample_count == mesh.shape["turb"] == TURBS and mesh.shape["sample"] == SAMPLES:
            return by_sample(*args)
        return on_device(*args)

    return jax.shard_map(
        plan,
        mesh=mesh,
        in_specs=placed,
        out_specs=(P("sample", "turb", None), P("sample", "turb", None), P(), P(), P(), P(), P()),
        check_vma=False,
    )
```
